32 devices in a mesh: dp: 8 (over z, y), head: 4 (over x, core).
Axes of the slice: x: 2, y: 2, z: 4, core: 2. Of those that a mesh axis runs over, the one named last changes fastest.
Arguments:
- features: float32 [65536, 1024], P('dp', 'head'), may hold values from -6 to 6
- adjacency: int32 [32, 256, 2048], P('dp'), may hold values from 0 to 1, as said below
- seed_counts: int32 [32], P('dp'), may hold values from 128 to 256, as said below
- w_proj: float32 [1024, 1024], P(None, 'head'), may hold values from -0.5 to 0.5
- w_skip: float32 [1024, 1024], P(None, 'head'), may hold values from -0.1875 to 0.1875
- attn_src: float32 [1024], P('head'), may hold values from -0.125 to 0.125
- attn_dst: float32 [1024], P('head'), may hold values from -0.125 to 0.125
- bias: float32 [1024], P('head'), may hold values from -3 to 3
- gamma: float32 [1024], P('head'), may hold values from 0.5 to 1.5
- beta: float32 [1024], P('head'), may hold values from -3 to 3
- cotangent: float32 [8192, 1024], P('dp', 'head'), may hold values from -6 to 6
Outputs:
- activations: float32 [8192, 1024], P('dp', 'head')
- grad_features: float32 [65536, 1024], P('dp', 'head')
- grad_w_proj: float32 [1024, 1024], P(None, 'head')
- grad_w_skip: float32 [1024, 1024], P(None, 'head')
- grad_attn_src: float32 [1024], P('head')
- grad_attn_dst: float32 [1024], P('head')
- grad_bias: float32 [1024], P('head')
- grad_gamma: float32 [1024], P('head')
- grad_beta: float32 [1024], P('head')
The draws below stay inside these ranges and needn't reach their ends.
Inputs may be any that keep to these rules, and one draw needn't show every extreme that they name: adjacency[b, i, i] = 1; adjacency[b, i, j] = 0 for every j at or past block b's number of real source nodes, which lies between 1024 and 2048 and is 2048 in some block. `seed_counts`: some block has 256 real destination nodes.
All inputs are finite; a program needn't handle non-finite values.
Results may differ from the reference program's by a relative error of at most 0.0003.
Values sent between devices are 32-bit elements; how exact they have to be, the bound alone decides.
No kernel may reach another device: no remote copies, remote signals or barrier semaphores. Data moves between devices by JAX's collectives and lax.ppermute only.
A program may use at most 192 MiB of HBM per device.

```python
import jax
import jax.numpy as jnp
from jax import lax

IN = 1024
HEADS = 4
HD = 256
D = 1024
DST = 256
NODES = 2048
BLOCKS = 32


def draw_seed_counts(key, part):
    key = jax.random.fold_in(key, 3)
    key_count, second = jax.random.split(key)
    counts = jax.random.randint(key_count, (BLOCKS,), DST // 2, DST + 1)
    fullest = jax.random.randint(second, (), 0, BLOCKS)
    return jnp.where(jnp.arange(BLOCKS) == fullest, DST, counts).astype(jnp.int32)


def draw_adjacency(key, part):
    key = jax.random.fold_in(key, 7)
    key_count, second, key_links = jax.random.split(key, 3)
    node_totals = jax.random.randint(key_count, (BLOCKS,), NODES // 2, NODES + 1)
    fullest = jax.random.randint(second, (), 0, BLOCKS)
    node_totals = jnp.where(jnp.arange(BLOCKS) == fullest, NODES, node_totals)
    sampled = jax.random.randint(key_links, (BLOCKS, DST, NODES), 0, NODES) < 10
    column = jnp.arange(NODES)[None, None, :]
    row_index = jnp.arange(DST)[None, :, None]
    linked = sampled & (column < node_totals[:, None, None]) | (column == row_index)
    return linked.astype(jnp.int32)


def block_levels(rng, dims, shards, least, largest):
    def one(dim, blocks):
        heights = jax.random.uniform(jax.random.fold_in(jax.random.fold_in(rng, 6), dim), (blocks,), jnp.float32, least / len(shards), largest / len(shards))
        return jnp.repeat(jnp.exp(heights), dims[dim] // blocks).reshape((-1,) + (1,) * (len(dims) - dim - 1))

    loudness = one(*shards[0])
    for cut in shards[1:]:
        loudness = loudness * one(*cut)
    return loudness


def scatter_about(key, shape, scale, most, shards=(), kind=jnp.bfloat16):
    gain = block_levels(key, shape, shards, -0.22, 0.18) if shards else 1.0
    entries = jax.random.normal(key, shape, jnp.float32) * scale * gain
    return jnp.minimum(jnp.maximum(entries, -most), most).astype(kind)


def setup_inputs(seed: int = 0) -> dict:
    splits = jax.random.split(jax.random.key(seed), 12)
    features = scatter_about(splits[0], (BLOCKS * NODES, IN), 1.0, 6.0, ((0, 8), (1, 4)), jnp.float32)
    adjacency = draw_adjacency(jax.random.fold_in(splits[11], 71), 0)
    seed_counts = draw_seed_counts(jax.random.fold_in(splits[11], 71), 0)
    w_proj = scatter_about(splits[3], (IN, D), (IN // 8) ** -0.5, 0.5, ((1, 4),), jnp.float32)
    w_skip = scatter_about(splits[4], (IN, D), IN ** -0.5, 0.1875, ((1, 4),), jnp.float32)
    attn_src = scatter_about(splits[5], (D,), (HD * 8) ** -0.5, 0.125, ((0, 4),), jnp.float32)
    attn_dst = scatter_about(splits[6], (D,), (HD * 8) ** -0.5, 0.125, ((0, 4),), jnp.float32)
    bias = scatter_about(splits[7], (D,), 0.5, 3.0, ((0, 4),), jnp.float32)
    gamma = jnp.clip(0.5 + 1.0 * jax.random.uniform(splits[8], (D,), jnp.float32) ** block_levels(splits[8], (D,), ((0, 4),), -0.2, 0.2), 0.5, 1.5)
    beta = scatter_about(splits[9], (D,), 0.5, 3.0, ((0, 4),), jnp.float32)
    cotangent = scatter_about(splits[10], (BLOCKS * DST, D), 1.0, 6.0, ((0, 8), (1, 4)), jnp.float32)
    return {"features": features, "adjacency": adjacency, "seed_counts": seed_counts, "w_proj": w_proj, "w_skip": w_skip, "attn_src": attn_src, "attn_dst": attn_dst, "bias": bias, "gamma": gamma, "beta": beta, "cotangent": cotangent}


exact_prec = lax.Precision.HIGHEST
eps = 1e-05

@jax.custom_vjp
def low(v):
    return lax.optimization_barrier(v.astype(jnp.bfloat16)).astype(jnp.float32)

@jax.custom_vjp
def low_back(v):
    return v

def low_keep(v):
    return (low(v), None)

def low_pass(kept, grad):
    return (grad,)

def back_keep(v):
    return (v, None)

def back_low(kept, grad):
    return (low(grad),)
low.defvjp(low_keep, low_pass)
low_back.defvjp(back_keep, back_low)

def smooth_leaky(summed):
    return 0.2 * summed + 0.8 * jax.nn.softplus(summed)

def block_layer(x_block, adj_block, w_proj, w_skip, attn_src, attn_dst, bias):
    projected = jnp.dot(x_block, w_proj, precision=exact_prec).reshape(NODES, HEADS, HD)
    src_score = jnp.einsum('jhd,hd->hj', projected, attn_src.reshape(HEADS, HD), precision=exact_prec)
    dst_score = jnp.einsum('ihd,hd->hi', projected[:DST], attn_dst.reshape(HEADS, HD), precision=exact_prec)
    summed = dst_score[:, :, None] + src_score[:, None, :]
    linked = adj_block[None] > 0
    logits = jnp.where(linked, smooth_leaky(summed), -1e+30)
    row_top = lax.optimization_barrier(jnp.max(logits, axis=2, keepdims=True))
    weights = jnp.where(linked, jnp.exp(logits - row_top), 0.0)
    attention = weights / lax.optimization_barrier(jnp.sum(weights, axis=2, keepdims=True))
    mixed = jnp.einsum('hij,jhd->ihd', attention, projected, precision=exact_prec).reshape(DST, D)
    return mixed + jnp.dot(x_block[:DST], w_skip, precision=exact_prec) + bias

def forward(features, w_proj, w_skip, attn_src, attn_dst, bias, gamma, beta, adjacency, live_rows):
    stacked = features.reshape(BLOCKS, NODES, IN)

    def per_block(inputs):
        return block_layer(inputs[0], inputs[1], w_proj, w_skip, attn_src, attn_dst, bias)
    pre_act = lax.map(jax.checkpoint(per_block), (stacked, adjacency)).reshape(BLOCKS * DST, D)
    activated = jax.nn.elu(pre_act)
    total_live = jnp.sum(live_rows)
    row_mean = lax.optimization_barrier(jnp.sum(live_rows * activated, axis=0)) / total_live
    spread = lax.optimization_barrier(jnp.sum(live_rows * activated * activated, axis=0)) / total_live - row_mean * row_mean
    normed = (activated - row_mean) * lax.rsqrt(spread + eps)
    return live_rows * (gamma * normed + beta)

def reference(features, adjacency, seed_counts, w_proj, w_skip, attn_src, attn_dst, bias, gamma, beta, cotangent):
    live_rows = (jnp.arange(DST, dtype=jnp.int32)[None, :] < seed_counts[:, None]).astype(jnp.float32).reshape(BLOCKS * DST, 1)

    def apply(x_in, p_in, s_in, a_in, b_in, c_in, g_in, e_in):
        return forward(x_in, p_in, s_in, a_in, b_in, c_in, g_in, e_in, adjacency, live_rows)
    output, pullback = jax.vjp(apply, features, w_proj, w_skip, attn_src, attn_dst, bias, gamma, beta)
    grads = pullback(cotangent)
    return (output, grads[0], grads[1], grads[2], grads[3], grads[4], grads[5], grads[6], grads[7])
```

```python
import functools

import jax
import jax.numpy as jnp
from jax import lax
from jax.experimental import pallas as pl
from jax.experimental.pallas import tpu as pltpu
from jax.sharding import PartitionSpec as P

HD = 256
HEADS = 4
TJ = 512
eps = 1e-05
LOG2E = 1.4426950408889634
F32 = jnp.float32
BF16 = jnp.bfloat16
NN = ((1,), (0,))
NT = ((1,), (1,))
TN = ((0,), (0,))
VMEM_BYTES = 56 * 2**20


def dot(a, b, form):
    return lax.dot_general(a, b, (form, ((), ())), preferred_element_type=F32)


def split2(x):
    hi = x.astype(BF16)
    return hi, (x - hi.astype(F32)).astype(BF16)


def dot3(a, b, form):
    return dot(a[0], b[0], form) + (dot(a[0], b[1], form) + dot(a[1], b[0], form))


def thin_rows(d):
    hi = d.astype(BF16).astype(F32)
    return jnp.concatenate([hi, hi, d - hi, jnp.zeros_like(d)], axis=0).astype(BF16)


def thin_cols(a):
    hi = a.astype(BF16).astype(F32)
    return jnp.concatenate([hi, a - hi, hi, jnp.zeros_like(a)], axis=0).astype(BF16)


def lane_groups(v):
    out = v[:, :128]
    for k in range(128, v.shape[1], 128):
        out = out + v[:, k : k + 128]
    return out


def leaky2(u):
    y = 1.0 + jnp.exp2(jnp.minimum(u, 126.0))
    return jnp.maximum(u, 0.2 * u + 0.8 * jnp.log2(y)), y


def elu(v):
    return jnp.where(v > 0, v, jnp.exp(jnp.minimum(v, 0.0)) - 1.0)


def params(*dims):
    return pltpu.CompilerParams(dimension_semantics=dims or None, vmem_limit_bytes=VMEM_BYTES)


def cost(flops, size):
    return pl.CostEstimate(flops=int(flops), bytes_accessed=int(size), transcendentals=0)


def score_kernel(x_ref, a_ref, o_ref):
    x = x_ref[...]
    x1 = x.astype(BF16)
    rest = x - x1.astype(F32)
    x2 = rest.astype(BF16)
    x3 = (rest - x2.astype(F32)).astype(BF16)
    a = a_ref[...]
    a1 = a.astype(BF16).astype(F32)
    a2 = (a - a1).astype(BF16).astype(F32)
    a3 = (a - a1) - a2
    stack = jnp.concatenate([a1, a2, a3, jnp.zeros_like(a)], axis=0).astype(BF16)
    r1 = dot(stack, x1, NT)
    r2 = dot(stack[:16], x2, NT)
    r3 = dot(stack[:16], x3, NT)
    o_ref[...] = r1[:8] + (r1[8:16] + r2[:8]) + (r1[16:24] + r2[8:16] + r3[:8])


def scores(features, a_own):
    rows, cols = features.shape
    tile = 1024
    return pl.pallas_call(
        score_kernel,
        grid=(rows // tile,),
        in_specs=[
            pl.BlockSpec((tile, cols), lambda i: (i, 0)),
            pl.BlockSpec((8, cols), lambda i: (0, 0)),
        ],
        out_specs=pl.BlockSpec((8, tile), lambda i: (0, i)),
        out_shape=jax.ShapeDtypeStruct((8, rows), F32),
        compiler_params=params("arbitrary"),
        cost_estimate=cost(2 * rows * cols * 48, rows * cols * 4),
        name="scores",
    )(features, a_own)


def top_kernel(idx_ref, adj_ref, s_ref, o_ref):
    rows, src = adj_ref.shape[1], adj_ref.shape[2]
    t_cols = jnp.transpose(s_ref[:, :rows])
    step = 64
    for r in range(0, rows, step):
        best = [jnp.full((step, 128), -3e38, F32) for _ in range(HEADS)]
        for k in range(0, src, 128):
            linked = adj_ref[0, r : r + step, k : k + 128] > 0
            for m in range(HEADS):
                best[m] = jnp.maximum(
                    best[m], jnp.where(linked, s_ref[m : m + 1, k : k + 128], -3e38)
                )
        for m in range(HEADS):
            t = t_cols[r : r + step, HEADS + m : HEADS + m + 1]
            top = leaky2(t + jnp.max(best[m], axis=1, keepdims=True))[0]
            o_ref[0, r : r + step, m : m + 1] = t
            o_ref[0, r : r + step, HEADS + m : HEADS + m + 1] = top


def row_tops(idx, adjacency, s_rel, nb2):
    rows, src = adjacency.shape[1:]
    return pl.pallas_call(
        top_kernel,
        grid_spec=pltpu.PrefetchScalarGridSpec(
            num_scalar_prefetch=1,
            grid=(nb2,),
            in_specs=[
                pl.BlockSpec((1, rows, src), lambda b, i: (i[0] * nb2 + b, 0, 0)),
                pl.BlockSpec((8, src), lambda b, i: (0, b)),
            ],
            out_specs=pl.BlockSpec((1, rows, 8), lambda b, i: (b, 0, 0)),
        ),
        out_shape=jax.ShapeDtypeStruct((nb2, rows, 8), F32),
        compiler_params=params("arbitrary"),
        cost_estimate=cost(2 * nb2 * rows * src * 9, nb2 * rows * src * 4),
        name="row_tops",
    )(idx, adjacency, s_rel)


def forward_kernel(
    pair,
    idx_ref,
    xo_ref,
    xs_ref,
    adj_ref,
    s_ref,
    tm_ref,
    wp_ref,
    ws_ref,
    wh_ref,
    wl_ref,
    a_ref,
    u_ref,
    linv_ref,
    pre_ref,
    lacc,
):
    j = pl.program_id(1)
    rows = adj_ref.shape[1]
    x = split2(jnp.concatenate([xo_ref[...], xs_ref[...]], axis=1))

    @pl.when(j == 0)
    def _():
        u_ref[...] = jnp.zeros_like(u_ref)
        lacc[...] = jnp.zeros_like(lacc)
        head_rows = (x[0][:rows], x[1][:rows])
        pre_ref[0] = dot3(head_rows, split2(ws_ref[...]), NN)

    step = 32
    for a in range(2):
        m = 2 * pair + a
        s = s_ref[m : m + 1, :]
        for r in range(0, rows, step):
            t = tm_ref[0, r : r + step, m : m + 1]
            top = tm_ref[0, r : r + step, HEADS + m : HEADS + m + 1]
            q, y = leaky2(t + s)
            w = jnp.where(adj_ref[0, r : r + step, :] > 0, jnp.exp2(q - top), 0.0)
            hi, lo = split2(w)
            at = a * rows + r
            wh_ref[0, at : at + step, :] = hi
            wl_ref[0, at : at + step, :] = lo
            a_ref[0, at : at + step, :] = w - 0.8 * w * jnp.exp2(-jnp.log2(y))
            lacc[at : at + step, :] += lane_groups(w)
    u_ref[0] += dot3((wh_ref[0], wl_ref[0]), x, NN)

    @pl.when(j == pl.num_programs(1) - 1)
    def _():
        linv = 1.0 / jnp.sum(lacc[...], axis=1, keepdims=True)
        linv_ref[0] = jnp.broadcast_to(linv, linv_ref.shape[1:])
        for a in range(2):
            mixed = split2(u_ref[0, a * rows : (a + 1) * rows, :] * linv[a * rows : (a + 1) * rows])
            cols = slice(a * HD, (a + 1) * HD)
            pre_ref[0, :, cols] += dot3(mixed, split2(wp_ref[:, cols]), NN)


def forward_pair(pair, idx, features, x_sib, adjacency, s_rel, tm, wp, ws, nb2):
    rows, src = adjacency.shape[1:]
    cols = features.shape[1]
    kd = 2 * cols
    nj = src // TJ
    two = 2 * rows
    whole = lambda shape: pl.BlockSpec(shape, lambda b, j, i: (0,) * len(shape))
    return pl.pallas_call(
        functools.partial(forward_kernel, pair),
        grid_spec=pltpu.PrefetchScalarGridSpec(
            num_scalar_prefetch=1,
            grid=(nb2, nj),
            in_specs=[
                pl.BlockSpec((TJ, cols), lambda b, j, i: ((i[0] * nb2 + b) * nj + j, 0)),
                pl.BlockSpec((TJ, cols), lambda b, j, i: (b * nj + j, 0)),
                pl.BlockSpec((1, rows, TJ), lambda b, j, i: (i[0] * nb2 + b, 0, j)),
                pl.BlockSpec((8, TJ), lambda b, j, i: (0, b * nj + j)),
                pl.BlockSpec((1, rows, 8), lambda b, j, i: (b, 0, 0)),
                whole((kd, 2 * HD)),
                whole((kd, 2 * HD)),
            ],
            out_specs=[
                pl.BlockSpec((1, two, TJ), lambda b, j, i: (b, 0, j)),
                pl.BlockSpec((1, two, TJ), lambda b, j, i: (b, 0, j)),
                pl.BlockSpec((1, two, TJ), lambda b, j, i: (b, 0, j)),
                pl.BlockSpec((1, two, kd), lambda b, j, i: (b, 0, 0)),
                pl.BlockSpec((1, two, 128), lambda b, j, i: (b, 0, 0)),
                pl.BlockSpec((1, rows, 2 * HD), lambda b, j, i: (b, 0, 0)),
            ],
            scratch_shapes=[pltpu.VMEM((two, 128), F32)],
        ),
        out_shape=[
            jax.ShapeDtypeStruct((nb2, two, src), BF16),
            jax.ShapeDtypeStruct((nb2, two, src), BF16),
            jax.ShapeDtypeStruct((nb2, two, src), F32),
            jax.ShapeDtypeStruct((nb2, two, kd), F32),
            jax.ShapeDtypeStruct((nb2, two, 128), F32),
            jax.ShapeDtypeStruct((nb2, rows, 2 * HD), F32),
        ],
        compiler_params=params("arbitrary", "arbitrary"),
        cost_estimate=cost(6 * nb2 * two * src * kd, nb2 * src * (kd * 4 + two * 9)),
        name="forward_pair",
    )(idx, features, x_sib, adjacency, s_rel, tm, wp, ws)


def live_rows(idx_ref, counts_ref, nb2, rows):
    parts = []
    for b in range(nb2):
        row = lax.broadcasted_iota(jnp.int32, (rows, 1), 0)
        parts.append((row < counts_ref[idx_ref[0] * nb2 + b]).astype(F32))
    return jnp.concatenate(parts, axis=0)


def stats_kernel(nb2, idx_ref, counts_ref, part_ref, recv_ref, ca_ref, cb_ref, par_ref, pre_ref, o_ref):
    rows = part_ref.shape[0] // nb2
    live = live_rows(idx_ref, counts_ref, nb2, rows)
    bias = par_ref[0:1, :]
    pre = part_ref[...] + recv_ref[...] + bias
    pre_ref[...] = pre
    act = (elu(pre) - elu(bias)) * live
    g = jnp.concatenate([ca_ref[...], cb_ref[...]], axis=1) * live
    total = lambda v: jnp.sum(v, axis=0, keepdims=True)
    o_ref[0:1, :] = total(act)
    o_ref[1:2, :] = total(act * act)
    o_ref[2:3, :] = total(g)
    o_ref[3:4, :] = total(g * act)
    o_ref[4:5, :] = jnp.broadcast_to(total(live), (1, pre.shape[1]))
    o_ref[5:8, :] = jnp.zeros((3, pre.shape[1]), F32)


def apply_kernel(
    nb2, idx_ref, counts_ref, pre_ref, ca_ref, cb_ref, par_ref, st_ref, act_ref, d_ref, o_ref
):
    rows = pre_ref.shape[0] // nb2
    live = live_rows(idx_ref, counts_ref, nb2, rows)
    bias, gamma, beta = par_ref[0:1, :], par_ref[1:2, :], par_ref[2:3, :]
    count = st_ref[4:5, :]
    mean = st_ref[0:1, :] / count
    inv = lax.rsqrt(st_ref[1:2, :] / count - mean * mean + eps)
    grad_beta = st_ref[2:3, :]
    grad_gamma = inv * (st_ref[3:4, :] - mean * grad_beta)
    pre = pre_ref[...]
    nrm = (elu(pre) - elu(bias) - mean) * inv
    act_ref[...] = live * (gamma * nrm + beta)
    g = jnp.concatenate([ca_ref[...], cb_ref[...]], axis=1) * live
    d = live * (gamma * inv) * (g - grad_beta / count - nrm * (grad_gamma / count))
    d = d * jnp.exp(jnp.minimum(pre, 0.0))
    d_ref[...] = d
    o_ref[0:1, :] = grad_gamma
    o_ref[1:2, :] = grad_beta
    o_ref[2:3, :] = jnp.sum(d, axis=0, keepdims=True)
    o_ref[3:8, :] = jnp.zeros((5, pre.shape[1]), F32)


def small_call(kernel, name, idx, counts, arrays, outs):
    spec = lambda shape: pl.BlockSpec(shape, lambda *_: (0,) * len(shape))
    return pl.pallas_call(
        kernel,
        grid_spec=pltpu.PrefetchScalarGridSpec(
            num_scalar_prefetch=2,
            grid=(1,),
            in_specs=[spec(v.shape) for v in arrays],
            out_specs=[spec(s) for s in outs],
        ),
        out_shape=[jax.ShapeDtypeStruct(s, F32) for s in outs],
        compiler_params=params("arbitrary"),
        cost_estimate=cost(1e6, 4e6),
        name=name,
    )(idx, counts, *arrays)


def back_kernel(
    idx_ref, xo_ref, xs_ref, a_ref, d_ref, linv_ref, u_ref, wp_ref, vh_ref, vl_ref, ds_ref, dt_ref, delta, tacc
):
    j = pl.program_id(1)
    rows = d_ref.shape[0]

    @pl.when(j == 0)
    def _():
        tacc[...] = jnp.zeros_like(tacc)
        for a in range(2):
            at = slice(a * rows, (a + 1) * rows)
            cols = slice(a * HD, (a + 1) * HD)
            d = split2(d_ref[:, cols] * linv_ref[0, at, 0:1])
            v = dot3(d, split2(wp_ref[:, cols]), NT)
            hi, lo = split2(v)
            vh_ref[0, at, :] = hi
            vl_ref[0, at, :] = lo
            delta[at, :] = jnp.broadcast_to(
                jnp.sum(v * u_ref[0, at, :], axis=1, keepdims=True), (rows, 128)
            ) * linv_ref[0, at, :]

    x = split2(jnp.concatenate([xo_ref[...], xs_ref[...]], axis=1))
    dp = dot3((vh_ref[0], vl_ref[0]), x, NT)
    step = 32
    for a in range(2):
        total = None
        for r in range(0, rows, step):
            at = slice(a * rows + r, a * rows + r + step)
            dv = a_ref[0, at, :] * (dp[at, :] - delta[at, 0:1])
            tacc[at, :] += lane_groups(dv)
            total = dv if total is None else total + dv
        ds_ref[0, a : a + 1, :] = jnp.sum(total, axis=0, keepdims=True)

    @pl.when(j == pl.num_programs(1) - 1)
    def _():
        for a in range(2):
            sums = jnp.sum(tacc[a * rows : (a + 1) * rows, :], axis=1, keepdims=True)
            turned = jnp.transpose(jnp.broadcast_to(sums, (rows, 128)))
            dt_ref[0, a : a + 1, :] = turned[0:1, :]


def back_pair(idx, features, x_sib, att, d, linv, u, wp, nb2):
    two, src = att.shape[1:]
    rows = two // 2
    cols = features.shape[1]
    kd = 2 * cols
    nj = src // TJ
    return pl.pallas_call(
        back_kernel,
        grid_spec=pltpu.PrefetchScalarGridSpec(
            num_scalar_prefetch=1,
            grid=(nb2, nj),
            in_specs=[
                pl.BlockSpec((TJ, cols), lambda b, j, i: ((i[0] * nb2 + b) * nj + j, 0)),
                pl.BlockSpec((TJ, cols), lambda b, j, i: (b * nj + j, 0)),
                pl.BlockSpec((1, two, TJ), lambda b, j, i: (b, 0, j)),
                pl.BlockSpec((rows, 2 * HD), lambda b, j, i: (b, 0)),
                pl.BlockSpec((1, two, 128), lambda b, j, i: (b, 0, 0)),
                pl.BlockSpec((1, two, kd), lambda b, j, i: (b, 0, 0)),
                pl.BlockSpec((kd, 2 * HD), lambda b, j, i: (0, 0)),
            ],
            out_specs=[
                pl.BlockSpec((1, two, kd), lambda b, j, i: (b, 0, 0)),
                pl.BlockSpec((1, two, kd), lambda b, j, i: (b, 0, 0)),
                pl.BlockSpec((1, 2, TJ), lambda b, j, i: (b, 0, j)),
                pl.BlockSpec((1, 2, rows), lambda b, j, i: (b, 0, 0)),
            ],
            scratch_shapes=[pltpu.VMEM((two, 128), F32), pltpu.VMEM((two, 128), F32)],
        ),
        out_shape=[
            jax.ShapeDtypeStruct((nb2, two, kd), BF16),
            jax.ShapeDtypeStruct((nb2, two, kd), BF16),
            jax.ShapeDtypeStruct((nb2, 2, src), F32),
            jax.ShapeDtypeStruct((nb2, 2, rows), F32),
        ],
        compiler_params=params("arbitrary", "arbitrary"),
        cost_estimate=cost(6 * nb2 * two * src * kd, nb2 * src * (kd * 4 + two * 4)),
        name="back_pair",
    )(idx, features, x_sib, att, d, linv, u, wp)


def weight_kernel(idx_ref, xo_ref, xs_ref, d_ref, linv_ref, u_ref, gp_ref, gs_ref):
    rows = d_ref.shape[0]

    @pl.when(pl.program_id(0) == 0)
    def _():
        gp_ref[...] = jnp.zeros_like(gp_ref)
        gs_ref[...] = jnp.zeros_like(gs_ref)

    for a in range(2):
        at = slice(a * rows, (a + 1) * rows)
        cols = slice(a * HD, (a + 1) * HD)
        d = split2(d_ref[:, cols] * linv_ref[0, at, 0:1])
        gp_ref[:, cols] += dot3(split2(u_ref[0, at, :]), d, TN)
    x = split2(jnp.concatenate([xo_ref[...], xs_ref[...]], axis=1))
    gs_ref[...] += dot3(x, split2(d_ref[...]), TN)


def weight_pair(idx, features, x_sib, d, linv, u, src, nb2):
    two, kd = u.shape[1:]
    rows = two // 2
    cols = features.shape[1]
    per = src // rows
    return pl.pallas_call(
        weight_kernel,
        grid_spec=pltpu.PrefetchScalarGridSpec(
            num_scalar_prefetch=1,
            grid=(nb2,),
            in_specs=[
                pl.BlockSpec((rows, cols), lambda b, i: ((i[0] * nb2 + b) * per, 0)),
                pl.BlockSpec((rows, cols), lambda b, i: (b * per, 0)),
                pl.BlockSpec((rows, 2 * HD), lambda b, i: (b, 0)),
                pl.BlockSpec((1, two, 128), lambda b, i: (b, 0, 0)),
                pl.BlockSpec((1, two, kd), lambda b, i: (b, 0, 0)),
            ],
            out_specs=[pl.BlockSpec((kd, 2 * HD), lambda b, i: (0, 0))] * 2,
        ),
        out_shape=[jax.ShapeDtypeStruct((kd, 2 * HD), F32)] * 2,
        compiler_params=params("arbitrary"),
        cost_estimate=cost(6 * nb2 * 4 * rows * kd * HD, nb2 * two * kd * 4),
        name="weight_pair",
    )(idx, features, x_sib, d, linv, u)


def thin_kernel(idx_ref, xo_ref, xs_ref, ds_ref, o_ref):
    @pl.when((pl.program_id(0) == 0) & (pl.program_id(1) == 0))
    def _():
        o_ref[...] = jnp.zeros_like(o_ref)

    x = split2(jnp.concatenate([xo_ref[...], xs_ref[...]], axis=1))
    d = ds_ref[0]
    hi = d.astype(BF16).astype(F32)
    stack = jnp.concatenate([hi, d - hi], axis=0).astype(BF16)
    r1 = dot(stack, x[0], NN)
    r2 = dot(stack, x[1], NN)
    o_ref[...] += r1[:8] + (r1[8:] + r2[:8])


def thin_sums(idx, features, x_sib, ds8, nb2):
    src = ds8.shape[2]
    cols = features.shape[1]
    nj = src // TJ
    return pl.pallas_call(
        thin_kernel,
        grid_spec=pltpu.PrefetchScalarGridSpec(
            num_scalar_prefetch=1,
            grid=(nb2, nj),
            in_specs=[
                pl.BlockSpec((TJ, cols), lambda b, j, i: ((i[0] * nb2 + b) * nj + j, 0)),
                pl.BlockSpec((TJ, cols), lambda b, j, i: (b * nj + j, 0)),
                pl.BlockSpec((1, 8, TJ), lambda b, j, i: (b, 0, j)),
            ],
            out_specs=pl.BlockSpec((8, 2 * cols), lambda b, j, i: (0, 0)),
        ),
        out_shape=jax.ShapeDtypeStruct((8, 2 * cols), F32),
        compiler_params=params("arbitrary", "arbitrary"),
        cost_estimate=cost(2 * nb2 * src * cols * 64, nb2 * src * cols * 8),
        name="thin_sums",
    )(idx, features, x_sib, ds8)


def feature_kernel(
    wh0_ref, wl0_ref, wh1_ref, wl1_ref, vh0_ref, vl0_ref, vh1_ref, vl1_ref,
    ds_ref, a_ref, d0_ref, d1_ref, ws0_ref, ws1_ref, oo_ref, os_ref,
):
    j = pl.program_id(0)
    rows = d0_ref.shape[0]
    half = oo_ref.shape[1]
    out = dot3((wh0_ref[0], wl0_ref[0]), (vh0_ref[0], vl0_ref[0]), TN)
    out = out + dot3((wh1_ref[0], wl1_ref[0]), (vh1_ref[0], vl1_ref[0]), TN)
    out = out + dot(thin_rows(ds_ref[0]), thin_cols(a_ref[...]), TN)
    oo_ref[...] = out[:, :half]
    os_ref[...] = out[:, half:]

    @pl.when(j == 0)
    def _():
        skip = dot3(split2(d0_ref[...]), split2(ws0_ref[...]), NT)
        skip = skip + dot3(split2(d1_ref[...]), split2(ws1_ref[...]), NT)
        oo_ref[0:rows, :] += skip[:, :half]
        os_ref[0:rows, :] += skip[:, half:]


def feature_block(b, w0, w1, v0, v1, ds8, a_half, d0, d1, ws0, ws1):
    two, src = w0[0].shape[1:]
    kd = v0[0].shape[2]
    rows = two // 2
    half = kd // 2
    tile = pl.BlockSpec((1, two, TJ), lambda j: (b, 0, j))
    vals = pl.BlockSpec((1, two, kd), lambda j: (b, 0, 0))
    dspec = pl.BlockSpec((rows, 2 * HD), lambda j: (b, 0))
    wspec = pl.BlockSpec((kd, 2 * HD), lambda j: (0, 0))
    return pl.pallas_call(
        feature_kernel,
        grid=(src // TJ,),
        in_specs=[tile] * 4
        + [vals] * 4
        + [
            pl.BlockSpec((1, 8, TJ), lambda j: (b, 0, j)),
            pl.BlockSpec((8, kd), lambda j: (0, 0)),
            dspec,
            dspec,
            wspec,
            wspec,
        ],
        out_specs=[pl.BlockSpec((TJ, half), lambda j: (j, 0))] * 2,
        out_shape=[jax.ShapeDtypeStruct((src, half), F32)] * 2,
        compiler_params=params("arbitrary"),
        cost_estimate=cost(12 * two * src * kd, src * two * 8 + src * kd * 4),
        name="feature_block",
    )(*w0, *w1, *v0, *v1, ds8, a_half, d0, d1, ws0, ws1)


def last_kernel(idx_ref, gp_ref, gs_ref, q_ref, att_ref, op_ref, os_ref):
    op_ref[...] = gp_ref[0, 0, 0] + dot(thin_rows(q_ref[0]), thin_cols(att_ref[...]), TN)
    os_ref[...] = gs_ref[0, 0, 0]


def last_step(idx, grads, q_own, att):
    cols = grads.shape[-1]
    pick = lambda mat: lambda r, i: ((r ^ i[1]) // 2, mat, (r ^ i[1]) % 2, 0, 0)
    return pl.pallas_call(
        last_kernel,
        grid_spec=pltpu.PrefetchScalarGridSpec(
            num_scalar_prefetch=1,
            grid=(HEADS,),
            in_specs=[
                pl.BlockSpec((1, 1, 1) + grads.shape[3:], pick(0)),
                pl.BlockSpec((1, 1, 1) + grads.shape[3:], pick(1)),
                pl.BlockSpec((1, 8, q_own.shape[2]), lambda r, i: (r, 0, 0)),
                pl.BlockSpec((8, cols), lambda r, i: (0, 0)),
            ],
            out_specs=[pl.BlockSpec(grads.shape[3:], lambda r, i: (r, 0))] * 2,
        ),
        out_shape=[jax.ShapeDtypeStruct((HEADS * grads.shape[3], cols), F32)] * 2,
        compiler_params=params("arbitrary"),
        cost_estimate=cost(1e6, 4e6),
        name="last_step",
    )(idx, grads, grads, q_own, att)


def swap_bits(v, h, axis=0):
    shape = v.shape
    pairs = v.reshape(shape[:axis] + (2, 2) + shape[axis + 1 :])
    pairs = jnp.where((h & 1) > 0, jnp.flip(pairs, axis + 1), pairs)
    pairs = jnp.where((h & 2) > 0, jnp.flip(pairs, axis), pairs)
    return pairs.reshape(shape)


def make_step(dp_size):
    def on_device(
        features, adjacency, seed_counts, w_proj, w_skip, attn_src, attn_dst, bias, gamma, beta, cotangent
    ):
        nb, rows, src = adjacency.shape
        cols = features.shape[1]
        nb2 = nb // 2
        h = lax.axis_index("head")
        dpi = lax.axis_index("dp")
        core, side = h & 1, h >> 1
        idx = jnp.stack([core, h]).astype(jnp.int32)

        def to_core(v):
            return lax.ppermute(v, "head", [(i, i ^ 1) for i in range(HEADS)])

        def to_cross(v):
            return lax.ppermute(v, "head", [(i, i ^ 2) for i in range(HEADS)])

        def to_dp(v, bit):
            return lax.ppermute(v, "dp", [(i, i ^ bit) for i in range(dp_size)])

        bits = [1 << k for k in range(dp_size.bit_length() - 1)]

        def other_half(v, axis=0):
            size = v.shape[axis] // 2
            return lax.dynamic_slice_in_dim(v, (1 - core) * size, size, axis)

        def own_half(v, axis=0):
            size = v.shape[axis] // 2
            return lax.dynamic_slice_in_dim(v, core * size, size, axis)

        def chip_order(mine, theirs):
            return jnp.where(
                core == 0, jnp.concatenate([mine, theirs]), jnp.concatenate([theirs, mine])
            )

        with jax.named_scope("fold_attention"):
            folded = jnp.stack(
                [jnp.sum(w_proj * attn_src, axis=1), jnp.sum(w_proj * attn_dst, axis=1)]
            )
            slot = (jnp.arange(HEADS) == h)[None, :, None]
            a_all = jnp.where(slot, folded[:, None, :], 0.0)
            a_all = a_all + to_core(a_all)
            a_all = a_all + to_cross(a_all)
            a_all = a_all.reshape(2 * HEADS, -1)

        with jax.named_scope("share_inputs"):
            x_sib = to_core(other_half(features))
            small = jnp.stack([bias, gamma, beta])
            par = jnp.concatenate([small, to_core(small)], axis=1)
            par = jnp.pad(par, ((0, 5), (0, 0)))
            cot_own = own_half(cotangent)
            cot_sib = to_core(other_half(cotangent))
            chunks = jnp.stack([w_proj, w_skip]).reshape(2, HEADS, cols, -1)
            chunks = swap_bits(chunks, h, 1)
            far = to_cross(chunks[:, 2:])
            near = to_core(jnp.stack([chunks[:, 1::-1], far[:, ::-1]]))
            w_pairs = [
                jnp.concatenate([chunks[:, :2], near[0]], axis=3).reshape(2, 2 * cols, 2 * HD),
                jnp.concatenate([far, near[1]], axis=3).reshape(2, 2 * cols, 2 * HD),
            ]

        with jax.named_scope("scores"):
            a_own = lax.dynamic_slice_in_dim(a_all, h * cols, cols, 1)
            part = scores(features, a_own * LOG2E)
            s_nat = own_half(part, 1) + to_core(other_half(part, 1))
            s_nat = s_nat + to_cross(s_nat)
            s_rel = swap_bits(s_nat.reshape(2, HEADS, -1), h, 1).reshape(2 * HEADS, -1)
            tm = row_tops(idx, adjacency, s_rel, nb2)

        with jax.named_scope("forward"):
            far_pair = forward_pair(
                1, idx, features, x_sib, adjacency, s_rel, tm, w_pairs[1][0], w_pairs[1][1], nb2
            )
            recv = to_cross(far_pair[5])
            own_pair = forward_pair(
                0, idx, features, x_sib, adjacency, s_rel, tm, w_pairs[0][0], w_pairs[0][1], nb2
            )

        with jax.named_scope("norm"):
            flat = (nb2 * rows, 2 * HD)
            pre, stats = small_call(
                lambda *r: stats_kernel(nb2, *r),
                "norm_sums",
                idx,
                seed_counts,
                [own_pair[5].reshape(flat), recv.reshape(flat), cot_own, cot_sib, par],
                [flat, (8, 2 * HD)],
            )
            stats = stats + to_core(jnp.concatenate([stats[:, HD:], stats[:, :HD]], axis=1))
            for bit in bits:
                stats = stats + to_dp(stats, bit)
            act, d_own, small_grads = small_call(
                lambda *r: apply_kernel(nb2, *r),
                "norm_apply",
                idx,
                seed_counts,
                [pre, cot_own, cot_sib, par, stats],
                [flat, flat, (8, 2 * HD)],
            )
            activations = chip_order(act[:, :HD], to_core(act[:, HD:]))
            grad_gamma, grad_beta = small_grads[0, :HD], small_grads[1, :HD]

        with jax.named_scope("backward"):
            d_far = to_cross(d_own)
            back_own = back_pair(
                idx, features, x_sib, own_pair[2], d_own, own_pair[4], own_pair[3], w_pairs[0][0], nb2
            )
            grads_own = weight_pair(idx, features, x_sib, d_own, own_pair[4], own_pair[3], src, nb2)
            grads_far = weight_pair(idx, features, x_sib, d_far, far_pair[4], far_pair[3], src, nb2)
            back_far = back_pair(
                idx, features, x_sib, far_pair[2], d_far, far_pair[4], far_pair[3], w_pairs[1][0], nb2
            )

        with jax.named_scope("weight_sums"):
            pairs = jnp.stack([jnp.stack(grads_own), jnp.stack(grads_far)])
            pairs = pairs.reshape(2, 2, 2, cols, 2 * HD)
            total = pairs[..., :HD] + to_core(pairs[:, :, ::-1, :, HD:])
            total = total.reshape(2, 4 * cols, HD)
            for bit in bits:
                size = total.shape[1] // 2
                up = (dpi & bit) > 0
                low, high = total[:, :size], total[:, size:]
                total = jnp.where(up, high, low) + to_dp(jnp.where(up, low, high), bit)
            total = jnp.stack([total[0], to_cross(total[1])])
            for bit in bits[::-1]:
                up = (dpi & bit) > 0
                more = to_dp(total, bit)
                total = jnp.where(
                    up,
                    jnp.concatenate([more, total], axis=1),
                    jnp.concatenate([total, more], axis=1),
                )
            total = total.reshape(2, 2, 2, cols, HD)

        with jax.named_scope("score_grads"):
            ds = jnp.stack([back_own[2], back_far[2]], axis=1)
            dt = jnp.stack([back_own[3], back_far[3]], axis=1)
            both = jnp.concatenate([ds, dt], axis=3)
            both = both + to_cross(both)[:, ::-1]
            both = both.reshape(nb2, HEADS, src + rows)
            ds8 = jnp.concatenate(
                [both[:, :, :src], jnp.pad(both[:, :, src:], ((0, 0), (0, 0), (0, src - rows)))], axis=1
            )
            q = thin_sums(idx, features, x_sib, ds8, nb2)
            q = swap_bits(q.reshape(2, HEADS, 2 * cols), h, 1).reshape(2 * HEADS, 2, cols)
            q = jnp.where(core == 0, q, q[:, ::-1])
            tail = jnp.concatenate([q.reshape(-1), small_grads[2, :HD], small_grads[2, HD:]])
            tail = tail.reshape(-1, cols)
            body, edge = tail[:-2], tail[-2:]
            tail = tail + to_core(jnp.concatenate([body, edge[::-1]]))
            for bit in bits:
                tail = tail + to_dp(tail, bit)
            grad_bias = tail[-2]
            q = tail[:-2].reshape(2 * HEADS, 2, cols)
            q_far = to_cross(q)
            q = jnp.where(side == 0, jnp.concatenate([q, q_far], 1), jnp.concatenate([q_far, q], 1))
            q_own = lax.dynamic_index_in_dim(q.reshape(2, HEADS, HEADS, cols), h, 1, False)

        with jax.named_scope("feature_grads"):
            half_cols = lambda i: lax.dynamic_slice_in_dim(a_all, i * cols, cols, 1)
            a_half = jnp.concatenate([half_cols(h), half_cols(h ^ 1)], axis=1)
            a_half = swap_bits(a_half.reshape(2, HEADS, -1), h, 1).reshape(2 * HEADS, -1)
            grad_features = jnp.zeros(features.shape, F32)
            for b in range(nb2):
                mine, theirs = feature_block(
                    b,
                    own_pair[:2],
                    far_pair[:2],
                    back_own[:2],
                    back_far[:2],
                    ds8,
                    a_half,
                    d_own,
                    d_far,
                    w_pairs[0][1],
                    w_pairs[1][1],
                )
                theirs = to_core(theirs)
                at = (core * nb2 + b) * src
                grad_features = lax.dynamic_update_slice_in_dim(grad_features, mine, at, 0)
                at = ((1 - core) * nb2 + b) * src
                grad_features = lax.dynamic_update_slice_in_dim(grad_features, theirs, at, 0)

        with jax.named_scope("last"):
            att = jnp.pad(jnp.stack([attn_src, attn_dst]), ((0, 6), (0, 0)))
            q8 = jnp.pad(q_own.transpose(1, 0, 2), ((0, 0), (0, 6), (0, 0)))
            grad_proj, grad_skip = last_step(idx, total, q8, att)
            flat_q = q_own.reshape(2, -1)
            grad_att = jnp.dot(flat_q, w_proj, precision=lax.Precision.HIGHEST)

        return (
            activations,
            grad_features,
            grad_proj,
            grad_skip,
            grad_att[0],
            grad_att[1],
            grad_bias,
            grad_gamma,
            grad_beta,
        )

    return on_device


def solution(mesh):
    return jax.shard_map(
        make_step(mesh.shape["dp"]),
        mesh=mesh,
        in_specs=(
            P("dp", "head"),
            P("dp", None, None),
            P("dp"),
            P(None, "head"),
            P(None, "head"),
            P("head"),
            P("head"),
            P("head"),
            P("head"),
            P("head"),
            P("dp", "head"),
        ),
        out_specs=(
            P("dp", "head"),
            P("dp", "head"),
            P(None, "head"),
            P(None, "head"),
            P("head"),
            P("head"),
            P("head"),
            P("head"),
            P("head"),
        ),
        check_vma=False,
    )
```

```python
import functools

import jax
import jax.numpy as jnp
from jax import lax
from jax.experimental import pallas as pl
from jax.experimental.pallas import tpu as pltpu
from jax.sharding import PartitionSpec as P

HD = 256
HEADS = 4
TJ = 512
EXTRA = 16
eps = 1e-05
LOG2E = 1.4426950408889634
HALF_LN2 = 0.34657359027997264
F32 = jnp.float32
BF16 = jnp.bfloat16
NN = ((1,), (0,))
NT = ((1,), (1,))
TN = ((0,), (0,))
LOW = -3e38
HBM = pl.BlockSpec(memory_space=pltpu.HBM)
ANY = pl.BlockSpec(memory_space=pl.ANY)


def dot(a, b, form):
    return lax.dot_general(a, b, (form, ((), ())), preferred_element_type=F32)


def split2(x):
    hi = x.astype(BF16)
    return hi, (x - hi.astype(F32)).astype(BF16)


def dot3(a, b, form):
    return dot(a[0], b[0], form) + (dot(a[0], b[1], form) + dot(a[1], b[0], form))


def cat3(a, axis, mixed):
    hi, lo = a
    return jnp.concatenate([hi, lo, hi] if mixed else [hi, hi, lo], axis=axis)


def thin_rows(d):
    hi = d.astype(BF16).astype(F32)
    return jnp.concatenate([hi, hi, d - hi, jnp.zeros_like(d)], axis=0).astype(BF16)


def thin_cols(a):
    hi = a.astype(BF16).astype(F32)
    return jnp.concatenate([hi, a - hi, hi, jnp.zeros_like(a)], axis=0).astype(BF16)


def lane_groups(v):
    out = v[:, :128]
    for k in range(128, v.shape[1], 128):
        out = out + v[:, k : k + 128]
    return out


def leaky2(u):
    soft = jnp.log2(1.0 + jnp.exp2(jnp.minimum(u, 126.0)))
    return jnp.maximum(u, 0.2 * u + 0.8 * soft)


def elu(v):
    return jnp.where(v > 0, v, jnp.exp(jnp.minimum(v, 0.0)) - 1.0)


def flip_rows(v, bit):
    return jnp.concatenate([v[m ^ bit : (m ^ bit) + 1] for m in range(8)], axis=0)


def large(v, least):
    return v.size * v.dtype.itemsize >= least


def far_memory(v, least):
    return pltpu.with_memory_space_constraint(v, pltpu.HBM) if large(v, least) else v


def call(kernel, name, grid, ins, outs, scratch=(), after=(), work=(1e6, 1e6), vmem=8, aliases=None, least=2**18):
    n_in = len(ins)
    n_after = len(after)
    ins = [(far_memory(v, least), spec) for v, spec in ins]
    after = [far_memory(v, least) for v in after]

    def body(*refs):
        kernel(*refs[:n_in], *refs[n_in + n_after :])

    return pl.pallas_call(
        body,
        grid_spec=pltpu.PrefetchScalarGridSpec(
            num_scalar_prefetch=1,
            grid=grid,
            in_specs=[s for _, s in ins[1:]] + [ANY] * n_after,
            out_specs=[s for _, s in outs],
            scratch_shapes=list(scratch),
        ),
        out_shape=[pltpu.HBM(s.shape, s.dtype) if large(s, least) else s for s, _ in outs],
        compiler_params=pltpu.CompilerParams(
            dimension_semantics=("arbitrary",) * len(grid), vmem_limit_bytes=vmem * 2**20
        ),
        cost_estimate=pl.CostEstimate(
            flops=int(work[0] * 0.01), bytes_accessed=int(work[1] * 0.01), transcendentals=0
        ),
        input_output_aliases=aliases or {},
        name=name,
    )(*[v for v, _ in ins], *after)


def shape(*dims, dtype=F32):
    return jax.ShapeDtypeStruct(dims, dtype)


def whole(*dims):
    return pl.BlockSpec(dims, lambda *_: (0,) * len(dims))


def pack_kernel(n, stacked, idx_ref, *refs):
    for k in range(n):
        if stacked:
            refs[n][k] = refs[k][...]
        else:
            refs[n + k][...] = refs[k][...]


def pack(idx, which, arrays, after=(), steps=1, stacked=False):
    n = len(arrays)
    ins, outs = [(idx, None)], []
    for v in arrays:
        rows = v.shape[0] // 2
        dims = (rows // steps, v.shape[1])
        ins.append((v, pl.BlockSpec(dims, lambda j, i: (i[which] * steps + j, 0))))
        outs.append((shape(rows, v.shape[1]), pl.BlockSpec(dims, lambda j, i: (j, 0))))
    if stacked:
        outs = [(shape(n, rows, v.shape[1]), whole(n, rows, v.shape[1]))]
    out = call(
        functools.partial(pack_kernel, n, stacked),
        "pack",
        (steps,),
        ins,
        outs,
        after=after,
        work=(1e3, sum(v.size for v in arrays) * 4),
        least=2**18,
        vmem=12,
    )
    return out[0] if stacked else out


def relay_kernel(idx_ref, v_ref, o_ref):
    o_ref[...] = v_ref[...]


def relay(idx, v, after=()):
    return call(
        relay_kernel,
        "relay",
        (1,),
        [(idx, None), (v, whole(*v.shape))],
        [(shape(*v.shape), whole(*v.shape))],
        after=after,
        work=(1e3, v.size * 8),
        least=3 * 2**19,
        vmem=12,
    )[0]


def score_kernel(idx_ref, x_ref, a_ref, send_ref, keep_ref):
    x = x_ref[...]
    x1 = x.astype(BF16)
    rest = x - x1.astype(F32)
    x2 = rest.astype(BF16)
    x3 = (rest - x2.astype(F32)).astype(BF16)
    a = a_ref[...]
    a1 = a.astype(BF16).astype(F32)
    a2 = (a - a1).astype(BF16).astype(F32)
    a3 = (a - a1) - a2
    stack = jnp.concatenate([a1, a2, a3, jnp.zeros_like(a)], axis=0).astype(BF16)
    r1 = dot(stack, x1, NT)
    r2 = dot(stack[:16], x2, NT)
    r3 = dot(stack[:16], x3, NT)
    s = r1[:8] + (r1[8:16] + r2[:8]) + (r1[16:24] + r2[8:16] + r3[:8])

    @pl.when(pl.program_id(0) == 0)
    def _():
        send_ref[...] = flip_rows(s, 1)

    @pl.when(pl.program_id(0) == 1)
    def _():
        keep_ref[...] = s


def scores(idx, features, a_own, after=()):
    rows, cols = features.shape
    tile = 2048
    n = rows // 2 // tile
    return call(
        score_kernel,
        "scores",
        (2, n),
        [
            (idx, None),
            (features, pl.BlockSpec((tile, cols), lambda g, i, s: ((s[0] ^ 1 ^ g) * n + i, 0))),
            (a_own, whole(8, cols)),
        ],
        [
            (shape(8, rows // 2), pl.BlockSpec((8, tile), lambda g, i, s: (0, i * (1 - g) + (n - 1) * g))),
            (shape(8, rows // 2), pl.BlockSpec((8, tile), lambda g, i, s: (0, i * g))),
        ],
        after=after,
        vmem=16,
        work=(2 * rows * cols * 24, rows * cols * 4),
    )


def forward_kernel(
    blk, nb2, idx_ref, adj_ref, sa_ref, sb_ref, feat_ref, xsib_ref,
    u_ref, linv_ref, tm_ref, s_ref, who_ref, wlo_ref,
    xbuf, xh, xl, wh0, wh1, wl0, wl1, sems, out_sems,
):
    rows, src = adj_ref.shape[1], adj_ref.shape[2]
    cols = feat_ref.shape[1]
    wh, wl = (wh0, wh1), (wl0, wl1)
    own = pltpu.make_async_copy(
        feat_ref.at[pl.ds((idx_ref[0] * nb2 + blk) * src, src), :], xbuf.at[0], sems.at[0]
    )
    sib = pltpu.make_async_copy(xsib_ref.at[pl.ds(blk * src, src), :], xbuf.at[1], sems.at[1])
    own.start()
    sib.start()
    s_ref[...] = sa_ref[...] + flip_rows(sb_ref[...], 2)
    tm_ref[:, 0:8] = jnp.transpose(s_ref[:, :rows])
    step = 64

    @pl.loop(0, rows, step=step)
    def _(r):
        best = [jnp.full((step, 128), LOW, F32) for _ in range(HEADS)]
        for k in range(0, src, 128):
            linked = adj_ref[0, pl.ds(r, step), k : k + 128] > 0
            for m in range(HEADS):
                best[m] = jnp.maximum(
                    best[m], jnp.where(linked, s_ref[m : m + 1, k : k + 128], LOW)
                )
        for m in range(HEADS):
            t = tm_ref[pl.ds(r, step), HEADS + m : HEADS + m + 1]
            top = leaky2(t + jnp.max(best[m], axis=1, keepdims=True))
            tm_ref[pl.ds(r, step), m : m + 1] = top

    own.wait()
    sib.wait()

    @pl.loop(0, src, step=256)
    def _(r):
        at = pl.ds(r, 256)
        for k in range(2):
            hi, lo = split2(xbuf[k, at, :])
            xh[at, k * cols : (k + 1) * cols] = hi
            xl[at, k * cols : (k + 1) * cols] = lo

    order = [2, 3, 0, 1]

    def stores(n):
        at = pl.ds(order[n] * rows, rows)
        return (
            pltpu.make_async_copy(wh[n % 2], who_ref.at[at, :], out_sems.at[0, n % 2]),
            pltpu.make_async_copy(wl[n % 2], wlo_ref.at[at, :], out_sems.at[1, n % 2]),
        )

    for n in range(HEADS + 1):
        if n < HEADS:
            m = order[n]
            if n >= 2:
                for copy in stores(n - 2):
                    copy.wait()
            for r in range(0, rows, 32):
                at = slice(r, r + 32)
                t = tm_ref[at, HEADS + m : HEADS + m + 1]
                top = tm_ref[at, m : m + 1]
                acc = None
                for k in range(0, src, 512):
                    ks = slice(k, k + 512)
                    q = leaky2(t + s_ref[m : m + 1, ks])
                    w = jnp.where(adj_ref[0, at, ks] > 0, jnp.exp2(q - top), 0.0)
                    hi, lo = split2(w)
                    wh[n % 2][at, ks] = hi
                    wl[n % 2][at, ks] = lo
                    acc = lane_groups(w) if acc is None else acc + lane_groups(w)
                linv = 1.0 / jnp.sum(acc, axis=1, keepdims=True)
                linv_ref[m * rows + r : m * rows + r + 32, :] = jnp.broadcast_to(linv, (32, 128))
            for copy in stores(n):
                copy.start()
        if n > 0:
            p = order[n - 1]
            lhs = cat3((wh[(n - 1) % 2][...], wl[(n - 1) % 2][...]), 1, False)
            rhs = cat3((xh[...], xl[...]), 0, True)
            u_ref[p * rows : (p + 1) * rows, :] = dot(lhs, rhs, NN)
    for n in (HEADS - 2, HEADS - 1):
        for copy in stores(n):
            copy.wait()


def forward_block(blk, idx, features, x_sib, adjacency, s_mine, s_cross, nb2, after=()):
    rows, src = adjacency.shape[1:]
    cols = features.shape[1]
    kd = 2 * cols
    hr = HEADS * rows
    piece = pl.BlockSpec((8, src), lambda g, i: (0, blk))
    return call(
        functools.partial(forward_kernel, blk, nb2),
        "forward_block",
        (1,),
        [
            (idx, None),
            (adjacency, pl.BlockSpec((1, rows, src), lambda g, i: (i[0] * nb2 + blk, 0, 0))),
            (s_mine, piece),
            (s_cross, piece),
            (features, HBM),
            (x_sib, HBM),
        ],
        [
            (shape(hr, kd), whole(hr, kd)),
            (shape(hr, 128), whole(hr, 128)),
            (shape(rows, 128), whole(rows, 128)),
            (shape(8, src), whole(8, src)),
            (shape(hr, src, dtype=BF16), HBM),
            (shape(hr, src, dtype=BF16), HBM),
        ],
        scratch=[
            pltpu.VMEM((2, src, cols), F32),
            pltpu.VMEM((src, kd), BF16),
            pltpu.VMEM((src, kd), BF16),
            pltpu.VMEM((rows, src), BF16),
            pltpu.VMEM((rows, src), BF16),
            pltpu.VMEM((rows, src), BF16),
            pltpu.VMEM((rows, src), BF16),
            pltpu.SemaphoreType.DMA((2,)),
            pltpu.SemaphoreType.DMA((2, 2)),
        ],
        after=after,
        vmem=28,
        work=(6 * hr * src * kd * 2, src * kd * 4 + rows * src * 4 + hr * kd * 4),
    )


def rel_rows(ref, core):
    cols = ref.shape[1] // 2
    own = pl.ds(pl.multiple_of(core * cols, cols), cols)
    sib = pl.ds(pl.multiple_of((core ^ 1) * cols, cols), cols)
    return jnp.concatenate([ref[0, own, :], ref[0, sib, :]], axis=0)


def weight_specs(pieces, mat, cols):
    return [(p, pl.BlockSpec((1, 2 * cols, HD), lambda *_: (mat, 0, 0))) for p in pieces]


def pre_kernel(idx_ref, u_ref, linv_ref, xo_ref, xs_ref, wa_ref, wb_ref, sa_ref, sb_ref, o_ref):
    core = idx_ref[0]
    rows = xo_ref.shape[0]
    x = split2(jnp.concatenate([xo_ref[...], xs_ref[...]], axis=1))
    for a, (w_ref, s_ref) in enumerate(((wa_ref, sa_ref), (wb_ref, sb_ref))):
        at = slice(a * rows, (a + 1) * rows)
        mixed = split2(u_ref[at, :] * linv_ref[at, 0:1])
        out = dot3(mixed, split2(rel_rows(w_ref, core)), NN)
        out = out + dot3(x, split2(rel_rows(s_ref, core)), NN)
        o_ref[:, a * HD : (a + 1) * HD] = out


def pre_block(blk, pair, idx, u, linv, features, x_sib, weights, src, nb2, after=()):
    hr, kd = u.shape
    rows = hr // HEADS
    cols = features.shape[1]
    per = src // rows
    return call(
        pre_kernel,
        "pre_block",
        (1,),
        [
            (idx, None),
            (u, pl.BlockSpec((2 * rows, kd), lambda g, i: (pair, 0))),
            (linv, pl.BlockSpec((2 * rows, 128), lambda g, i: (pair, 0))),
            (features, pl.BlockSpec((rows, cols), lambda g, i: ((i[0] * nb2 + blk) * per, 0))),
            (x_sib, pl.BlockSpec((rows, cols), lambda g, i: (blk * per, 0))),
        ]
        + weight_specs(weights, 0, cols)
        + weight_specs(weights, 1, cols),
        [(shape(rows, 2 * HD), whole(rows, 2 * HD))],
        after=after,
        least=3 * 2**19,
        vmem=16,
        work=(6 * 4 * rows * kd * HD, 4e6),
    )[0]


def live_rows(idx_ref, counts_ref, nb2, rows):
    parts = []
    for b in range(nb2):
        row = lax.broadcasted_iota(jnp.int32, (rows, 1), 0)
        parts.append((row < counts_ref[idx_ref[0] * nb2 + b]).astype(F32))
    return jnp.concatenate(parts, axis=0)


def stats_kernel(nb2, idx_ref, counts_ref, ca_ref, cb_ref, pa_ref, pb_ref, *refs):
    parts, recvs = refs[:nb2], refs[nb2 : 2 * nb2]
    pre_ref, st_ref, flip_ref = refs[2 * nb2 :]
    rows = parts[0].shape[0]
    total = lambda v: jnp.sum(v, axis=0, keepdims=True)
    live = live_rows(idx_ref, counts_ref, nb2, rows)
    for a, (c_ref, p_ref) in enumerate(((ca_ref, pa_ref), (cb_ref, pb_ref))):
        cols = slice(a * HD, (a + 1) * HD)
        bias = p_ref[0:1, :]
        pre = jnp.concatenate(
            [part[:, cols] + recv[:, cols] for part, recv in zip(parts, recvs)], axis=0
        )
        pre = pre + bias
        pre_ref[:, cols] = pre
        act = (elu(pre) - elu(bias)) * live
        g = c_ref[...] * live
        rows8 = [total(act), total(act * act), total(g), total(g * act)]
        rows8.append(jnp.broadcast_to(total(live), (1, HD)))
        rows8.append(jnp.zeros((3, HD), F32))
        stats = jnp.concatenate(rows8, axis=0)
        st_ref[a] = stats
        flip_ref[1 - a] = stats


def norm_sums(idx, counts, cotangent, cot_sib, par, par_sib, parts, recvs, nb2):
    rows = parts[0].shape[0]
    full = nb2 * rows
    return call(
        functools.partial(stats_kernel, nb2),
        "norm_sums",
        (1,),
        [
            (idx, None),
            (counts, pl.BlockSpec(memory_space=pltpu.SMEM)),
            (cotangent, pl.BlockSpec((full, HD), lambda g, i: (i[0], 0))),
            (cot_sib, whole(full, HD)),
            (par, whole(8, HD)),
            (par_sib, whole(8, HD)),
        ]
        + [(v, whole(rows, 2 * HD)) for v in parts + recvs],
        [
            (shape(full, 2 * HD), whole(full, 2 * HD)),
            (shape(2, 8, HD), whole(2, 8, HD)),
            (shape(2, 8, HD), whole(2, 8, HD)),
        ],
        least=3 * 2**19,
        vmem=16,
        work=(1e6, 6e6),
    )


def apply_kernel(
    nb2, idx_ref, counts_ref, pre_ref, ca_ref, cb_ref, pa_ref, pb_ref, st_ref, act_ref, send_ref, d_ref, o_ref
):
    rows = pre_ref.shape[0] // nb2
    live = live_rows(idx_ref, counts_ref, nb2, rows)
    for a, (c_ref, p_ref, out_ref) in enumerate(
        ((ca_ref, pa_ref, act_ref), (cb_ref, pb_ref, send_ref))
    ):
        cols = slice(a * HD, (a + 1) * HD)
        bias, gamma, beta = p_ref[0:1, :], p_ref[1:2, :], p_ref[2:3, :]
        count = st_ref[a, 4:5, :]
        mean = st_ref[a, 0:1, :] / count
        inv = lax.rsqrt(st_ref[a, 1:2, :] / count - mean * mean + eps)
        grad_beta = st_ref[a, 2:3, :]
        grad_gamma = inv * (st_ref[a, 3:4, :] - mean * grad_beta)
        pre = pre_ref[:, cols]
        nrm = (elu(pre) - elu(bias) - mean) * inv
        out_ref[...] = live * (gamma * nrm + beta)
        g = c_ref[...] * live
        d = live * (gamma * inv) * (g - grad_beta / count - nrm * (grad_gamma / count))
        d = d * jnp.exp(jnp.minimum(pre, 0.0))
        d_ref[:, cols] = d
        o_ref[a, 0:1, :] = grad_gamma
        o_ref[a, 1:2, :] = grad_beta
        o_ref[a, 2:3, :] = jnp.sum(d, axis=0, keepdims=True)
        o_ref[a, 3:8, :] = jnp.zeros((5, HD), F32)


def norm_apply(idx, counts, pre, cotangent, cot_sib, par, par_sib, stats, nb2):
    full = pre.shape[0]
    return call(
        functools.partial(apply_kernel, nb2),
        "norm_apply",
        (1,),
        [
            (idx, None),
            (counts, pl.BlockSpec(memory_space=pltpu.SMEM)),
            (pre, whole(full, 2 * HD)),
            (cotangent, pl.BlockSpec((full, HD), lambda g, i: (i[0], 0))),
            (cot_sib, whole(full, HD)),
            (par, whole(8, HD)),
            (par_sib, whole(8, HD)),
            (stats, whole(2, 8, HD)),
        ],
        [
            (shape(2 * full, HD), pl.BlockSpec((full, HD), lambda g, i: (i[0], 0))),
            (shape(full, HD), whole(full, HD)),
            (shape(full, 2 * HD), whole(full, 2 * HD)),
            (shape(2, 8, HD), whole(2, 8, HD)),
        ],
        least=3 * 2**19,
        vmem=20,
        work=(1e6, 8e6),
    )


def back_kernel(
    pair, idx_ref, xo_ref, xs_ref, wh_ref, wl_ref, s_ref, tm_ref, d_ref, linv_ref, u_ref, wa_ref, wb_ref, *refs
):
    before_ref = refs[0] if pair == 1 else None
    vh_ref, vl_ref, ds_ref, dp, delta, tacc = refs[pair:]
    j = pl.program_id(0)
    rows = d_ref.shape[0]
    core = idx_ref[0]

    @pl.when(j == 0)
    def _():
        tacc[...] = jnp.zeros_like(tacc)
        for a, w_ref in enumerate((wa_ref, wb_ref)):
            at = slice(a * rows, (a + 1) * rows)
            linv = linv_ref[at, :]
            d = split2(d_ref[:, a * HD : (a + 1) * HD] * linv[:, 0:1])
            v = dot3(d, split2(rel_rows(w_ref, core)), NT)
            hi, lo = split2(v)
            vh_ref[at, :] = hi
            vl_ref[at, :] = lo
            delta[at, :] = jnp.sum(v * u_ref[at, :], axis=1, keepdims=True) * linv

    x = split2(jnp.concatenate([xo_ref[...], xs_ref[...]], axis=1))
    dp[...] = dot(cat3((vh_ref[...], vl_ref[...]), 1, False), cat3(x, 1, True), NT)
    width = dp.shape[1]
    at_j = pl.ds(pl.multiple_of(j * width, width), width)
    if before_ref is None:
        ds_ref[:, at_j] = jnp.zeros((8, width), F32)
    else:
        ds_ref[:, at_j] = before_ref[:, at_j]
    for a in range(2):
        m = 2 * pair + a
        s = s_ref[m : m + 1, :] * HALF_LN2
        total = None
        for r in range(0, rows, 32):
            at = slice(r, r + 32)
            ar = slice(a * rows + r, a * rows + r + 32)
            t = tm_ref[at, HEADS + m : HEADS + m + 1] * HALF_LN2
            slope = 0.6 + 0.4 * jnp.tanh(t + s)
            w = wh_ref[ar, :].astype(F32) + wl_ref[ar, :].astype(F32)
            dv = (w * slope) * (dp[ar, :] - delta[ar, 0:1])
            tacc[ar, :] += lane_groups(dv)
            total = dv if total is None else total + dv
        ds_ref[m : m + 1, at_j] = jnp.sum(total, axis=0, keepdims=True)

    @pl.when(j == pl.num_programs(0) - 1)
    def _():
        for a in range(2):
            m = HEADS + 2 * pair + a
            sums = jnp.sum(tacc[a * rows : (a + 1) * rows, :], axis=1, keepdims=True)
            turned = jnp.transpose(jnp.broadcast_to(sums, (rows, 128)))
            ds_ref[m : m + 1, 0:rows] = turned[0:1, :]


def back_block(blk, pair, idx, features, x_sib, fwd, d, weights, nb2, before=None, after=()):
    u, linv, tm, s, wh, wl = fwd
    hr, src = wh.shape
    kd = u.shape[1]
    two = hr // 2
    rows = two // 2
    cols = features.shape[1]
    tj = 2 * TJ
    nj = src // tj
    tile = pl.BlockSpec((two, tj), lambda j, i: (pair, j))
    return call(
        functools.partial(back_kernel, pair),
        "back_block",
        (nj,),
        [
            (idx, None),
            (features, pl.BlockSpec((tj, cols), lambda j, i: ((i[0] * nb2 + blk) * nj + j, 0))),
            (x_sib, pl.BlockSpec((tj, cols), lambda j, i: (blk * nj + j, 0))),
            (wh, tile),
            (wl, tile),
            (s, pl.BlockSpec((8, tj), lambda j, i: (0, j))),
            (tm, whole(rows, 128)),
            (d, pl.BlockSpec((rows, 2 * HD), lambda j, i: (blk, 0))),
            (linv, pl.BlockSpec((two, 128), lambda j, i: (pair, 0))),
            (u, pl.BlockSpec((two, kd), lambda j, i: (pair, 0))),
        ]
        + weight_specs(weights, 0, cols)
        + ([(before, whole(8, src))] if pair == 1 else []),
        [
            (shape(two, kd, dtype=BF16), whole(two, kd)),
            (shape(two, kd, dtype=BF16), whole(two, kd)),
            (shape(8, src), whole(8, src)),
        ],
        scratch=[pltpu.VMEM((two, tj), F32), pltpu.VMEM((two, 128), F32), pltpu.VMEM((two, 128), F32)],
        after=after,
        least=3 * 2**19,
        vmem=48,
        work=(6 * two * src * kd * 2, src * kd * 4 + two * src * 4),
    )


def weight_kernel(nb2, idx_ref, *refs):
    core = idx_ref[0]
    step = pl.program_id(0)
    ins, (send_ref, keep_ref) = refs[:-2], refs[-2:]
    gp, gs = None, None
    for b in range(nb2):
        u_ref, linv_ref, d_ref, xo_ref, xs_ref = ins[5 * b : 5 * b + 5]
        d = d_ref[...]
        dn = split2(d * linv_ref[:, 0:1])
        x = split2(jnp.concatenate([xo_ref[...], xs_ref[...]], axis=1))
        p = dot3(split2(u_ref[...]), dn, TN)
        s = dot3(x, split2(d), TN)
        gp = p if gp is None else gp + p
        gs = s if gs is None else gs + s
    cols = gp.shape[0] // 2

    def put(ref):
        for mat, g in enumerate((gp, gs)):
            ref[mat, core] = g[:cols]
            ref[mat, core ^ 1] = g[cols:]

    @pl.when(step == 0)
    def _():
        put(send_ref)

    @pl.when(step == 1)
    def _():
        put(keep_ref)


def weight_pair(pair, idx, features, x_sib, fwds, d, src, nb2, after=()):
    hr, kd = fwds[0][0].shape
    rows = hr // HEADS
    cols = features.shape[1]
    per = src // rows
    ins = [(idx, None)]
    head = lambda g: 2 * pair + 1 - g
    for b in range(nb2):
        ins += [
            (fwds[b][0], pl.BlockSpec((rows, kd), lambda g, i: (head(g), 0))),
            (fwds[b][1], pl.BlockSpec((rows, 128), lambda g, i: (head(g), 0))),
            (d, pl.BlockSpec((rows, HD), lambda g, i, b=b: (b, 1 - g))),
            (features, pl.BlockSpec((rows, cols), lambda g, i, b=b: ((i[0] * nb2 + b) * per, 0))),
            (x_sib, pl.BlockSpec((rows, cols), lambda g, i, b=b: (b * per, 0))),
        ]
    return call(
        functools.partial(weight_kernel, nb2),
        "weight_pair",
        (2,),
        ins,
        [(shape(2, 2, cols, HD), whole(2, 2, cols, HD))] * 2,
        after=after,
        least=3 * 2**19,
        vmem=16,
        work=(6 * nb2 * 4 * rows * kd * HD, nb2 * hr * kd * 2),
    )


def thin_kernel(first, idx_ref, xo_ref, xs_ref, da_ref, db_ref, *refs):
    o_ref, flip_ref = refs[-2:]
    core = idx_ref[0]
    cols = xo_ref.shape[1]

    @pl.when(pl.program_id(0) == 0)
    def _():
        o_ref[...] = jnp.zeros_like(o_ref) if first else refs[0][...]

    x = split2(jnp.concatenate([xo_ref[...], xs_ref[...]], axis=1))
    d = da_ref[...] + flip_rows(db_ref[...], 2)
    hi = d.astype(BF16).astype(F32)
    stack = jnp.concatenate([hi, d - hi], axis=0).astype(BF16)
    r1 = dot(stack, x[0], NN)
    r2 = dot(stack, x[1], NN)
    q = r1[:8] + (r1[8:] + r2[:8])
    o_ref[core] += q[:, :cols]
    o_ref[core ^ 1] += q[:, cols:]

    @pl.when(pl.program_id(0) == pl.num_programs(0) - 1)
    def _():
        for k in range(2):
            flip_ref[k] = flip_rows(o_ref[k], 1)


def thin_sums(blk, idx, features, x_sib, ds, ds_cross, nb2, before=None, after=()):
    src = ds.shape[1]
    cols = features.shape[1]
    tj = 2 * TJ
    nj = src // tj
    piece = pl.BlockSpec((8, tj), lambda j, i: (0, j))
    return call(
        functools.partial(thin_kernel, before is None),
        "thin_sums",
        (nj,),
        [
            (idx, None),
            (features, pl.BlockSpec((tj, cols), lambda j, i: ((i[0] * nb2 + blk) * nj + j, 0))),
            (x_sib, pl.BlockSpec((tj, cols), lambda j, i: (blk * nj + j, 0))),
            (ds, piece),
            (ds_cross, piece),
        ]
        + ([] if before is None else [(before, whole(2, 8, cols))]),
        [(shape(2, 8, cols), whole(2, 8, cols))] * 2,
        after=after,
        vmem=12,
        work=(2 * src * cols * 64, src * cols * 8),
    )


def feature_kernel(
    idx_ref, wh_ref, wl_ref, vh0_ref, vl0_ref, vh1_ref, vl1_ref, da_ref, db_ref, a_ref, d0_ref, d1_ref,
    s0_ref, s1_ref, s2_ref, s3_ref, *refs
):
    o_ref, mark_ref = refs[-2:]
    core = idx_ref[0]
    j = pl.program_id(0)
    mark_ref[...] = jnp.zeros_like(mark_ref)
    rows = d0_ref.shape[0]
    lhs = cat3((wh_ref[...], wl_ref[...]), 0, False)
    vh = jnp.concatenate([vh0_ref[...], vh1_ref[...]], axis=0)
    vl = jnp.concatenate([vl0_ref[...], vl1_ref[...]], axis=0)
    d = da_ref[...] + flip_rows(db_ref[...], 2)
    out = dot(lhs, cat3((vh, vl), 0, True), TN) + dot(thin_rows(d), thin_cols(a_ref[...]), TN)
    o_ref[...] = out

    @pl.when(j == 0)
    def _():
        skip = None
        for a, s_ref in enumerate((s0_ref, s1_ref, s2_ref, s3_ref)):
            d_ref = d0_ref if a < 2 else d1_ref
            part = split2(d_ref[:, (a % 2) * HD : (a % 2 + 1) * HD])
            new = dot3(part, split2(s_ref[0]), NT)
            skip = new if skip is None else skip + new
        o_ref[0:rows, :] += skip


def feature_block(blk, mine, idx, fwd, v0, v1, ds, ds_cross, a_half, d0, d1, weights, full, nb2, before=None, after=()):
    wh, wl = fwd[4], fwd[5]
    hr, src = wh.shape
    two, kd = v0[0].shape
    rows = two // 2
    half = kd // 2
    k = 0 if mine else 1
    nj = src // TJ
    tile = pl.BlockSpec((hr, TJ), lambda j, i: (0, j))
    vals = pl.BlockSpec((two, half), lambda j, i: (0, k))
    piece = pl.BlockSpec((8, TJ), lambda j, i: (0, j))
    dspec = pl.BlockSpec((rows, 2 * HD), lambda j, i: (blk, 0))
    ins = [
        (idx, None),
        (wh, tile),
        (wl, tile),
        (v0[0], vals),
        (v0[1], vals),
        (v1[0], vals),
        (v1[1], vals),
        (ds, piece),
        (ds_cross, piece),
        (a_half, pl.BlockSpec((8, half), lambda j, i: (0, k))),
        (d0, dspec),
        (d1, dspec),
    ] + [(p, pl.BlockSpec((1, half, HD), lambda j, i: (1, i[0] ^ k, 0))) for p in weights]
    aliases = {}
    if before is not None:
        aliases[len(ins)] = 0
        ins.append((before, HBM))
    out = (shape(src, half), pl.BlockSpec((TJ, half), lambda j, i: (j, 0)))
    if mine:
        out = (shape(*full), pl.BlockSpec((TJ, half), lambda j, i: ((i[0] * nb2 + blk) * nj + j, 0)))
    return call(
        feature_kernel,
        "feature_block",
        (nj,),
        ins,
        [out, (shape(8, 128), whole(8, 128))],
        after=after,
        work=(6 * two * src * kd, src * two * 8 + src * kd * 2),
        least=3 * 2**19,
        vmem=48,
        aliases=aliases,
    )


def place_kernel(nb2, idx_ref, *refs):
    for b in range(nb2):

        @pl.when(pl.program_id(0) == b)
        def _():
            refs[-1][...] = refs[b][...]


def place(idx, parts, before, nb2, after=()):
    src, half = parts[0].shape
    size = src // 2
    spec = lambda b: pl.BlockSpec((size, half), lambda g, j, i: (jnp.where(g == b, j, jnp.where(g < b, 0, 1)), 0))
    return call(
        functools.partial(place_kernel, nb2),
        "place",
        (nb2, 2),
        [(idx, None)] + [(v, spec(b)) for b, v in enumerate(parts)] + [(before, HBM)],
        [(shape(*before.shape), pl.BlockSpec((size, half), lambda g, j, i: ((i[2] * nb2 + g) * 2 + j, 0)))],
        after=after,
        work=(1e3, src * half * 8),
        least=3 * 2**19,
        vmem=16,
        aliases={1 + nb2: 0},
    )[0]


def split_kernel(at, idx_ref, keep_ref, recv_ref, send_ref, next_ref):
    size = next_ref.shape[1]
    mine = pl.ds(pl.multiple_of(idx_ref[at] * size, size), size)
    other = pl.ds(pl.multiple_of((1 - idx_ref[at]) * size, size), size)
    send_ref[...] = keep_ref[:, other, :] + recv_ref[:, other, :]
    next_ref[...] = keep_ref[:, mine, :] + recv_ref[:, mine, :]


def split_step(at, idx, keep, recv, after=()):
    n, rows, cols = keep.shape
    part = (n, rows // 2, cols)
    return call(
        functools.partial(split_kernel, at),
        "split_step",
        (1,),
        [(idx, None), (keep, whole(n, rows, cols)), (recv, whole(n, rows, cols))],
        [(shape(*part), whole(*part))] * 2,
        after=after,
        least=3 * 2**19,
        vmem=8,
        work=(1e3, keep.size * 8),
    )


def add_kernel(idx_ref, a_ref, b_ref, o_ref):
    o_ref[...] = a_ref[...] + b_ref[...]


def add_step(idx, a, b, after=()):
    return call(
        add_kernel,
        "add_step",
        (1,),
        [(idx, None), (a, whole(*a.shape)), (b, whole(*a.shape))],
        [(shape(*a.shape), whole(*a.shape))],
        after=after,
        least=3 * 2**19,
        vmem=8,
        work=(1e3, a.size * 8),
    )[0]


def join_kernel(at, idx_ref, mine_ref, recv_ref, o_ref):
    size = (mine_ref.shape[0] - EXTRA) // 2
    for mat in range(2):
        old = slice(mat * size, (mat + 1) * size)
        put = lambda up: pl.ds(pl.multiple_of(2 * mat * size + up * size, size), size)
        o_ref[put(idx_ref[at]), :] = mine_ref[old, :]
        o_ref[put(1 - idx_ref[at]), :] = recv_ref[old, :]
    o_ref[4 * size :, :] = mine_ref[2 * size :, :] + recv_ref[2 * size :, :]


def join_step(at, idx, mine, recv, after=()):
    rows, cols = mine.shape
    full = 2 * (rows - EXTRA) + EXTRA
    return call(
        functools.partial(join_kernel, at),
        "join_step",
        (1,),
        [(idx, None), (mine, whole(rows, cols)), (recv, whole(rows, cols))],
        [(shape(full, cols), whole(full, cols))],
        after=after,
        work=(1e3, mine.size * 16),
        least=3 * 2**19,
        vmem=12,
    )[0]


def end_kernel(idx_ref, keep_ref, recv_ref, o_ref):
    size = keep_ref.shape[1]
    for mat in range(2):
        o_ref[mat * size : (mat + 1) * size, :] = keep_ref[mat] + recv_ref[mat]
    o_ref[2 * size :, :] = jnp.zeros((EXTRA, o_ref.shape[1]), F32)


def end_step(idx, keep, recv, after=()):
    n, rows, cols = keep.shape
    full = n * rows + EXTRA
    return call(
        end_kernel,
        "end_step",
        (1,),
        [(idx, None), (keep, whole(n, rows, cols)), (recv, whole(n, rows, cols))],
        [(shape(full, cols), whole(full, cols))],
        after=after,
        work=(1e3, keep.size * 8),
        least=3 * 2**19,
        vmem=8,
    )[0]


def swap_kernel(idx_ref, keep_ref, recv_ref, q_ref, qr_ref, b_ref, br_ref, o_ref, extra_ref):
    size = keep_ref.shape[1]
    for mat in range(2):
        o_ref[mat * size : (mat + 1) * size, :] = keep_ref[mat] + recv_ref[mat]
    q = q_ref[...] + qr_ref[...]
    width = o_ref.shape[1]
    pick = lambda m: [q[k, n : n + 1, :] for k in range(2) for n in (m, HEADS + m)]
    zero = lambda n: [jnp.zeros((n, width), F32)]
    o_ref[2 * size :, :] = jnp.concatenate(pick(2) + zero(EXTRA - 4), axis=0)
    bias = b_ref[0, 2:3, :] + br_ref[1, 2:3, :]
    extra_ref[...] = jnp.concatenate(zero(4) + pick(0) + [bias] + zero(EXTRA - 9), axis=0)


def swap_step(idx, keep, recv, q, q_recv, sums, sums_recv, after=()):
    n, rows, cols = keep.shape
    full = n * rows + EXTRA
    arrays = [keep, recv, q, q_recv, sums, sums_recv]
    return call(
        swap_kernel,
        "swap_step",
        (1,),
        [(idx, None)] + [(v, whole(*v.shape)) for v in arrays],
        [(shape(full, cols), whole(full, cols)), (shape(EXTRA, cols), whole(EXTRA, cols))],
        after=after,
        work=(1e3, keep.size * 8),
        least=3 * 2**19,
        vmem=8,
    )


def enter_kernel(idx_ref, recv_ref, extra_ref, o_ref):
    rows = recv_ref.shape[0] - EXTRA
    o_ref[:rows, :] = recv_ref[:rows, :]
    o_ref[rows:, :] = recv_ref[rows:, :] + extra_ref[...]


def enter_step(idx, recv, extra, after=()):
    return call(
        enter_kernel,
        "enter_step",
        (1,),
        [(idx, None), (recv, whole(*recv.shape)), (extra, whole(*extra.shape))],
        [(shape(*recv.shape), whole(*recv.shape))],
        after=after,
        work=(1e3, recv.size * 8),
        least=3 * 2**19,
        vmem=8,
    )[0]


def last_kernel(idx_ref, own_ref, far_ref, att_ref, op_ref, os_ref):
    tall = own_ref.shape[0] - EXTRA
    size = tall // 2

    def put(g_ref, first):
        for k in range(2):
            at = slice(k * size // 2, (k + 1) * size // 2)
            q = far_ref[tall + first + 2 * k : tall + first + 2 * k + 2, :]
            q = jnp.concatenate([q, jnp.zeros((6, q.shape[1]), F32)], axis=0)
            op_ref[at, :] = g_ref[at, :] + dot(thin_rows(q), thin_cols(att_ref[...]), TN)
        os_ref[...] = g_ref[size:tall, :]

    @pl.when(pl.program_id(0) == 0)
    def _():
        put(own_ref, 4)

    @pl.when(pl.program_id(0) == 1)
    def _():
        put(far_ref, 0)


def last_step(idx, own, far, att, after=()):
    rows, width = own.shape
    size = (rows - EXTRA) // 2
    out = pl.BlockSpec((size, width), lambda g, i: (i[1] ^ g, 0))
    return call(
        last_kernel,
        "last_step",
        (2,),
        [(idx, None)] + [(v, whole(*v.shape)) for v in (own, far, att)],
        [(shape(2 * size, width), out)] * 2,
        after=after,
        work=(1e6, 4e6),
        least=3 * 2**19,
        vmem=16,
    )


def make_step(dp_size):
    bits = [1 << k for k in range(dp_size.bit_length() - 1)]

    def on_device(
        features, adjacency, seed_counts, w_proj, w_skip, attn_src, attn_dst, bias, gamma, beta, cotangent
    ):
        nb, rows, src = adjacency.shape
        cols = features.shape[1]
        nb2 = nb // 2
        h = lax.axis_index("head")
        dpi = lax.axis_index("dp")
        core, side = h & 1, h >> 1
        def to_core(v):
            return lax.ppermute(v, "head", [(i, i ^ 1) for i in range(HEADS)])

        def to_cross(v):
            return lax.ppermute(v, "head", [(i, i ^ 2) for i in range(HEADS)])

        def to_dp(v, bit):
            return lax.ppermute(v, "dp", [(i, i ^ bit) for i in range(dp_size)])

        def half(v, which):
            size = v.shape[0] // 2
            return lax.dynamic_slice_in_dim(v, which * size, size, 0)

        ups = [(dpi >> k) & 1 for k in range(len(bits))]
        idx = jnp.stack([core, side, 1 - core, 1 - side] + ups).astype(jnp.int32)

        with jax.named_scope("fold_attention"):
            folded = jnp.stack(
                [jnp.sum(w_proj * attn_src, axis=1), jnp.sum(w_proj * attn_dst, axis=1)]
            )
            near_folded = to_core(folded)
            folded = jnp.stack([folded, near_folded])
            a_all = jnp.concatenate([folded, to_cross(folded)])
            a_all = a_all.transpose(1, 0, 2).reshape(2 * HEADS, -1)
            a_own = lax.dynamic_slice_in_dim(a_all, h * cols, cols, 1) * LOG2E

        with jax.named_scope("share_inputs"):
            par = jnp.pad(jnp.stack([bias, gamma, beta]), ((0, 5), (0, 0)))
            par_sib = to_core(par)
            x_send, cot_send = pack(idx, 2, [features, cotangent], after=[near_folded], steps=4)
            x_sib, cot_sib = to_core(x_send), to_core(cot_send)

        with jax.named_scope("scores"):
            s_send, s_keep = scores(idx, features, a_own, after=[x_send])
            s_mine = add_step(idx, s_keep, to_core(s_send))
            s_cross = to_cross(s_mine)

        with jax.named_scope("share_weights"):
            halves = pack(idx, 3, [w_proj, w_skip], after=[s_cross], stacked=True)
            w_far = to_cross(halves)
            w_own = pack(idx, 1, [w_proj, w_skip], after=[halves], stacked=True)
            own_weights = [w_own, to_core(w_own)]

        with jax.named_scope("forward"):
            fwds, parts, recvs = [], [], []
            for b in range(nb2):
                fwds.append(
                    forward_block(
                        b, idx, features, x_sib, adjacency, s_mine, s_cross, nb2,
                        after=parts[-1:] + [par_sib, cot_sib, own_weights[1], halves],
                    )
                )
                if b == 0:
                    w_far = relay(idx, w_far, after=[fwds[0][1]])
                    far_weights = [w_far, to_core(w_far)]
                parts.append(
                    pre_block(
                        b, 1, idx, *fwds[b][:2], features, x_sib, far_weights, src, nb2,
                        after=recvs[-1:],
                    )
                )
                recvs.append(to_cross(parts[-1]))
            owns = [
                pre_block(b, 0, idx, *fwds[b][:2], features, x_sib, own_weights, src, nb2, after=parts[-1:])
                for b in range(nb2)
            ]

        with jax.named_scope("norm"):
            pre, stats, flipped = norm_sums(
                idx, seed_counts, cotangent, cot_sib, par, par_sib, owns, recvs, nb2
            )
            stats = stats + to_core(flipped)
            for bit in bits:
                stats = stats + to_dp(stats, bit)
            act, act_send, d_own, small = norm_apply(
                idx, seed_counts, pre, cotangent, cot_sib, par, par_sib, stats, nb2
            )
            act_recv = to_core(act_send)
            activations = lax.dynamic_update_slice_in_dim(
                act, act_recv, (1 - core) * nb2 * rows, 0
            )
            d_far = to_cross(d_own)

        token = [d_own]

        def note(out):
            token[:] = [out]
            return out

        flat = lambda v: v.reshape(2, 2 * cols, HD)
        backs, fars, ds_cross, theirs = [], [], [], []
        state = {}

        def scatter(send, keep, recv):
            for k, bit in enumerate(bits):
                send, keep = split_step(4 + k, idx, keep, recv, after=token)
                note(keep)
                recv = to_dp(send, bit)
                yield
            return keep, recv

        def gather(rows):
            for k, bit in reversed(list(enumerate(bits))):
                recv = to_dp(rows, bit)
                yield
                rows = note(join_step(4 + k, idx, rows, recv, after=token))
            return rows

        def own_chain(send, keep):
            keep, recv = yield from scatter(send, flat(keep), flat(to_core(send)))
            rows = note(end_step(idx, keep, recv, after=token))
            state["own"] = yield from gather(rows)

        def far_chain(send, keep):
            keep, recv = yield from scatter(send, flat(keep), flat(to_core(send)))
            while "flip" not in state:
                yield
            message, extra = swap_step(
                idx, keep, recv, state["q"], state["q_recv"], small, state["sums_recv"], after=token
            )
            note(extra)
            recv = to_cross(message)
            yield
            rows = note(enter_step(idx, recv, extra, after=token))
            state["far"] = yield from gather(rows)

        def advance(*chains):
            for c in chains:
                next(c, None)

        def back_far(b):
            fars.append(
                back_block(
                    b, 1, idx, features, x_sib, fwds[b], d_far, far_weights, nb2,
                    before=backs[b][2], after=token,
                )
            )
            note(fars[-1][2])
            ds_cross.append(to_cross(fars[-1][2]))

        def thin(b):
            state["q"], state["q_flip"] = thin_sums(
                b, idx, features, x_sib, fars[b][2], ds_cross[b], nb2, before=state.get("q"),
                after=token,
            )
            note(state["q"])

        half_cols = lambda i: lax.dynamic_slice_in_dim(a_all, i * cols, cols, 1)
        a_half = jnp.concatenate([half_cols(h), half_cols(h ^ 1)], axis=1)

        def features_of(b, mine):
            out, mark = feature_block(
                b, mine, idx, fwds[b], backs[b][:2], fars[b][:2], fars[b][2], ds_cross[b],
                a_half, d_own, d_far, own_weights + far_weights, features.shape, nb2,
                before=state.get("gf") if mine else None, after=token,
            )
            note(mark)
            if mine:
                state["gf"] = out
            else:
                theirs.append(to_core(out))

        with jax.named_scope("backward"):
            state["sums_recv"] = to_core(small)
            send, keep = weight_pair(
                0, idx, features, x_sib, fwds, d_own, src, nb2, after=token + [state["sums_recv"], act_recv]
            )
            note(keep)
            own = own_chain(send, keep)
            for b in range(nb2):
                backs.append(
                    back_block(
                        b, 0, idx, features, x_sib, fwds[b], d_own, own_weights, nb2, after=token
                    )
                )
                note(backs[-1][2])
                advance(own)
            send, keep = weight_pair(1, idx, features, x_sib, fwds, d_far, src, nb2, after=token)
            note(keep)
            far = far_chain(send, keep)
            advance(far)
            for b in range(nb2):
                back_far(b)
                advance(far, own)
            for b in range(nb2):
                thin(b)
            state["q_recv"] = to_core(state["q_flip"])
            state["flip"] = True
            advance(own, far)
            for b in range(nb2):
                for mine in (False, True):
                    features_of(b, mine)
                    if (b, mine) != (nb2 - 1, True):
                        advance(far, own)
            grad_features = note(place(idx, theirs, state["gf"], nb2, after=token))
            for c in (own, far):
                for _ in c:
                    pass

        with jax.named_scope("last"):
            att = jnp.pad(jnp.stack([attn_src, attn_dst]), ((0, 6), (0, 0)))
            grad_proj, grad_skip = last_step(idx, state["own"], state["far"], att)
            extra = state["far"][-EXTRA:]
            q_far, q_own = extra[0:4].reshape(2, 2, cols), extra[4:8].reshape(2, 2, cols)
            near = jnp.where(side == 0, q_own, q_far)
            away = jnp.where(side == 0, q_far, q_own)
            thin_all = jnp.concatenate([near, away]).transpose(1, 0, 2).reshape(2, -1)
            grad_att = jnp.dot(thin_all, w_proj, precision=lax.Precision.HIGHEST)

        return (
            activations,
            grad_features,
            grad_proj,
            grad_skip,
            grad_att[0],
            grad_att[1],
            extra[8],
            small[0, 0],
            small[0, 1],
        )

    return on_device


def solution(mesh):
    return jax.shard_map(
        make_step(mesh.shape["dp"]),
        mesh=mesh,
        in_specs=(
            P("dp", "head"),
            P("dp", None, None),
            P("dp"),
            P(None, "head"),
            P(None, "head"),
            P("head"),
            P("head"),
            P("head"),
            P("head"),
            P("head"),
            P("dp", "head"),
        ),
        out_specs=(
            P("dp", "head"),
            P("dp", "head"),
            P(None, "head"),
            P(None, "head"),
            P("head"),
            P("head"),
            P("head"),
            P("head"),
            P("head"),
        ),
        check_vma=False,
    )
```

```python
import functools

import jax
import jax.numpy as jnp
from jax import lax
from jax.experimental import pallas as pl
from jax.experimental.pallas import tpu as pltpu
from jax.sharding import PartitionSpec as P

HD = 256
HEADS = 4
TJ = 512
PARTS = 2
EXTRA = 16
eps = 1e-05
LOG2E = 1.4426950408889634
HALF_LN2 = 0.34657359027997264
F32 = jnp.float32
BF16 = jnp.bfloat16
NN = ((1,), (0,))
NT = ((1,), (1,))
TN = ((0,), (0,))
LOW = -3e38
HBM = pl.BlockSpec(memory_space=pltpu.HBM)
ANY = pl.BlockSpec(memory_space=pl.ANY)
NEAR = pl.BlockSpec(memory_space=pltpu.VMEM)


def dot(a, b, form):
    return lax.dot_general(a, b, (form, ((), ())), preferred_element_type=F32)


def split2(x):
    hi = x.astype(BF16)
    return hi, (x - hi.astype(F32)).astype(BF16)


def dot3(a, b, form):
    return dot(a[0], b[0], form) + (dot(a[0], b[1], form) + dot(a[1], b[0], form))


def cat3(a, axis, mixed):
    hi, lo = a
    return jnp.concatenate([hi, lo, hi] if mixed else [hi, hi, lo], axis=axis)


def thin_rows(d):
    hi = d.astype(BF16).astype(F32)
    return jnp.concatenate([hi, hi, d - hi, jnp.zeros_like(d)], axis=0).astype(BF16)


def thin_cols(a):
    hi = a.astype(BF16).astype(F32)
    return jnp.concatenate([hi, a - hi, hi, jnp.zeros_like(a)], axis=0).astype(BF16)


def lane_groups(v):
    out = v[:, :128]
    for k in range(128, v.shape[1], 128):
        out = out + v[:, k : k + 128]
    return out


def leaky2(u):
    soft = jnp.log2(1.0 + jnp.exp2(jnp.minimum(u, 126.0)))
    return jnp.maximum(u, 0.2 * u + 0.8 * soft)


def elu(v):
    return jnp.where(v > 0, v, jnp.exp(jnp.minimum(v, 0.0)) - 1.0)


def flip_rows(v, bit):
    return jnp.concatenate([v[m ^ bit : (m ^ bit) + 1] for m in range(8)], axis=0)


def large(v, least):
    return v.size * v.dtype.itemsize >= least


def held(v, spec, least):
    if spec is NEAR:
        return pltpu.with_memory_space_constraint(v, pltpu.VMEM)
    if spec is ANY:
        return v
    return pltpu.with_memory_space_constraint(v, pltpu.HBM) if large(v, least) else v


def result(v, spec, least):
    if spec is NEAR:
        return pltpu.VMEM(v.shape, v.dtype)
    return pltpu.HBM(v.shape, v.dtype) if large(v, least) else v


def call(kernel, name, grid, ins, outs, scratch=(), after=(), work=(1e6, 1e6), vmem=8, aliases=None, least=3 * 2**19):
    n_in = len(ins)
    n_after = len(after)
    ins = [ins[0]] + [(held(v, spec, least), spec) for v, spec in ins[1:]]

    def body(*refs):
        kernel(*refs[:n_in], *refs[n_in + n_after :])

    return pl.pallas_call(
        body,
        grid_spec=pltpu.PrefetchScalarGridSpec(
            num_scalar_prefetch=1,
            grid=grid,
            in_specs=[s for _, s in ins[1:]] + [ANY] * n_after,
            out_specs=[s for _, s in outs],
            scratch_shapes=list(scratch),
        ),
        out_shape=[result(v, spec, least) for v, spec in outs],
        compiler_params=pltpu.CompilerParams(
            dimension_semantics=("arbitrary",) * len(grid), vmem_limit_bytes=vmem * 2**20
        ),
        cost_estimate=pl.CostEstimate(
            flops=int(work[0]), bytes_accessed=int(work[1]), transcendentals=0
        ),
        input_output_aliases=aliases or {},
        name=name,
    )(*[v for v, _ in ins], *after)


def shape(*dims, dtype=F32):
    return jax.ShapeDtypeStruct(dims, dtype)


def whole(*dims):
    return pl.BlockSpec(dims, lambda *_: (0,) * len(dims))


def pack_kernel(idx_ref, a_ref, b_ref, c_ref, w_ref, o_ref, mark_ref):
    mark_ref[...] = jnp.zeros_like(mark_ref)
    w_ref[0] = a_ref[...]
    w_ref[1] = b_ref[...]
    o_ref[...] = c_ref[...]


def pack(idx, w_proj, w_skip, cotangent, after=()):
    rows, cols = w_proj.shape
    half = rows // 2
    mine = cotangent.shape[0] // 2
    weight = pl.BlockSpec((half, cols), lambda g, i: (i[3], 0))
    return call(
        pack_kernel,
        "pack",
        (1,),
        [
            (idx, None),
            (w_proj, weight),
            (w_skip, weight),
            (cotangent, pl.BlockSpec((mine, cols), lambda g, i: (i[2], 0))),
        ],
        [
            (shape(2, half, cols), whole(2, half, cols)),
            (shape(mine, cols), whole(mine, cols)),
            (shape(8, 128), whole(8, 128)),
        ],
        after=after,
        work=(1e3, 1e6),
        least=2**18,
        vmem=12,
    )


def relay(idx, v, after=()):
    return call(
        lambda *_: None,
        "relay",
        (1,),
        [(idx, None), (v, HBM)],
        [(shape(*v.shape), HBM)],
        after=after,
        work=(1e3, 1e3),
        least=2**18,
        aliases={1: 0},
    )[0]


def score_kernel(idx_ref, x_ref, a_ref, send_ref, keep_ref, copy_ref):
    x = x_ref[...]
    x1 = x.astype(BF16)
    rest = x - x1.astype(F32)
    x2 = rest.astype(BF16)
    x3 = (rest - x2.astype(F32)).astype(BF16)
    a = a_ref[...]
    a1 = a.astype(BF16).astype(F32)
    a2 = (a - a1).astype(BF16).astype(F32)
    a3 = (a - a1) - a2
    stack = jnp.concatenate([a1, a2, a3, jnp.zeros_like(a)], axis=0).astype(BF16)
    r1 = dot(stack, x1, NT)
    r2 = dot(stack[:16], x2, NT)
    r3 = dot(stack[:16], x3, NT)
    s = r1[:8] + (r1[8:16] + r2[:8]) + (r1[16:24] + r2[8:16] + r3[:8])

    @pl.when(pl.program_id(0) == 0)
    def _():
        send_ref[...] = flip_rows(s, 1)
        copy_ref[...] = x

    @pl.when(pl.program_id(0) == 1)
    def _():
        keep_ref[...] = s


def scores(idx, features, a_own, after=()):
    rows, cols = features.shape
    tile = 2048
    n = rows // 2 // tile
    return call(
        score_kernel,
        "scores",
        (2, n),
        [
            (idx, None),
            (features, pl.BlockSpec((tile, cols), lambda g, i, s: ((s[0] ^ 1 ^ g) * n + i, 0))),
            (a_own, whole(8, cols)),
        ],
        [
            (shape(8, rows // 2), pl.BlockSpec((8, tile), lambda g, i, s: (0, i * (1 - g) + (n - 1) * g))),
            (shape(8, rows // 2), pl.BlockSpec((8, tile), lambda g, i, s: (0, i * g))),
            (
                shape(rows // 2, cols),
                pl.BlockSpec((tile, cols), lambda g, i, s: (i * (1 - g) + (n - 1) * g, 0)),
            ),
        ],
        after=after,
        vmem=24,
        work=(2 * rows * cols * 24, rows * cols * 4),
    )


def forward_kernel(pair, idx_ref, adj_ref, sa_ref, sb_ref, xa_ref, xb_ref, *refs):
    first = pair == 1
    u_ref, linv_ref, tm_ref, s_ref, wh_ref, wl_ref = refs[:6]
    xh_ref, xl_ref = refs[6:8] if first else (xa_ref, xb_ref)
    rows, src = adj_ref.shape[1], adj_ref.shape[2]
    b = pl.program_id(0)
    nb2 = pl.num_programs(0)
    block = pl.ds(pl.multiple_of(b * src, src), src)

    def loads(blk):
        xbuf, sems = refs[8:]
        to = lax.rem(blk, 2)
        at = pl.ds(pl.multiple_of(blk * src, src), src)
        own = pl.ds(pl.multiple_of((idx_ref[0] * nb2 + blk) * src, src), src)
        return (
            pltpu.make_async_copy(xa_ref.at[own, :], xbuf.at[to, 0], sems.at[to, 0]),
            pltpu.make_async_copy(xb_ref.at[at, :], xbuf.at[to, 1], sems.at[to, 1]),
        )

    if first:

        @pl.when(b == 0)
        def _():
            for copy in loads(b):
                copy.start()

    s_all = sa_ref[:, block] + flip_rows(sb_ref[:, block], 2)
    s_ref[:, block] = s_all
    tm_ref[b, :, 0:8] = jnp.transpose(s_all[:, :rows])
    part = lambda m, k, n: s_ref[m : m + 1, pl.ds(pl.multiple_of(b * src + k, 128), n)]
    heads = (2 * pair, 2 * pair + 1)
    step = 64

    @pl.loop(0, rows, step=step)
    def _(r):
        best = [jnp.full((step, 128), LOW, F32) for _ in heads]
        for k in range(0, src, 128):
            linked = adj_ref[0, pl.ds(r, step), k : k + 128] > 0
            for n, m in enumerate(heads):
                best[n] = jnp.maximum(best[n], jnp.where(linked, part(m, k, 128), LOW))
        for n, m in enumerate(heads):
            t = tm_ref[b, pl.ds(r, step), HEADS + m : HEADS + m + 1]
            top = leaky2(t + jnp.max(best[n], axis=1, keepdims=True))
            tm_ref[b, pl.ds(r, step), m : m + 1] = top

    for n in range(3):
        if n < 2:
            m = heads[n]
            for r in range(0, rows, 32):
                at = slice(r, r + 32)
                to = slice(n * rows + r, n * rows + r + 32)
                t = tm_ref[b, at, HEADS + m : HEADS + m + 1]
                top = tm_ref[b, at, m : m + 1]
                acc = None
                for k in range(0, src, 512):
                    ks = slice(k, k + 512)
                    q = leaky2(t + part(m, k, 512))
                    w = jnp.where(adj_ref[0, at, ks] > 0, jnp.exp2(q - top), 0.0)
                    hi, lo = split2(w)
                    wh_ref[b, to, ks] = hi
                    wl_ref[b, to, ks] = lo
                    acc = lane_groups(w) if acc is None else acc + lane_groups(w)
                linv = 1.0 / jnp.sum(acc, axis=1, keepdims=True)
                linv_ref[b, to, :] = jnp.broadcast_to(linv, (32, 128))
        if n == 0 and first:
            cols = xa_ref.shape[1]
            xbuf = refs[8]
            slot = lax.rem(b, 2)
            for copy in loads(b):
                copy.wait()

            @pl.when(b + 1 < nb2)
            def _():
                for copy in loads(b + 1):
                    copy.start()

            @pl.loop(0, src, step=256)
            def _(r):
                at = pl.ds(pl.multiple_of(b * src + r, 256), 256)
                for k in range(2):
                    hi, lo = split2(xbuf[slot, k, pl.ds(r, 256), :])
                    xh_ref[at, k * cols : (k + 1) * cols] = hi
                    xl_ref[at, k * cols : (k + 1) * cols] = lo

        if n > 0:
            at = slice((n - 1) * rows, n * rows)
            lhs = cat3((wh_ref[b, at, :], wl_ref[b, at, :]), 1, False)
            rhs = cat3((xh_ref[block, :], xl_ref[block, :]), 0, True)
            u_ref[b, at, :] = dot(lhs, rhs, NN)


def forward_pair(pair, idx, xa, xb, adjacency, s_mine, s_cross, nb2, after=()):
    rows, src = adjacency.shape[1:]
    first = pair == 1
    cols = xa.shape[1]
    kd = 2 * cols if first else cols
    two = 2 * rows
    outs = [
        shape(nb2, two, kd),
        shape(nb2, two, 128),
        shape(nb2, rows, 128),
        shape(8, nb2 * src),
        shape(nb2, two, src, dtype=BF16),
        shape(nb2, two, src, dtype=BF16),
    ]
    if first:
        outs += [shape(nb2 * src, kd, dtype=BF16)] * 2
    return call(
        functools.partial(forward_kernel, pair),
        "forward_pair",
        (nb2,),
        [
            (idx, None),
            (adjacency, pl.BlockSpec((1, rows, src), lambda b, i: (i[0] * nb2 + b, 0, 0))),
            (s_mine, NEAR),
            (s_cross, NEAR),
            (xa, HBM if first else NEAR),
            (xb, ANY if first else NEAR),
        ],
        [(v, NEAR) for v in outs],
        scratch=[pltpu.VMEM((2, 2, src, cols), F32), pltpu.SemaphoreType.DMA((2, 2))] if first else [],
        after=after,
        work=(1e12 if first else 5e8, 1e5),
        vmem=22 if first else 16,
    )


def rel_rows(piece, mat, idx_ref):
    core, side = idx_ref[0], idx_ref[1]
    if len(piece) == 2:
        ref = piece[mat]
        cols = ref.shape[0] // 4
        first = side * 2 * cols
    else:
        ref = piece[0].at[mat]
        cols = ref.shape[0] // 2
        first = 0
    at = lambda k: pl.ds(pl.multiple_of(first + k * cols, cols), cols)
    return jnp.concatenate([ref[at(core), :], ref[at(core ^ 1), :]], axis=0)


def flat_weights(pieces):
    return [(v, NEAR) for p in pieces for v in p]


def take_weights(pieces, refs):
    out = []
    for p in pieces:
        out.append(refs[: len(p)])
        refs = refs[len(p) :]
    return out, refs


def pre_kernel(form, src, idx_ref, u_ref, linv_ref, xh_ref, xl_ref, *refs):
    weights, (o_ref,) = take_weights(form, refs)
    nb2, two = u_ref.shape[:2]
    rows = two // 2
    stack = lambda parts: jnp.concatenate(list(parts), axis=0)
    tops = [slice(b * src, b * src + rows) for b in range(nb2)]
    x = (stack(xh_ref[t, :] for t in tops), stack(xl_ref[t, :] for t in tops))
    for a, piece in enumerate(weights):
        at = slice(a * rows, (a + 1) * rows)
        mixed = split2(stack(u_ref[b, at, :] * linv_ref[b, at, 0:1] for b in range(nb2)))
        lhs = jnp.concatenate([cat3(mixed, 1, False), cat3(x, 1, False)], axis=1)
        proj, skip = split2(rel_rows(piece, 0, idx_ref)), split2(rel_rows(piece, 1, idx_ref))
        rhs = jnp.concatenate([cat3(proj, 0, True), cat3(skip, 0, True)], axis=0)
        o_ref[:, a * HD : (a + 1) * HD] = dot(lhs, rhs, NN)


def pre_pair(idx, u, linv, x_split, weights, src, spec, after=()):
    nb2, two, kd = u.shape
    rows = two // 2
    return call(
        functools.partial(pre_kernel, weights, src),
        "pre_pair",
        (1,),
        [(idx, None), (u, NEAR), (linv, NEAR), (x_split[0], NEAR), (x_split[1], NEAR)] + flat_weights(weights),
        [(shape(nb2 * rows, 2 * HD), spec)],
        after=after,
        work=(5e8, 1e5),
        vmem=16,
    )[0]


def live_rows(idx_ref, counts_ref, nb2, rows):
    parts = []
    for b in range(nb2):
        row = lax.broadcasted_iota(jnp.int32, (rows, 1), 0)
        parts.append((row < counts_ref[idx_ref[0] * nb2 + b]).astype(F32))
    return jnp.concatenate(parts, axis=0)


def stats_kernel(nb2, idx_ref, counts_ref, ca_ref, cb_ref, pa_ref, pb_ref, part_ref, recv_ref, pre_ref, st_ref, flip_ref):
    rows = part_ref.shape[0] // nb2
    total = lambda v: jnp.sum(v, axis=0, keepdims=True)
    live = live_rows(idx_ref, counts_ref, nb2, rows)
    for a, (c_ref, p_ref) in enumerate(((ca_ref, pa_ref), (cb_ref, pb_ref))):
        cols = slice(a * HD, (a + 1) * HD)
        bias = p_ref[0:1, :]
        pre = part_ref[:, cols] + recv_ref[:, cols] + bias
        pre_ref[:, cols] = pre
        act = (elu(pre) - elu(bias)) * live
        g = c_ref[...] * live
        rows8 = [total(act), total(act * act), total(g), total(g * act)]
        rows8.append(jnp.broadcast_to(total(live), (1, HD)))
        rows8.append(jnp.zeros((3, HD), F32))
        stats = jnp.concatenate(rows8, axis=0)
        st_ref[a] = stats
        flip_ref[1 - a] = stats


def norm_sums(idx, counts, cotangent, cot_sib, par, par_sib, part, recv, nb2):
    full = part.shape[0]
    return call(
        functools.partial(stats_kernel, nb2),
        "norm_sums",
        (1,),
        [
            (idx, None),
            (counts, pl.BlockSpec(memory_space=pltpu.SMEM)),
            (cotangent, pl.BlockSpec((full, HD), lambda g, i: (i[0], 0))),
            (cot_sib, whole(full, HD)),
            (par, whole(8, HD)),
            (par_sib, whole(8, HD)),
            (part, NEAR),
            (recv, whole(full, 2 * HD)),
        ],
        [
            (shape(full, 2 * HD), NEAR),
            (shape(2, 8, HD), whole(2, 8, HD)),
            (shape(2, 8, HD), whole(2, 8, HD)),
        ],
        work=(5e8, 1e5),
        least=3 * 2**19,
        vmem=14,
    )


def apply_kernel(
    nb2, idx_ref, counts_ref, pre_ref, ca_ref, cb_ref, pa_ref, pb_ref, st_ref, act_ref, send_ref, d_ref, o_ref
):
    rows = pre_ref.shape[0] // nb2
    live = live_rows(idx_ref, counts_ref, nb2, rows)
    for a, (c_ref, p_ref, out_ref) in enumerate(
        ((ca_ref, pa_ref, act_ref), (cb_ref, pb_ref, send_ref))
    ):
        cols = slice(a * HD, (a + 1) * HD)
        bias, gamma, beta = p_ref[0:1, :], p_ref[1:2, :], p_ref[2:3, :]
        count = st_ref[a, 4:5, :]
        mean = st_ref[a, 0:1, :] / count
        inv = lax.rsqrt(st_ref[a, 1:2, :] / count - mean * mean + eps)
        grad_beta = st_ref[a, 2:3, :]
        grad_gamma = inv * (st_ref[a, 3:4, :] - mean * grad_beta)
        pre = pre_ref[:, cols]
        nrm = (elu(pre) - elu(bias) - mean) * inv
        out_ref[...] = live * (gamma * nrm + beta)
        g = c_ref[...] * live
        d = live * (gamma * inv) * (g - grad_beta / count - nrm * (grad_gamma / count))
        d = d * jnp.exp(jnp.minimum(pre, 0.0))
        d_ref[:, cols] = d
        o_ref[a, 0:1, :] = grad_gamma
        o_ref[a, 1:2, :] = grad_beta
        o_ref[a, 2:3, :] = jnp.sum(d, axis=0, keepdims=True)
        o_ref[a, 3:8, :] = jnp.zeros((5, HD), F32)


def norm_apply(idx, counts, pre, cotangent, cot_sib, par, par_sib, stats, nb2):
    full = pre.shape[0]
    return call(
        functools.partial(apply_kernel, nb2),
        "norm_apply",
        (1,),
        [
            (idx, None),
            (counts, pl.BlockSpec(memory_space=pltpu.SMEM)),
            (pre, NEAR),
            (cotangent, pl.BlockSpec((full, HD), lambda g, i: (i[0], 0))),
            (cot_sib, whole(full, HD)),
            (par, whole(8, HD)),
            (par_sib, whole(8, HD)),
            (stats, whole(2, 8, HD)),
        ],
        [
            (shape(2 * full, HD), pl.BlockSpec((full, HD), lambda g, i: (i[0], 0))),
            (shape(full, HD), whole(full, HD)),
            (shape(full, 2 * HD), NEAR),
            (shape(2, 8, HD), whole(2, 8, HD)),
        ],
        least=3 * 2**19,
        vmem=14,
        work=(5e8, 1e5),
    )


def back_kernel(
    blk, pair, form, prior, idx_ref, xh_ref, xl_ref, wh_ref, wl_ref, s_ref, tm_ref, d_ref, linv_ref, u_ref, *refs
):
    weights, refs = take_weights(form, refs)
    before, refs = refs[:pair], refs[pair:]
    earlier, refs = refs[:prior], refs[prior:]
    vh_ref, vl_ref, ds_ref, dp, delta, tacc = refs
    rows = tm_ref.shape[1]
    src = wh_ref.shape[2]
    base = 8 * prior
    for n, v in enumerate(earlier):
        ds_ref[8 * n : 8 * n + 8, :] = v[...]
    ds_ref[base : base + 8, :] = before[0][...] if pair == 1 else jnp.zeros((8, src), F32)
    tacc[...] = jnp.zeros_like(tacc)
    for a, piece in enumerate(weights):
        at = slice(a * rows, (a + 1) * rows)
        linv = linv_ref[blk, at, :]
        d = split2(d_ref[blk * rows : (blk + 1) * rows, a * HD : (a + 1) * HD] * linv[:, 0:1])
        v = dot(cat3(d, 1, False), cat3(split2(rel_rows(piece, 0, idx_ref)), 1, True), NT)
        hi, lo = split2(v)
        vh_ref[at, :] = hi
        vl_ref[at, :] = lo
        delta[at, :] = jnp.sum(v * u_ref[blk, at, :], axis=1, keepdims=True) * linv
    width = dp.shape[1]
    for j in range(src // width):
        js = slice(j * width, (j + 1) * width)
        xs = slice(blk * src + j * width, blk * src + (j + 1) * width)
        x = (xh_ref[xs, :], xl_ref[xs, :])
        dp[...] = dot(cat3((vh_ref[...], vl_ref[...]), 1, False), cat3(x, 1, True), NT)
        for a in range(2):
            m = 2 * pair + a
            s = s_ref[m : m + 1, xs] * HALF_LN2
            total = None
            for r in range(0, rows, 32):
                at = slice(r, r + 32)
                ar = slice(a * rows + r, a * rows + r + 32)
                t = tm_ref[blk, at, HEADS + m : HEADS + m + 1] * HALF_LN2
                slope = 0.6 + 0.4 * jnp.tanh(t + s)
                w = wh_ref[blk, ar, js].astype(F32) + wl_ref[blk, ar, js].astype(F32)
                dv = (w * slope) * (dp[ar, :] - delta[ar, 0:1])
                tacc[ar, :] += lane_groups(dv)
                total = dv if total is None else total + dv
            ds_ref[base + m : base + m + 1, js] = jnp.sum(total, axis=0, keepdims=True)
    for a in range(2):
        m = HEADS + 2 * pair + a
        sums = jnp.sum(tacc[a * rows : (a + 1) * rows, :], axis=1, keepdims=True)
        turned = jnp.transpose(jnp.broadcast_to(sums, (rows, 128)))
        ds_ref[base + m : base + m + 1, 0:rows] = turned[0:1, :]


def back_block(blk, pair, idx, x_split, fwd, d, weights, before=(), earlier=(), after=()):
    u, linv, tm, s, wh, wl = fwd
    two, src = wh.shape[1:]
    kd = u.shape[2]
    tj = 2 * TJ
    arrays = [*x_split, wh, wl, s, tm, d, linv, u]
    rest = [*before, *earlier]
    spec = NEAR if pair == 0 or not earlier else whole(8 * len(earlier) + 8, src)
    return call(
        functools.partial(back_kernel, blk, pair, weights, len(earlier)),
        "back_block",
        (1,),
        [(idx, None)] + [(v, NEAR) for v in arrays] + flat_weights(weights) + [(v, NEAR) for v in rest],
        [
            (shape(two, kd, dtype=BF16), NEAR),
            (shape(two, kd, dtype=BF16), NEAR),
            (shape(8 * len(earlier) + 8, src), spec),
        ],
        scratch=[pltpu.VMEM((two, tj), F32), pltpu.VMEM((two, 128), F32), pltpu.VMEM((two, 128), F32)],
        after=after,
        work=(5e8, 1e5),
        vmem=16,
    )


def weight_kernel(src, idx_ref, u_ref, linv_ref, d_ref, xh_ref, xl_ref, send_ref, keep_ref):
    core = idx_ref[0]
    nb2, two = u_ref.shape[:2]
    rows = two // 2
    stack = lambda parts: jnp.concatenate(list(parts), axis=0)
    tops = [slice(b * src, b * src + rows) for b in range(nb2)]
    x = cat3((stack(xh_ref[t, :] for t in tops), stack(xl_ref[t, :] for t in tops)), 0, False)
    for a, ref in ((1, send_ref), (0, keep_ref)):
        at = slice(a * rows, (a + 1) * rows)
        d = d_ref[:, a * HD : (a + 1) * HD]
        u = split2(stack(u_ref[b, at, :] for b in range(nb2)))
        dn = split2(d * stack(linv_ref[b, at, 0:1] for b in range(nb2)))
        gp = dot(cat3(u, 0, False), cat3(dn, 0, True), TN)
        gs = dot(x, cat3(split2(d), 0, True), TN)
        cols = gp.shape[0] // 2
        for mat, g in enumerate((gp, gs)):
            ref[mat, core] = g[:cols]
            ref[mat, core ^ 1] = g[cols:]


def weight_pair(idx, x_split, fwd, d, src, after=()):
    u, linv = fwd[:2]
    cols = u.shape[2] // 2
    arrays = [u, linv, d, *x_split]
    out = shape(2, 2, cols, HD)
    return call(
        functools.partial(weight_kernel, src),
        "weight_pair",
        (1,),
        [(idx, None)] + [(v, NEAR) for v in arrays],
        [(out, whole(2, 2, cols, HD)), (out, NEAR)],
        after=after,
        work=(5e8, 1e5),
        vmem=16,
    )


def thin_kernel(idx_ref, xh_ref, xl_ref, da_ref, db_ref, o_ref, flip_ref):
    core = idx_ref[0]
    cols = xh_ref.shape[1] // 2
    nb2, src = da_ref.shape[0] // 8, da_ref.shape[1]
    total = None
    for b in range(nb2):
        rows8 = slice(8 * b, 8 * b + 8)
        d = da_ref[rows8, :] + flip_rows(db_ref[rows8, :], 2)
        hi = d.astype(BF16).astype(F32)
        stack = jnp.concatenate([hi, d - hi], axis=0).astype(BF16)
        at = slice(b * src, (b + 1) * src)
        r1 = dot(stack, xh_ref[at, :], NN)
        r2 = dot(stack, xl_ref[at, :], NN)
        q = r1[:8] + (r1[8:] + r2[:8])
        total = q if total is None else total + q
    for k, q in enumerate((total[:, :cols], total[:, cols:])):
        o_ref[core ^ k] = q
        flip_ref[core ^ k] = flip_rows(q, 1)


def thin_sums(idx, x_split, ds, ds_cross, after=()):
    cols = x_split[0].shape[1] // 2
    return call(
        thin_kernel,
        "thin_sums",
        (1,),
        [(idx, None), (x_split[0], NEAR), (x_split[1], NEAR), (ds, whole(*ds.shape)), (ds_cross, whole(*ds.shape))],
        [(shape(2, 8, cols), whole(2, 8, cols))] * 2,
        after=after,
        work=(5e8, 1e5),
        vmem=14,
    )


def skip_back(at, d_ref, weights, idx_ref):
    pair = [split2(rel_rows(piece, 1, idx_ref)) for piece in weights]
    both = [jnp.concatenate([p[n] for p in pair], axis=1) for n in range(2)]
    return dot(cat3(split2(d_ref[at, :]), 1, False), cat3(both, 1, True), NT)


def mix_kernel(blk, form, idx_ref, wh, wl, vh, vl, d_ref, *refs):
    weights, (o_ref, mark_ref) = take_weights(form, refs)
    mark_ref[...] = jnp.zeros_like(mark_ref)
    j = pl.program_id(0)
    rows = vh.shape[0] // 2
    js = pl.ds(pl.multiple_of(j * TJ, TJ), TJ)
    rhs = cat3((vh[...], vl[...]), 0, True)
    o_ref[...] = dot(cat3((wh[blk, :, js], wl[blk, :, js]), 0, False), rhs, TN)

    @pl.when(j == 0)
    def _():
        o_ref[0:rows, :] += skip_back(slice(blk * rows, (blk + 1) * rows), d_ref, weights, idx_ref)


def mix_block(blk, idx, w, v, d, weights, after=()):
    src = w[0].shape[2]
    kd = v[0].shape[1]
    return call(
        functools.partial(mix_kernel, blk, weights),
        "mix_block",
        (src // TJ,),
        [(idx, None)] + [(a, NEAR) for a in (*w, *v, d)] + flat_weights(weights),
        [(shape(src, kd), pl.BlockSpec((TJ, kd), lambda j, i: (j, 0))), (shape(8, 128), whole(8, 128))],
        after=after,
        work=(5e8, 1e5),
        vmem=16,
    )


def feature_kernel(blk, part, form, idx_ref, g_ref, wh, wl, vh, vl, da_ref, db_ref, a_ref, d_ref, *refs):
    weights, refs = take_weights(form, refs)
    oo_ref, os_ref, mark_ref = refs[-3:]
    j = pl.program_id(0)
    mark_ref[...] = jnp.zeros_like(mark_ref)
    half = oo_ref.shape[1]
    rows = vh.shape[0] // 2
    js = pl.ds(pl.multiple_of((part * pl.num_programs(0) + j) * TJ, TJ), TJ)
    rows8 = slice(8 * blk, 8 * blk + 8)
    d = da_ref[rows8, js] + flip_rows(db_ref[rows8, js], 2)
    out = dot(cat3((wh[blk, :, js], wl[blk, :, js]), 0, False), cat3((vh[...], vl[...]), 0, True), TN)
    out = out + (g_ref[...] + dot(thin_rows(d), thin_cols(a_ref[...]), TN))
    oo_ref[...] = out[:, :half]
    os_ref[...] = out[:, half:]
    if part == 0:

        @pl.when(j == 0)
        def _():
            more = skip_back(slice(blk * rows, (blk + 1) * rows), d_ref, weights, idx_ref)
            oo_ref[0:rows, :] += more[:, :half]
            os_ref[0:rows, :] += more[:, half:]


def feature_block(
    blk, part, idx, mixed, w, v, ds, ds_cross, a_half, d, weights, full, nb2, before, after=()
):
    src = w[0].shape[2]
    kd = v[0].shape[1]
    half = kd // 2
    nj = src // TJ
    count = nj // PARTS
    first = part * count
    ins = [(idx, None), (mixed, pl.BlockSpec((TJ, kd), lambda j, i: (first + j, 0)))]
    ins += [(a, NEAR) for a in (*w, *v)]
    ins += [(ds, whole(*ds.shape)), (ds_cross, whole(*ds.shape)), (a_half, whole(8, kd)), (d, NEAR)]
    ins += flat_weights(weights)
    aliases = {}
    if before is not None:
        aliases[len(ins)] = 0
        ins.append((before, HBM))
    return call(
        functools.partial(feature_kernel, blk, part, weights),
        "feature_block",
        (count,),
        ins,
        [
            (shape(*full), pl.BlockSpec((TJ, half), lambda j, i: ((i[0] * nb2 + blk) * nj + first + j, 0))),
            (shape(src // PARTS, half), pl.BlockSpec((TJ, half), lambda j, i: (j, 0))),
            (shape(8, 128), whole(8, 128)),
        ],
        after=after,
        work=(6.4e9, 1e5),
        vmem=18,
        aliases=aliases,
    )


def place_kernel(nb2, idx_ref, *refs):
    parts, (out_ref, mark_ref, buf, sems) = refs[:nb2], refs[nb2 + 1 :]
    mark_ref[...] = jnp.zeros_like(mark_ref)
    src = parts[0].shape[0]
    size = buf.shape[1]
    n = src // size

    def load(b, k):
        return pltpu.make_async_copy(parts[b].at[pl.ds(k * size, size), :], buf.at[b * n + k], sems.at[0, b * n + k])

    def store(b, k):
        at = pl.multiple_of((idx_ref[2] * nb2 + b) * src + k * size, size)
        return pltpu.make_async_copy(buf.at[b * n + k], out_ref.at[pl.ds(at, size), :], sems.at[1, b * n + k])

    every = [(b, k) for b in range(nb2) for k in range(n)]
    for b, k in every:
        load(b, k).start()
    for b, k in every:
        load(b, k).wait()
        store(b, k).start()
    for b, k in every:
        store(b, k).wait()


def place(idx, parts, before, after=()):
    nb2 = len(parts)
    src, half = parts[0].shape
    count = nb2 * src // TJ
    return call(
        functools.partial(place_kernel, nb2),
        "place",
        (1,),
        [(idx, None)] + [(v, HBM) for v in parts] + [(before, HBM)],
        [(shape(*before.shape), HBM), (shape(8, 128), whole(8, 128))],
        scratch=[pltpu.VMEM((count, TJ, half), F32), pltpu.SemaphoreType.DMA((2, count))],
        after=after,
        work=(1e3, 1e6),
        least=2**18,
        vmem=14,
        aliases={1 + nb2: 0},
    )


def split_kernel(at, idx_ref, keep_ref, recv_ref, send_ref, next_ref):
    size = next_ref.shape[1]
    mine = pl.ds(pl.multiple_of(idx_ref[at] * size, size), size)
    other = pl.ds(pl.multiple_of((1 - idx_ref[at]) * size, size), size)
    send_ref[...] = keep_ref[:, other, :] + recv_ref[:, other, :]
    next_ref[...] = keep_ref[:, mine, :] + recv_ref[:, mine, :]


def split_step(at, idx, keep, recv, after=()):
    n, rows, cols = keep.shape
    part = (n, rows // 2, cols)
    return call(
        functools.partial(split_kernel, at),
        "split_step",
        (1,),
        [(idx, None), (keep, NEAR), (recv, whole(n, rows, cols))],
        [(shape(*part), whole(*part)), (shape(*part), NEAR)],
        after=after,
        work=(1e3, keep.size * 8),
        vmem=8,
    )


def add_kernel(idx_ref, a_ref, b_ref, o_ref):
    o_ref[...] = a_ref[...] + b_ref[...]


def add_step(idx, a, b, after=()):
    return call(
        add_kernel,
        "add_step",
        (1,),
        [(idx, None), (a, whole(*a.shape)), (b, whole(*a.shape))],
        [(shape(*a.shape), whole(*a.shape))],
        after=after,
        least=3 * 2**19,
        vmem=8,
        work=(1e3, a.size * 8),
    )[0]


def join_kernel(at, idx_ref, mine_ref, recv_ref, o_ref):
    size = (mine_ref.shape[0] - EXTRA) // 2
    for mat in range(2):
        old = slice(mat * size, (mat + 1) * size)
        put = lambda up: pl.ds(pl.multiple_of(2 * mat * size + up * size, size), size)
        o_ref[put(idx_ref[at]), :] = mine_ref[old, :]
        o_ref[put(1 - idx_ref[at]), :] = recv_ref[old, :]
    o_ref[4 * size :, :] = mine_ref[2 * size :, :] + recv_ref[2 * size :, :]


def join_step(at, idx, mine, recv, after=()):
    rows, cols = mine.shape
    full = 2 * (rows - EXTRA) + EXTRA
    return call(
        functools.partial(join_kernel, at),
        "join_step",
        (1,),
        [(idx, None), (mine, whole(rows, cols)), (recv, whole(rows, cols))],
        [(shape(full, cols), whole(full, cols))],
        after=after,
        work=(1e3, mine.size * 16),
        least=3 * 2**19,
        vmem=10,
    )[0]


def end_kernel(idx_ref, keep_ref, recv_ref, o_ref):
    size = keep_ref.shape[1]
    for mat in range(2):
        o_ref[mat * size : (mat + 1) * size, :] = keep_ref[mat] + recv_ref[mat]
    o_ref[2 * size :, :] = jnp.zeros((EXTRA, o_ref.shape[1]), F32)


def end_step(idx, keep, recv, after=()):
    n, rows, cols = keep.shape
    full = n * rows + EXTRA
    return call(
        end_kernel,
        "end_step",
        (1,),
        [(idx, None), (keep, NEAR), (recv, whole(n, rows, cols))],
        [(shape(full, cols), whole(full, cols))],
        after=after,
        work=(1e3, keep.size * 8),
        least=3 * 2**19,
        vmem=8,
    )[0]


def swap_kernel(idx_ref, keep_ref, recv_ref, q_ref, qr_ref, b_ref, br_ref, o_ref, extra_ref):
    size = keep_ref.shape[1]
    for mat in range(2):
        o_ref[mat * size : (mat + 1) * size, :] = keep_ref[mat] + recv_ref[mat]
    q = q_ref[...] + qr_ref[...]
    width = o_ref.shape[1]
    pick = lambda m: [q[k, n : n + 1, :] for k in range(2) for n in (m, HEADS + m)]
    zero = lambda n: [jnp.zeros((n, width), F32)]
    o_ref[2 * size :, :] = jnp.concatenate(pick(2) + zero(EXTRA - 4), axis=0)
    bias = b_ref[0, 2:3, :] + br_ref[1, 2:3, :]
    extra_ref[...] = jnp.concatenate(zero(4) + pick(0) + [bias] + zero(EXTRA - 9), axis=0)


def swap_step(idx, keep, recv, q, q_recv, sums, sums_recv, after=()):
    n, rows, cols = keep.shape
    full = n * rows + EXTRA
    arrays = [keep, recv, q, q_recv, sums, sums_recv]
    return call(
        swap_kernel,
        "swap_step",
        (1,),
        [(idx, None), (keep, NEAR)] + [(v, whole(*v.shape)) for v in arrays[1:]],
        [(shape(full, cols), whole(full, cols)), (shape(EXTRA, cols), whole(EXTRA, cols))],
        after=after,
        work=(1e3, keep.size * 8),
        least=3 * 2**19,
        vmem=8,
    )


def enter_kernel(idx_ref, recv_ref, extra_ref, o_ref):
    rows = recv_ref.shape[0] - EXTRA
    o_ref[:rows, :] = recv_ref[:rows, :]
    o_ref[rows:, :] = recv_ref[rows:, :] + extra_ref[...]


def enter_step(idx, recv, extra, after=()):
    return call(
        enter_kernel,
        "enter_step",
        (1,),
        [(idx, None), (recv, whole(*recv.shape)), (extra, whole(*extra.shape))],
        [(shape(*recv.shape), whole(*recv.shape))],
        after=after,
        work=(1e3, recv.size * 8),
        least=3 * 2**19,
        vmem=8,
    )[0]


def last_kernel(idx_ref, own_ref, far_ref, att_ref, w_ref, op_ref, os_ref, oa_ref, ob_ref, bias_ref):
    tall = own_ref.shape[0] - EXTRA
    size = tall // 2

    def put(g_ref, first):
        total = None
        for k in range(2):
            at = slice(k * size // 2, (k + 1) * size // 2)
            q = far_ref[tall + first + 2 * k : tall + first + 2 * k + 2, :]
            q = jnp.concatenate([q, jnp.zeros((6, q.shape[1]), F32)], axis=0)
            op_ref[at, :] = g_ref[at, :] + dot(thin_rows(q), thin_cols(att_ref[...]), TN)
            hi = q.astype(BF16).astype(F32)
            stack = jnp.concatenate([hi, q - hi], axis=0).astype(BF16)
            wh, wl = split2(w_ref[at, :])
            r1, r2 = dot(stack, wh, NN), dot(stack, wl, NN)
            new = r1[:8] + (r1[8:] + r2[:8])
            total = new if total is None else total + new
        os_ref[...] = g_ref[size:tall, :]
        return total[0:1], total[1:2]

    @pl.when(pl.program_id(0) == 0)
    def _():
        a, b = put(own_ref, 4)
        oa_ref[...] = a
        ob_ref[...] = b
        bias_ref[...] = far_ref[tall + 8 : tall + 9, :]

    @pl.when(pl.program_id(0) == 1)
    def _():
        a, b = put(far_ref, 0)
        oa_ref[...] += a
        ob_ref[...] += b


def last_step(idx, own, far, att, w_proj, after=()):
    rows, width = own.shape
    size = (rows - EXTRA) // 2
    out = pl.BlockSpec((size, width), lambda g, i: (i[1] ^ g, 0))
    return call(
        last_kernel,
        "last_step",
        (2,),
        [(idx, None)] + [(v, whole(*v.shape)) for v in (own, far, att)] + [(w_proj, out)],
        [(shape(2 * size, width), out)] * 2 + [(shape(1, width), whole(1, width))] * 3,
        after=after,
        work=(1e12, 4e6),
        least=3 * 2**19,
        vmem=16,
    )


def make_step(dp_size):
    bits = [1 << k for k in range(dp_size.bit_length() - 1)]

    def on_device(
        features, adjacency, seed_counts, w_proj, w_skip, attn_src, attn_dst, bias, gamma, beta, cotangent
    ):
        nb, rows, src = adjacency.shape
        cols = features.shape[1]
        nb2 = nb // 2
        h = lax.axis_index("head")
        dpi = lax.axis_index("dp")
        core, side = h & 1, h >> 1
        def to_core(v):
            return lax.ppermute(v, "head", [(i, i ^ 1) for i in range(HEADS)])

        def to_cross(v):
            return lax.ppermute(v, "head", [(i, i ^ 2) for i in range(HEADS)])

        def to_dp(v, bit):
            return lax.ppermute(v, "dp", [(i, i ^ bit) for i in range(dp_size)])

        def half(v, which):
            size = v.shape[0] // 2
            return lax.dynamic_slice_in_dim(v, which * size, size, 0)

        ups = [(dpi >> k) & 1 for k in range(len(bits))]
        idx = jnp.stack([core, side, 1 - core, 1 - side] + ups).astype(jnp.int32)

        with jax.named_scope("fold_attention"):
            folded = jnp.stack(
                [jnp.sum(w_proj * attn_src, axis=1), jnp.sum(w_proj * attn_dst, axis=1)]
            )
            near_folded = to_core(folded)
            folded = jnp.stack([folded, near_folded])
            a_all = jnp.concatenate([folded, to_cross(folded)])
            a_all = a_all.transpose(1, 0, 2).reshape(2 * HEADS, -1)
            a_own = lax.dynamic_slice_in_dim(a_all, h * cols, cols, 1) * LOG2E

        with jax.named_scope("scores"):
            par = jnp.pad(jnp.stack([bias, gamma, beta]), ((0, 5), (0, 0)))
            par_sib = to_core(par)
            s_send, s_keep, x_send = scores(idx, features, a_own)
            s_mine = add_step(idx, s_keep, to_core(s_send))
            x_sib = to_core(relay(idx, x_send, after=[s_mine]))
            s_cross = to_cross(s_mine)

        with jax.named_scope("share_weights"):
            halves, cot_send, mark = pack(idx, w_proj, w_skip, cotangent, after=[s_mine])
            w_far = to_cross(halves)
            cot_sib = to_core(cot_send)

        with jax.named_scope("forward"):
            far_fwd = forward_pair(
                1, idx, features, x_sib, adjacency, s_mine, s_cross, nb2, after=[par_sib, mark]
            )
            x_split, far_fwd = far_fwd[6:], far_fwd[:6]
            w_far = relay(idx, w_far, after=[far_fwd[3]])
            far_weights = [(w_far,), (to_core(w_far),)]
            far_part = pre_pair(idx, *far_fwd[:2], x_split, far_weights, src, whole(nb2 * rows, 2 * HD))
            recv = to_cross(far_part)
            own_fwd = forward_pair(
                0, idx, *x_split, adjacency, s_mine, s_cross, nb2, after=[far_part, cot_sib]
            )
            own_weights = [(w_proj, w_skip), (to_core(w_proj), to_core(w_skip))]
            own_part = pre_pair(idx, *own_fwd[:2], x_split, own_weights, src, NEAR)

        with jax.named_scope("norm"):
            pre, stats, flipped = norm_sums(
                idx, seed_counts, cotangent, cot_sib, par, par_sib, own_part, recv, nb2
            )
            stats = stats + to_core(flipped)
            for bit in bits:
                stats = stats + to_dp(stats, bit)
            act, act_send, d_own, small = norm_apply(
                idx, seed_counts, pre, cotangent, cot_sib, par, par_sib, stats, nb2
            )
            act_recv = to_core(act_send)
            activations = lax.dynamic_update_slice_in_dim(
                act, act_recv, (1 - core) * nb2 * rows, 0
            )
            d_far = to_cross(d_own)

        token = [d_own]

        def note(out):
            token[:] = [out]
            return out

        flat = lambda v: v.reshape(2, 2 * cols, HD)
        backs, fars, theirs = [], [], []
        state = {}

        def scatter(send, keep, recv):
            for k, bit in enumerate(bits):
                send, keep = split_step(4 + k, idx, keep, recv, after=token)
                note(keep)
                recv = to_dp(send, bit)
                yield
            return keep, recv

        def gather(rows):
            for k, bit in reversed(list(enumerate(bits))):
                recv = to_dp(rows, bit)
                yield
                rows = note(join_step(4 + k, idx, rows, recv, after=token))
            return rows

        def own_chain(send, keep):
            keep, recv = yield from scatter(send, flat(keep), flat(to_core(send)))
            rows = note(end_step(idx, keep, recv, after=token))
            state["own"] = yield from gather(rows)

        def far_chain(send, keep):
            keep, recv = yield from scatter(send, flat(keep), flat(to_core(send)))
            while "flip" not in state:
                yield
            message, extra = swap_step(
                idx, keep, recv, state["q"], state["q_recv"], small, state["sums_recv"], after=token
            )
            note(extra)
            recv = to_cross(message)
            yield
            rows = note(enter_step(idx, recv, extra, after=token))
            state["far"] = yield from gather(rows)

        def advance(*chains):
            for c in chains:
                next(c, None)

        def back_far(b):
            fars.append(
                back_block(
                    b, 1, idx, x_split, far_fwd, d_far, far_weights, before=[backs[b][2]],
                    earlier=[f[2] for f in fars] if b == nb2 - 1 else (), after=token,
                )
            )
            note(fars[-1][2])

        half_cols = lambda i: lax.dynamic_slice_in_dim(a_all, i * cols, cols, 1)
        a_half = jnp.concatenate([half_cols(h), half_cols(h ^ 1)], axis=1)

        def features_of(b, part):
            state["gf"], other, mark = feature_block(
                b, part, idx, mixed[b], far_fwd[4:], fars[b][:2], ds, ds_cross, a_half, d_far,
                far_weights, features.shape, nb2,
                before=state.get("gf"), after=token,
            )
            note(mark)
            theirs.append(to_core(other))

        with jax.named_scope("backward"):
            state["sums_recv"] = to_core(small)
            send, keep = weight_pair(
                idx, x_split, own_fwd, d_own, src, after=token + [state["sums_recv"], act_recv]
            )
            note(keep)
            own = own_chain(send, keep)
            mixed = []
            for b in range(nb2):
                backs.append(back_block(b, 0, idx, x_split, own_fwd, d_own, own_weights, after=token))
                note(backs[-1][2])
                if b == 0:
                    advance(own)
            for b in range(nb2):
                out, mark = mix_block(b, idx, own_fwd[4:], backs[b][:2], d_own, own_weights, after=token)
                note(mark)
                mixed.append(out)
            send, keep = weight_pair(idx, x_split, far_fwd, d_far, src, after=token)
            note(keep)
            advance(own)
            far = far_chain(relay(idx, send, after=token), keep)
            advance(far)
            for b in range(nb2):
                back_far(b)
                if b < nb2 - 1:
                    advance(own)
            advance(far, own)
            ds = relay(idx, fars[-1][2], after=token)
            ds_cross = to_cross(ds)
            state["q"], state["q_flip"] = thin_sums(idx, x_split, ds, ds_cross, after=token)
            note(state["q"])
            state["q_recv"] = to_core(state["q_flip"])
            state["flip"] = True
            advance(far, own)
            for b in range(nb2):
                for part in range(PARTS):
                    features_of(b, part)
                    advance(far)
                    if part == 1:
                        advance(own)
            grad_features, mark = place(idx, theirs, state["gf"], after=token)
            note(mark)
            for c in (own, far):
                for _ in c:
                    pass

        with jax.named_scope("last"):
            att = jnp.pad(jnp.stack([attn_src, attn_dst]), ((0, 6), (0, 0)))
            grad_proj, grad_skip, grad_src, grad_dst, grad_bias = last_step(
                idx, state["own"], state["far"], att, w_proj
            )

        return (
            activations,
            grad_features,
            grad_proj,
            grad_skip,
            grad_src[0],
            grad_dst[0],
            grad_bias[0],
            small[0, 0],
            small[0, 1],
        )

    return on_device


def solution(mesh):
    return jax.shard_map(
        make_step(mesh.shape["dp"]),
        mesh=mesh,
        in_specs=(
            P("dp", "head"),
            P("dp", None, None),
            P("dp"),
            P(None, "head"),
            P(None, "head"),
            P("head"),
            P("head"),
            P("head"),
            P("head"),
            P("head"),
            P("dp", "head"),
        ),
        out_specs=(
            P("dp", "head"),
            P("dp", "head"),
            P(None, "head"),
            P(None, "head"),
            P("head"),
            P("head"),
            P("head"),
            P("head"),
            P("head"),
        ),
        check_vma=False,
    )
```

```python
import functools

import jax
import jax.numpy as jnp
from jax import lax
from jax.experimental import pallas as pl
from jax.experimental.pallas import tpu as pltpu
from jax.sharding import PartitionSpec as P

HD = 256
HEADS = 4
TJ = 512
PARTS = 2
EXTRA = 16
eps = 1e-05
LOG2E = 1.4426950408889634
HALF_LN2 = 0.34657359027997264
F32 = jnp.float32
BF16 = jnp.bfloat16
NN = ((1,), (0,))
NT = ((1,), (1,))
TN = ((0,), (0,))
LOW = -3e38
HBM = pl.BlockSpec(memory_space=pltpu.HBM)
ANY = pl.BlockSpec(memory_space=pl.ANY)
NEAR = pl.BlockSpec(memory_space=pltpu.VMEM)


def dot(a, b, form):
    return lax.dot_general(a, b, (form, ((), ())), preferred_element_type=F32)


def split2(x):
    hi = x.astype(BF16)
    return hi, (x - hi.astype(F32)).astype(BF16)


def dot3(a, b, form):
    return dot(a[0], b[0], form) + (dot(a[0], b[1], form) + dot(a[1], b[0], form))


def cat3(a, axis, mixed):
    hi, lo = a
    return jnp.concatenate([hi, lo, hi] if mixed else [hi, hi, lo], axis=axis)


def thin_rows(d):
    hi = d.astype(BF16).astype(F32)
    return jnp.concatenate([hi, hi, d - hi, jnp.zeros_like(d)], axis=0).astype(BF16)


def thin_cols(a):
    hi = a.astype(BF16).astype(F32)
    return jnp.concatenate([hi, a - hi, hi, jnp.zeros_like(a)], axis=0).astype(BF16)


def lane_groups(v):
    out = v[:, :128]
    for k in range(128, v.shape[1], 128):
        out = out + v[:, k : k + 128]
    return out


def leaky2(u):
    soft = jnp.log2(1.0 + jnp.exp2(jnp.minimum(u, 126.0)))
    return jnp.maximum(u, 0.2 * u + 0.8 * soft)


def elu(v):
    return jnp.where(v > 0, v, jnp.exp(jnp.minimum(v, 0.0)) - 1.0)


def flip_rows(v, bit):
    return jnp.concatenate([v[m ^ bit : (m ^ bit) + 1] for m in range(8)], axis=0)


def large(v, least):
    return v.size * v.dtype.itemsize >= least


def held(v, spec, least):
    if spec is NEAR:
        return pltpu.with_memory_space_constraint(v, pltpu.VMEM)
    if spec is ANY:
        return v
    return pltpu.with_memory_space_constraint(v, pltpu.HBM) if large(v, least) else v


def result(v, spec, least):
    if spec is NEAR:
        return pltpu.VMEM(v.shape, v.dtype)
    return pltpu.HBM(v.shape, v.dtype) if large(v, least) else v


def call(kernel, name, grid, ins, outs, scratch=(), after=(), work=(1e6, 1e6), vmem=8, aliases=None, least=3 * 2**19, hold=()):
    n_in = len(ins)
    n_after = len(after) + len(hold)
    hold = [held(v, NEAR, least) for v in hold]
    scalars = 1 if ins[0][1] is None else 0
    ins = ins[:scalars] + [(held(v, spec, least), spec) for v, spec in ins[scalars:]]

    def body(*refs):
        kernel(*refs[:n_in], *refs[n_in + n_after :])

    return pl.pallas_call(
        body,
        grid_spec=pltpu.PrefetchScalarGridSpec(
            num_scalar_prefetch=scalars,
            grid=grid,
            in_specs=[s for _, s in ins[scalars:]] + [ANY] * len(after) + [NEAR] * len(hold),
            out_specs=[s for _, s in outs],
            scratch_shapes=list(scratch),
        ),
        out_shape=[result(v, spec, least) for v, spec in outs],
        compiler_params=pltpu.CompilerParams(
            dimension_semantics=("arbitrary",) * len(grid), vmem_limit_bytes=vmem * 2**20
        ),
        cost_estimate=pl.CostEstimate(
            flops=int(work[0]), bytes_accessed=int(work[1]), transcendentals=0
        ),
        input_output_aliases=aliases or {},
        name=name,
    )(*[v for v, _ in ins], *after, *hold)


class Place:
    def __getitem__(self, k):
        h = lax.axis_index("head")
        if k < 4:
            bit = (h & 1, h >> 1)[k % 2]
            return bit if k < 2 else 1 - bit
        return (lax.axis_index("dp") >> (k - 4)) & 1


def shape(*dims, dtype=F32):
    return jax.ShapeDtypeStruct(dims, dtype)


def whole(*dims):
    return pl.BlockSpec(dims, lambda *_: (0,) * len(dims))


def pack_kernel(idx_ref, a_ref, b_ref, c_ref, d_ref, e_ref, w_ref, o_ref, mine_ref, mark_ref):
    mark_ref[...] = jnp.zeros_like(mark_ref)
    w_ref[0] = a_ref[...]
    w_ref[1] = b_ref[...]
    o_ref[...] = c_ref[...]
    mine_ref[0] = d_ref[...]
    mine_ref[1] = e_ref[...]


def pack(idx, w_proj, w_skip, cotangent, after=()):
    rows, cols = w_proj.shape
    half = rows // 2
    mine = cotangent.shape[0] // 2
    weight = pl.BlockSpec((half, cols), lambda g, i: (i[3], 0))
    return call(
        pack_kernel,
        "pack",
        (1,),
        [
            (idx, None),
            (w_proj, weight),
            (w_skip, weight),
            (cotangent, pl.BlockSpec((mine, cols), lambda g, i: (i[2], 0))),
            (w_proj, pl.BlockSpec((half, cols), lambda g, i: (i[1], 0))),
            (w_skip, pl.BlockSpec((half, cols), lambda g, i: (i[1], 0))),
        ],
        [
            (shape(2, half, cols), whole(2, half, cols)),
            (shape(mine, cols), whole(mine, cols)),
            (shape(2, half, cols), whole(2, half, cols)),
            (shape(8, 128), whole(8, 128)),
        ],
        after=after,
        work=(1e3, 1e6),
        least=2**18,
        vmem=16,
    )


def relay_kernel(v_ref, o_ref):
    o_ref[...] = v_ref[...]


def relay(v, spec, after=()):
    near = spec is NEAR
    return call(
        relay_kernel if near else lambda *_: None,
        "relay",
        (1,),
        [(v, spec)],
        [(shape(*v.shape), spec)],
        after=after,
        work=(1e3, 1e3),
        least=2**18,
        aliases=None if near else {0: 0},
    )[0]


def score_kernel(idx_ref, x_ref, a_ref, send_ref, keep_ref, copy_ref):
    x = x_ref[...]
    x1 = x.astype(BF16)
    rest = x - x1.astype(F32)
    x2 = rest.astype(BF16)
    x3 = (rest - x2.astype(F32)).astype(BF16)
    a = a_ref[...]
    a1 = a.astype(BF16).astype(F32)
    a2 = (a - a1).astype(BF16).astype(F32)
    a3 = (a - a1) - a2
    stack = jnp.concatenate([a1, a2, a3, jnp.zeros_like(a)], axis=0).astype(BF16)
    r1 = dot(stack, x1, NT)
    r2 = dot(stack[:16], x2, NT)
    r3 = dot(stack[:16], x3, NT)
    s = r1[:8] + (r1[8:16] + r2[:8]) + (r1[16:24] + r2[8:16] + r3[:8])

    @pl.when(pl.program_id(0) == 0)
    def _():
        send_ref[...] = flip_rows(s, 1)
        copy_ref[...] = x

    @pl.when(pl.program_id(0) == 1)
    def _():
        keep_ref[...] = s


def scores(idx, features, a_own, after=()):
    rows, cols = features.shape
    tile = 2048
    n = rows // 2 // tile
    return call(
        score_kernel,
        "scores",
        (2, n),
        [
            (idx, None),
            (features, pl.BlockSpec((tile, cols), lambda g, i, s: ((s[0] ^ 1 ^ g) * n + i, 0))),
            (a_own, whole(8, cols)),
        ],
        [
            (shape(8, rows // 2), pl.BlockSpec((8, tile), lambda g, i, s: (0, i * (1 - g) + (n - 1) * g))),
            (shape(8, rows // 2), pl.BlockSpec((8, tile), lambda g, i, s: (0, i * g))),
            (
                shape(rows // 2, cols),
                pl.BlockSpec((tile, cols), lambda g, i, s: (i * (1 - g) + (n - 1) * g, 0)),
            ),
        ],
        after=after,
        vmem=24,
        work=(2 * rows * cols * 24, rows * cols * 4),
    )


def forward_kernel(pair, idx_ref, adj_ref, sa_ref, sb_ref, xa_ref, xb_ref, *refs):
    first = pair == 1
    u_ref, linv_ref, tm_ref, s_ref, wh_ref, wl_ref = refs[:6]
    xh_ref, xl_ref = refs[6:8] if first else (xa_ref, xb_ref)
    rows, src = adj_ref.shape[1], adj_ref.shape[2]
    b = pl.program_id(0)
    nb2 = pl.num_programs(0)
    block = pl.ds(pl.multiple_of(b * src, src), src)

    def loads(blk):
        xbuf, sems = refs[8:]
        to = lax.rem(blk, 2)
        at = pl.ds(pl.multiple_of(blk * src, src), src)
        own = pl.ds(pl.multiple_of((idx_ref[0] * nb2 + blk) * src, src), src)
        return (
            pltpu.make_async_copy(xa_ref.at[own, :], xbuf.at[to, 0], sems.at[to, 0]),
            pltpu.make_async_copy(xb_ref.at[at, :], xbuf.at[to, 1], sems.at[to, 1]),
        )

    if first:

        @pl.when(b == 0)
        def _():
            for copy in loads(b):
                copy.start()

    s_all = sa_ref[:, block] + flip_rows(sb_ref[:, block], 2)
    s_ref[:, block] = s_all
    tm_ref[b, :, 0:8] = jnp.transpose(s_all[:, :rows])
    part = lambda m, k, n: s_ref[m : m + 1, pl.ds(pl.multiple_of(b * src + k, 128), n)]
    heads = (2 * pair, 2 * pair + 1)
    step = 64

    for r in range(0, rows, step):
        best = [jnp.full((step, 128), LOW, F32) for _ in heads]
        for k in range(0, src, 128):
            linked = adj_ref[0, r : r + step, k : k + 128] > 0
            for n, m in enumerate(heads):
                best[n] = jnp.maximum(best[n], jnp.where(linked, part(m, k, 128), LOW))
        for n, m in enumerate(heads):
            t = tm_ref[b, r : r + step, HEADS + m : HEADS + m + 1]
            top = leaky2(t + jnp.max(best[n], axis=1, keepdims=True))
            tm_ref[b, r : r + step, m : m + 1] = top

    for n in range(3):
        if n < 2:
            m = heads[n]
            for r in range(0, rows, 32):
                at = slice(r, r + 32)
                to = slice(n * rows + r, n * rows + r + 32)
                t = tm_ref[b, at, HEADS + m : HEADS + m + 1]
                top = tm_ref[b, at, m : m + 1]
                acc = None
                for k in range(0, src, 512):
                    ks = slice(k, k + 512)
                    q = leaky2(t + part(m, k, 512))
                    w = jnp.where(adj_ref[0, at, ks] > 0, jnp.exp2(q - top), 0.0)
                    hi, lo = split2(w)
                    wh_ref[b, to, ks] = hi
                    wl_ref[b, to, ks] = lo
                    acc = lane_groups(w) if acc is None else acc + lane_groups(w)
                linv = 1.0 / jnp.sum(acc, axis=1, keepdims=True)
                linv_ref[b, to, :] = jnp.broadcast_to(linv, (32, 128))
        if n == 0 and first:
            cols = xa_ref.shape[1]
            xbuf = refs[8]
            slot = lax.rem(b, 2)
            for copy in loads(b):
                copy.wait()

            @pl.when(b + 1 < nb2)
            def _():
                for copy in loads(b + 1):
                    copy.start()

            @pl.loop(0, src, step=256)
            def _(r):
                at = pl.ds(pl.multiple_of(b * src + r, 256), 256)
                for k in range(2):
                    hi, lo = split2(xbuf[slot, k, pl.ds(r, 256), :])
                    xh_ref[at, k * cols : (k + 1) * cols] = hi
                    xl_ref[at, k * cols : (k + 1) * cols] = lo

        if n > 0:
            at = slice((n - 1) * rows, n * rows)
            lhs = cat3((wh_ref[b, at, :], wl_ref[b, at, :]), 1, False)
            rhs = cat3((xh_ref[block, :], xl_ref[block, :]), 0, True)
            u_ref[b, at, :] = dot(lhs, rhs, NN)


def forward_pair(pair, idx, xa, xb, adjacency, s_mine, s_cross, nb2, after=()):
    rows, src = adjacency.shape[1:]
    first = pair == 1
    cols = xa.shape[1]
    kd = 2 * cols if first else cols
    two = 2 * rows
    outs = [
        shape(nb2, two, kd),
        shape(nb2, two, 128),
        shape(nb2, rows, 128),
        shape(8, nb2 * src),
        shape(nb2, two, src, dtype=BF16),
        shape(nb2, two, src, dtype=BF16),
    ]
    if first:
        outs += [shape(nb2 * src, kd, dtype=BF16)] * 2
    return call(
        functools.partial(forward_kernel, pair),
        "forward_pair",
        (nb2,),
        [
            (idx, None),
            (adjacency, pl.BlockSpec((1, rows, src), lambda b, i: (i[0] * nb2 + b, 0, 0))),
            (s_mine, NEAR),
            (s_cross, NEAR),
            (xa, HBM if first else NEAR),
            (xb, ANY if first else NEAR),
        ],
        [(v, NEAR) for v in outs],
        scratch=[pltpu.VMEM((2, 2, src, cols), F32), pltpu.SemaphoreType.DMA((2, 2))] if first else [],
        after=after,
        work=(1e12 if first else 1e8, 1e5),
        vmem=22 if first else 16,
    )


def rel_rows(piece, mat, idx_ref):
    core, side = idx_ref[0], idx_ref[1]
    if len(piece) == 2:
        ref = piece[mat]
        cols = ref.shape[0] // 4
        first = side * 2 * cols
    else:
        ref = piece[0].at[mat]
        cols = ref.shape[0] // 2
        first = 0
    at = lambda k: pl.ds(pl.multiple_of(first + k * cols, cols), cols)
    return jnp.concatenate([ref[at(core), :], ref[at(core ^ 1), :]], axis=0)


def flat_weights(pieces):
    return [(v, NEAR) for p in pieces for v in p]


def take_weights(pieces, refs):
    out = []
    for p in pieces:
        out.append(refs[: len(p)])
        refs = refs[len(p) :]
    return out, refs


def pre_kernel(form, src, u_ref, linv_ref, xh_ref, xl_ref, *refs):
    idx_ref = Place()
    weights, (o_ref,) = take_weights(form, refs)
    nb2, two = u_ref.shape[:2]
    rows = two // 2
    stack = lambda parts: jnp.concatenate(list(parts), axis=0)
    tops = [slice(b * src, b * src + rows) for b in range(nb2)]
    x = (stack(xh_ref[t, :] for t in tops), stack(xl_ref[t, :] for t in tops))
    for a, piece in enumerate(weights):
        at = slice(a * rows, (a + 1) * rows)
        mixed = split2(stack(u_ref[b, at, :] * linv_ref[b, at, 0:1] for b in range(nb2)))
        lhs = jnp.concatenate([cat3(mixed, 1, False), cat3(x, 1, False)], axis=1)
        proj, skip = split2(rel_rows(piece, 0, idx_ref)), split2(rel_rows(piece, 1, idx_ref))
        rhs = jnp.concatenate([cat3(proj, 0, True), cat3(skip, 0, True)], axis=0)
        o_ref[:, a * HD : (a + 1) * HD] = dot(lhs, rhs, NN)


def pre_pair(idx, u, linv, x_split, weights, src, spec, after=()):
    nb2, two, kd = u.shape
    rows = two // 2
    return call(
        functools.partial(pre_kernel, weights, src),
        "pre_pair",
        (1,),
        [(u, NEAR), (linv, NEAR), (x_split[0], NEAR), (x_split[1], NEAR)] + flat_weights(weights),
        [(shape(nb2 * rows, 2 * HD), spec)],
        after=after,
        work=(1e8, 1e5),
        vmem=16,
    )[0]


def live_rows(idx_ref, counts_ref, nb2, rows):
    parts = []
    for b in range(nb2):
        row = lax.broadcasted_iota(jnp.int32, (rows, 1), 0)
        parts.append((row < counts_ref[idx_ref[0] * nb2 + b]).astype(F32))
    return jnp.concatenate(parts, axis=0)


def stats_kernel(nb2, idx_ref, counts_ref, ca_ref, cb_ref, pa_ref, pb_ref, part_ref, recv_ref, pre_ref, st_ref, flip_ref):
    rows = part_ref.shape[0] // nb2
    total = lambda v: jnp.sum(v, axis=0, keepdims=True)
    live = live_rows(idx_ref, counts_ref, nb2, rows)
    for a, (c_ref, p_ref) in enumerate(((ca_ref, pa_ref), (cb_ref, pb_ref))):
        cols = slice(a * HD, (a + 1) * HD)
        bias = p_ref[0:1, :]
        pre = part_ref[:, cols] + recv_ref[:, cols] + bias
        pre_ref[:, cols] = pre
        act = (elu(pre) - elu(bias)) * live
        g = c_ref[...] * live
        rows8 = [total(act), total(act * act), total(g), total(g * act)]
        rows8.append(jnp.broadcast_to(total(live), (1, HD)))
        rows8.append(jnp.zeros((3, HD), F32))
        stats = jnp.concatenate(rows8, axis=0)
        st_ref[a] = stats
        flip_ref[1 - a] = stats


def norm_sums(hold, idx, counts, cotangent, cot_sib, par, par_sib, part, recv, nb2):
    full = part.shape[0]
    return call(
        functools.partial(stats_kernel, nb2),
        "norm_sums",
        (1,),
        [
            (idx, None),
            (counts, pl.BlockSpec(memory_space=pltpu.SMEM)),
            (cotangent, pl.BlockSpec((full, HD), lambda g, i: (i[0], 0))),
            (cot_sib, whole(full, HD)),
            (par, whole(8, HD)),
            (par_sib, whole(8, HD)),
            (part, NEAR),
            (recv, whole(full, 2 * HD)),
        ],
        [
            (shape(full, 2 * HD), NEAR),
            (shape(2, 8, HD), whole(2, 8, HD)),
            (shape(2, 8, HD), whole(2, 8, HD)),
        ],
        work=(1e8, 1e5),
        least=3 * 2**19,
        hold=hold,
        vmem=14,
    )


def apply_kernel(
    nb2, idx_ref, counts_ref, pre_ref, ca_ref, cb_ref, pa_ref, pb_ref, st_ref, act_ref, send_ref, d_ref, o_ref
):
    rows = pre_ref.shape[0] // nb2
    live = live_rows(idx_ref, counts_ref, nb2, rows)
    for a, (c_ref, p_ref, out_ref) in enumerate(
        ((ca_ref, pa_ref, act_ref), (cb_ref, pb_ref, send_ref))
    ):
        cols = slice(a * HD, (a + 1) * HD)
        bias, gamma, beta = p_ref[0:1, :], p_ref[1:2, :], p_ref[2:3, :]
        count = st_ref[a, 4:5, :]
        mean = st_ref[a, 0:1, :] / count
        inv = lax.rsqrt(st_ref[a, 1:2, :] / count - mean * mean + eps)
        grad_beta = st_ref[a, 2:3, :]
        grad_gamma = inv * (st_ref[a, 3:4, :] - mean * grad_beta)
        pre = pre_ref[:, cols]
        nrm = (elu(pre) - elu(bias) - mean) * inv
        out_ref[...] = live * (gamma * nrm + beta)
        g = c_ref[...] * live
        d = live * (gamma * inv) * (g - grad_beta / count - nrm * (grad_gamma / count))
        d = d * jnp.exp(jnp.minimum(pre, 0.0))
        d_ref[:, cols] = d
        o_ref[a, 0:1, :] = grad_gamma
        o_ref[a, 1:2, :] = grad_beta
        o_ref[a, 2:3, :] = jnp.sum(d, axis=0, keepdims=True)
        o_ref[a, 3:8, :] = jnp.zeros((5, HD), F32)


def norm_apply(hold, idx, counts, pre, cotangent, cot_sib, par, par_sib, stats, nb2):
    full = pre.shape[0]
    return call(
        functools.partial(apply_kernel, nb2),
        "norm_apply",
        (1,),
        [
            (idx, None),
            (counts, pl.BlockSpec(memory_space=pltpu.SMEM)),
            (pre, NEAR),
            (cotangent, pl.BlockSpec((full, HD), lambda g, i: (i[0], 0))),
            (cot_sib, whole(full, HD)),
            (par, whole(8, HD)),
            (par_sib, whole(8, HD)),
            (stats, whole(2, 8, HD)),
        ],
        [
            (shape(2 * full, HD), pl.BlockSpec((full, HD), lambda g, i: (i[0], 0))),
            (shape(full, HD), whole(full, HD)),
            (shape(full, 2 * HD), NEAR),
            (shape(2, 8, HD), whole(2, 8, HD)),
        ],
        least=3 * 2**19,
        hold=hold,
        vmem=14,
        work=(1e8, 1e5),
    )


def back_kernel(
    blk, pair, form, prior, xh_ref, xl_ref, wh_ref, wl_ref, s_ref, tm_ref, d_ref, linv_ref, u_ref, *refs
):
    idx_ref = Place()
    weights, refs = take_weights(form, refs)
    before, refs = refs[:pair], refs[pair:]
    earlier, refs = refs[:prior], refs[prior:]
    vh_ref, vl_ref, ds_ref, dp, delta, tacc = refs
    rows = tm_ref.shape[1]
    src = wh_ref.shape[2]
    base = 8 * prior
    for n, v in enumerate(earlier):
        ds_ref[8 * n : 8 * n + 8, :] = v[...]
    ds_ref[base : base + 8, :] = before[0][...] if pair == 1 else jnp.zeros((8, src), F32)
    tacc[...] = jnp.zeros_like(tacc)
    for a, piece in enumerate(weights):
        at = slice(a * rows, (a + 1) * rows)
        linv = linv_ref[blk, at, :]
        d = split2(d_ref[blk * rows : (blk + 1) * rows, a * HD : (a + 1) * HD] * linv[:, 0:1])
        v = dot(cat3(d, 1, False), cat3(split2(rel_rows(piece, 0, idx_ref)), 1, True), NT)
        hi, lo = split2(v)
        vh_ref[at, :] = hi
        vl_ref[at, :] = lo
        delta[at, :] = jnp.sum(v * u_ref[blk, at, :], axis=1, keepdims=True) * linv
    width = dp.shape[1]
    for j in range(src // width):
        js = slice(j * width, (j + 1) * width)
        xs = slice(blk * src + j * width, blk * src + (j + 1) * width)
        x = (xh_ref[xs, :], xl_ref[xs, :])
        dp[...] = dot(cat3((vh_ref[...], vl_ref[...]), 1, False), cat3(x, 1, True), NT)
        for a in range(2):
            m = 2 * pair + a
            s = s_ref[m : m + 1, xs] * HALF_LN2
            total = None
            for r in range(0, rows, 32):
                at = slice(r, r + 32)
                ar = slice(a * rows + r, a * rows + r + 32)
                t = tm_ref[blk, at, HEADS + m : HEADS + m + 1] * HALF_LN2
                slope = 0.6 + 0.4 * jnp.tanh(t + s)
                w = wh_ref[blk, ar, js].astype(F32) + wl_ref[blk, ar, js].astype(F32)
                dv = (w * slope) * (dp[ar, :] - delta[ar, 0:1])
                tacc[ar, :] += lane_groups(dv)
                total = dv if total is None else total + dv
            ds_ref[base + m : base + m + 1, js] = jnp.sum(total, axis=0, keepdims=True)
    for a in range(2):
        m = HEADS + 2 * pair + a
        sums = jnp.sum(tacc[a * rows : (a + 1) * rows, :], axis=1, keepdims=True)
        turned = jnp.transpose(jnp.broadcast_to(sums, (rows, 128)))
        ds_ref[base + m : base + m + 1, 0:rows] = turned[0:1, :]


def back_block(blk, pair, idx, x_split, fwd, d, weights, before=(), earlier=(), after=()):
    u, linv, tm, s, wh, wl = fwd
    two, src = wh.shape[1:]
    kd = u.shape[2]
    tj = 2 * TJ
    arrays = [*x_split, wh, wl, s, tm, d, linv, u]
    rest = [*before, *earlier]
    return call(
        functools.partial(back_kernel, blk, pair, weights, len(earlier)),
        "back_block",
        (1,),
        [(v, NEAR) for v in arrays] + flat_weights(weights) + [(v, NEAR) for v in rest],
        [
            (shape(two, kd, dtype=BF16), NEAR),
            (shape(two, kd, dtype=BF16), NEAR),
            (shape(8 * len(earlier) + 8, src), NEAR),
        ],
        scratch=[pltpu.VMEM((two, tj), F32), pltpu.VMEM((two, 128), F32), pltpu.VMEM((two, 128), F32)],
        after=after,
        work=(1e8, 1e5),
        vmem=16,
    )


def weight_kernel(src, u_ref, linv_ref, d_ref, xh_ref, xl_ref, send_ref, keep_ref):
    idx_ref = Place()
    core = idx_ref[0]
    nb2, two = u_ref.shape[:2]
    rows = two // 2
    stack = lambda parts: jnp.concatenate(list(parts), axis=0)
    tops = [slice(b * src, b * src + rows) for b in range(nb2)]
    x = cat3((stack(xh_ref[t, :] for t in tops), stack(xl_ref[t, :] for t in tops)), 0, False)
    for a, ref in ((1, send_ref), (0, keep_ref)):
        at = slice(a * rows, (a + 1) * rows)
        d = d_ref[:, a * HD : (a + 1) * HD]
        u = split2(stack(u_ref[b, at, :] for b in range(nb2)))
        dn = split2(d * stack(linv_ref[b, at, 0:1] for b in range(nb2)))
        gp = dot(cat3(u, 0, False), cat3(dn, 0, True), TN)
        gs = dot(x, cat3(split2(d), 0, True), TN)
        cols = gp.shape[0] // 2
        for mat, g in enumerate((gp, gs)):
            ref[mat, core] = g[:cols]
            ref[mat, core ^ 1] = g[cols:]


def weight_pair(idx, x_split, fwd, d, src, after=()):
    u, linv = fwd[:2]
    cols = u.shape[2] // 2
    arrays = [u, linv, d, *x_split]
    out = shape(2, 2, cols, HD)
    return call(
        functools.partial(weight_kernel, src),
        "weight_pair",
        (1,),
        [(v, NEAR) for v in arrays],
        [(out, NEAR), (out, NEAR)],
        after=after,
        work=(1e8, 1e5),
        vmem=16,
    )


def thin_kernel(xh_ref, xl_ref, da_ref, db_ref, o_ref, flip_ref):
    idx_ref = Place()
    core = idx_ref[0]
    cols = xh_ref.shape[1] // 2
    nb2, src = da_ref.shape[0] // 8, da_ref.shape[1]
    total = None
    for b in range(nb2):
        rows8 = slice(8 * b, 8 * b + 8)
        d = da_ref[rows8, :] + flip_rows(db_ref[rows8, :], 2)
        hi = d.astype(BF16).astype(F32)
        stack = jnp.concatenate([hi, d - hi], axis=0).astype(BF16)
        at = slice(b * src, (b + 1) * src)
        r1 = dot(stack, xh_ref[at, :], NN)
        r2 = dot(stack, xl_ref[at, :], NN)
        q = r1[:8] + (r1[8:] + r2[:8])
        total = q if total is None else total + q
    for k, q in enumerate((total[:, :cols], total[:, cols:])):
        o_ref[core ^ k] = q
        flip_ref[core ^ k] = flip_rows(q, 1)


def thin_sums(idx, x_split, ds, ds_cross, after=()):
    cols = x_split[0].shape[1] // 2
    return call(
        thin_kernel,
        "thin_sums",
        (1,),
        [(x_split[0], NEAR), (x_split[1], NEAR), (ds, NEAR), (ds_cross, NEAR)],
        [(shape(2, 8, cols), NEAR)] * 2,
        after=after,
        work=(1e8, 1e5),
        vmem=14,
    )


def skip_back(at, d_ref, weights, idx_ref):
    pair = [split2(rel_rows(piece, 1, idx_ref)) for piece in weights]
    both = [jnp.concatenate([p[n] for p in pair], axis=1) for n in range(2)]
    return dot(cat3(split2(d_ref[at, :]), 1, False), cat3(both, 1, True), NT)


def mix_kernel(blk, form, wh, wl, vh, vl, d_ref, *refs):
    idx_ref = Place()
    weights, (o_ref, mark_ref) = take_weights(form, refs)
    mark_ref[...] = jnp.zeros_like(mark_ref)
    j = pl.program_id(0)
    rows = vh.shape[0] // 2
    js = pl.ds(pl.multiple_of(j * TJ, TJ), TJ)
    rhs = cat3((vh[...], vl[...]), 0, True)
    o_ref[...] = dot(cat3((wh[blk, :, js], wl[blk, :, js]), 0, False), rhs, TN)

    @pl.when(j == 0)
    def _():
        o_ref[0:rows, :] += skip_back(slice(blk * rows, (blk + 1) * rows), d_ref, weights, idx_ref)


def mix_block(blk, idx, w, v, d, weights, after=()):
    src = w[0].shape[2]
    kd = v[0].shape[1]
    return call(
        functools.partial(mix_kernel, blk, weights),
        "mix_block",
        (src // TJ,),
        [(a, NEAR) for a in (*w, *v, d)] + flat_weights(weights),
        [(shape(src, kd), pl.BlockSpec((TJ, kd), lambda j: (j, 0))), (shape(8, 128), whole(8, 128))],
        after=after,
        work=(1e8, 1e5),
        vmem=16,
    )


def feature_kernel(blk, part, form, idx_ref, g_ref, wh, wl, vh, vl, da_ref, db_ref, a_ref, d_ref, *refs):
    weights, refs = take_weights(form, refs)
    oo_ref, os_ref, mark_ref = refs[-3:]
    j = pl.program_id(0)
    mark_ref[...] = jnp.zeros_like(mark_ref)
    half = oo_ref.shape[1]
    rows = vh.shape[0] // 2
    js = pl.ds(pl.multiple_of((part * pl.num_programs(0) + j) * TJ, TJ), TJ)
    rows8 = slice(8 * blk, 8 * blk + 8)
    d = da_ref[rows8, js] + flip_rows(db_ref[rows8, js], 2)
    out = dot(cat3((wh[blk, :, js], wl[blk, :, js]), 0, False), cat3((vh[...], vl[...]), 0, True), TN)
    out = out + (g_ref[...] + dot(thin_rows(d), thin_cols(a_ref[...]), TN))
    oo_ref[...] = out[:, :half]
    os_ref[...] = out[:, half:]
    if part == 0:

        @pl.when(j == 0)
        def _():
            more = skip_back(slice(blk * rows, (blk + 1) * rows), d_ref, weights, idx_ref)
            oo_ref[0:rows, :] += more[:, :half]
            os_ref[0:rows, :] += more[:, half:]


def feature_block(
    blk, part, idx, mixed, w, v, ds, ds_cross, a_half, d, weights, full, nb2, before, after=()
):
    src = w[0].shape[2]
    kd = v[0].shape[1]
    half = kd // 2
    nj = src // TJ
    count = nj // PARTS
    first = part * count
    ins = [(idx, None), (mixed, pl.BlockSpec((TJ, kd), lambda j, i: (first + j, 0)))]
    ins += [(a, NEAR) for a in (*w, *v)]
    ins += [(ds, NEAR), (ds_cross, NEAR), (a_half, NEAR), (d, NEAR)]
    ins += flat_weights(weights)
    aliases = {}
    if before is not None:
        aliases[len(ins)] = 0
        ins.append((before, HBM))
    return call(
        functools.partial(feature_kernel, blk, part, weights),
        "feature_block",
        (count,),
        ins,
        [
            (shape(*full), pl.BlockSpec((TJ, half), lambda j, i: ((i[0] * nb2 + blk) * nj + first + j, 0))),
            (shape(src // PARTS, half), pl.BlockSpec((TJ, half), lambda j, i: (j, 0))),
            (shape(8, 128), whole(8, 128)),
        ],
        after=after,
        work=(6.4e9, 1e5),
        vmem=18,
        aliases=aliases,
    )


def place_kernel(nb2, idx_ref, *refs):
    parts, (out_ref, mark_ref, buf, sems) = refs[:nb2], refs[nb2 + 1 :]
    mark_ref[...] = jnp.zeros_like(mark_ref)
    src = parts[0].shape[0]
    size = buf.shape[1]
    n = src // size

    def load(b, k):
        return pltpu.make_async_copy(parts[b].at[pl.ds(k * size, size), :], buf.at[b * n + k], sems.at[0, b * n + k])

    def store(b, k):
        at = pl.multiple_of((idx_ref[2] * nb2 + b) * src + k * size, size)
        return pltpu.make_async_copy(buf.at[b * n + k], out_ref.at[pl.ds(at, size), :], sems.at[1, b * n + k])

    every = [(b, k) for b in range(nb2) for k in range(n)]
    for b, k in every:
        load(b, k).start()
    for b, k in every:
        load(b, k).wait()
        store(b, k).start()
    for b, k in every:
        store(b, k).wait()


def place(idx, parts, before, after=()):
    nb2 = len(parts)
    src, half = parts[0].shape
    count = nb2 * src // TJ
    return call(
        functools.partial(place_kernel, nb2),
        "place",
        (1,),
        [(idx, None)] + [(v, HBM) for v in parts] + [(before, HBM)],
        [(shape(*before.shape), HBM), (shape(8, 128), whole(8, 128))],
        scratch=[pltpu.VMEM((count, TJ, half), F32), pltpu.SemaphoreType.DMA((2, count))],
        after=after,
        work=(1e3, 1e6),
        least=2**18,
        vmem=14,
        aliases={1 + nb2: 0},
    )


def split_kernel(at, keep_ref, recv_ref, send_ref, next_ref):
    idx_ref = Place()
    size = next_ref.shape[1]
    mine = pl.ds(pl.multiple_of(idx_ref[at] * size, size), size)
    other = pl.ds(pl.multiple_of((1 - idx_ref[at]) * size, size), size)
    send_ref[...] = keep_ref[:, other, :] + recv_ref[:, other, :]
    next_ref[...] = keep_ref[:, mine, :] + recv_ref[:, mine, :]


def split_step(at, idx, keep, recv, after=()):
    n, rows, cols = keep.shape
    part = (n, rows // 2, cols)
    return call(
        functools.partial(split_kernel, at),
        "split_step",
        (1,),
        [(keep, NEAR), (recv, NEAR)],
        [(shape(*part), NEAR)] * 2,
        after=after,
        work=(1e3, keep.size * 8),
        vmem=8,
    )


def add_kernel(a_ref, b_ref, o_ref):
    o_ref[...] = a_ref[...] + b_ref[...]


def add_step(idx, a, b, after=()):
    return call(
        add_kernel,
        "add_step",
        (1,),
        [(a, NEAR), (b, NEAR)],
        [(shape(*a.shape), NEAR)],
        after=after,
        least=3 * 2**19,
        vmem=8,
        work=(1e3, a.size * 8),
    )[0]


def join_kernel(at, mine_ref, recv_ref, o_ref):
    idx_ref = Place()
    size = (mine_ref.shape[0] - EXTRA) // 2
    for mat in range(2):
        old = slice(mat * size, (mat + 1) * size)
        put = lambda up: pl.ds(pl.multiple_of(2 * mat * size + up * size, size), size)
        o_ref[put(idx_ref[at]), :] = mine_ref[old, :]
        o_ref[put(1 - idx_ref[at]), :] = recv_ref[old, :]
    o_ref[4 * size :, :] = mine_ref[2 * size :, :] + recv_ref[2 * size :, :]


def join_step(at, idx, mine, recv, after=()):
    rows, cols = mine.shape
    full = 2 * (rows - EXTRA) + EXTRA
    return call(
        functools.partial(join_kernel, at),
        "join_step",
        (1,),
        [(mine, NEAR), (recv, NEAR)],
        [(shape(full, cols), NEAR)],
        after=after,
        work=(1e3, mine.size * 16),
        least=3 * 2**19,
        vmem=10,
    )[0]


def end_kernel(keep_ref, recv_ref, o_ref):
    size = keep_ref.shape[1]
    for mat in range(2):
        o_ref[mat * size : (mat + 1) * size, :] = keep_ref[mat] + recv_ref[mat]
    o_ref[2 * size :, :] = jnp.zeros((EXTRA, o_ref.shape[1]), F32)


def end_step(idx, keep, recv, after=()):
    n, rows, cols = keep.shape
    full = n * rows + EXTRA
    return call(
        end_kernel,
        "end_step",
        (1,),
        [(keep, NEAR), (recv, NEAR)],
        [(shape(full, cols), NEAR)],
        after=after,
        work=(1e3, keep.size * 8),
        least=3 * 2**19,
        vmem=8,
    )[0]


def swap_kernel(keep_ref, recv_ref, q_ref, qr_ref, b_ref, br_ref, o_ref, extra_ref):
    size = keep_ref.shape[1]
    for mat in range(2):
        o_ref[mat * size : (mat + 1) * size, :] = keep_ref[mat] + recv_ref[mat]
    q = q_ref[...] + qr_ref[...]
    width = o_ref.shape[1]
    pick = lambda m: [q[k, n : n + 1, :] for k in range(2) for n in (m, HEADS + m)]
    zero = lambda n: [jnp.zeros((n, width), F32)]
    o_ref[2 * size :, :] = jnp.concatenate(pick(2) + zero(EXTRA - 4), axis=0)
    bias = b_ref[0, 2:3, :] + br_ref[1, 2:3, :]
    extra_ref[...] = jnp.concatenate(zero(4) + pick(0) + [bias] + zero(EXTRA - 9), axis=0)


def swap_step(idx, keep, recv, q, q_recv, sums, sums_recv, after=()):
    n, rows, cols = keep.shape
    full = n * rows + EXTRA
    arrays = [keep, recv, q, q_recv, sums, sums_recv]
    return call(
        swap_kernel,
        "swap_step",
        (1,),
        [(v, NEAR) for v in arrays],
        [(shape(full, cols), NEAR), (shape(EXTRA, cols), NEAR)],
        after=after,
        work=(1e3, keep.size * 8),
        least=3 * 2**19,
        vmem=8,
    )


def enter_kernel(recv_ref, extra_ref, o_ref):
    rows = recv_ref.shape[0] - EXTRA
    o_ref[:rows, :] = recv_ref[:rows, :]
    o_ref[rows:, :] = recv_ref[rows:, :] + extra_ref[...]


def enter_step(idx, recv, extra, after=()):
    return call(
        enter_kernel,
        "enter_step",
        (1,),
        [(recv, NEAR), (extra, NEAR)],
        [(shape(*recv.shape), NEAR)],
        after=after,
        work=(1e3, recv.size * 8),
        least=3 * 2**19,
        vmem=8,
    )[0]


def last_kernel(idx_ref, own_ref, far_ref, att_ref, w_ref, op_ref, os_ref, oa_ref, ob_ref, bias_ref):
    tall = own_ref.shape[0] - EXTRA
    size = tall // 2

    def put(g_ref, first):
        total = None
        for k in range(2):
            at = slice(k * size // 2, (k + 1) * size // 2)
            q = far_ref[tall + first + 2 * k : tall + first + 2 * k + 2, :]
            q = jnp.concatenate([q, jnp.zeros((6, q.shape[1]), F32)], axis=0)
            op_ref[at, :] = g_ref[at, :] + dot(thin_rows(q), thin_cols(att_ref[...]), TN)
            hi = q.astype(BF16).astype(F32)
            stack = jnp.concatenate([hi, q - hi], axis=0).astype(BF16)
            wh, wl = split2(w_ref[at, :])
            r1, r2 = dot(stack, wh, NN), dot(stack, wl, NN)
            new = r1[:8] + (r1[8:] + r2[:8])
            total = new if total is None else total + new
        os_ref[...] = g_ref[size:tall, :]
        return total[0:1], total[1:2]

    @pl.when(pl.program_id(0) == 0)
    def _():
        a, b = put(own_ref, 4)
        oa_ref[...] = a
        ob_ref[...] = b
        bias_ref[...] = far_ref[tall + 8 : tall + 9, :]

    @pl.when(pl.program_id(0) == 1)
    def _():
        a, b = put(far_ref, 0)
        oa_ref[...] += a
        ob_ref[...] += b


def last_step(idx, own, far, att, w_proj, after=()):
    rows, width = own.shape
    size = (rows - EXTRA) // 2
    out = pl.BlockSpec((size, width), lambda g, i: (i[1] ^ g, 0))
    return call(
        last_kernel,
        "last_step",
        (2,),
        [(idx, None)] + [(v, NEAR) for v in (own, far, att)] + [(w_proj, out)],
        [(shape(2 * size, width), out)] * 2 + [(shape(1, width), whole(1, width))] * 3,
        after=after,
        work=(1e12, 4e6),
        least=3 * 2**19,
        vmem=16,
    )


def make_step(dp_size):
    bits = [1 << k for k in range(dp_size.bit_length() - 1)]

    def on_device(
        features, adjacency, seed_counts, w_proj, w_skip, attn_src, attn_dst, bias, gamma, beta, cotangent
    ):
        nb, rows, src = adjacency.shape
        cols = features.shape[1]
        nb2 = nb // 2
        h = lax.axis_index("head")
        dpi = lax.axis_index("dp")
        core, side = h & 1, h >> 1
        def to_core(v):
            return lax.ppermute(v, "head", [(i, i ^ 1) for i in range(HEADS)])

        def to_cross(v):
            return lax.ppermute(v, "head", [(i, i ^ 2) for i in range(HEADS)])

        def to_dp(v, bit):
            return lax.ppermute(v, "dp", [(i, i ^ bit) for i in range(dp_size)])

        def half(v, which):
            size = v.shape[0] // 2
            return lax.dynamic_slice_in_dim(v, which * size, size, 0)

        ups = [(dpi >> k) & 1 for k in range(len(bits))]
        idx = jnp.stack([core, side, 1 - core, 1 - side] + ups).astype(jnp.int32)

        with jax.named_scope("fold_attention"):
            folded = jnp.stack(
                [jnp.sum(w_proj * attn_src, axis=1), jnp.sum(w_proj * attn_dst, axis=1)]
            )
            near_folded = to_core(folded)
            folded = jnp.stack([folded, near_folded])
            a_all = jnp.concatenate([folded, to_cross(folded)])
            a_all = a_all.transpose(1, 0, 2).reshape(2 * HEADS, -1)
            a_own = lax.dynamic_slice_in_dim(a_all, h * cols, cols, 1) * LOG2E

        with jax.named_scope("scores"):
            par = jnp.pad(jnp.stack([bias, gamma, beta]), ((0, 5), (0, 0)))
            par_sib = to_core(par)
            s_send, s_keep, x_send = scores(idx, features, a_own)
            s_mine = add_step(idx, s_keep, to_core(s_send))
            x_sib = to_core(relay(x_send, HBM, after=[s_mine]))
            s_cross = to_cross(s_mine)

        with jax.named_scope("share_weights"):
            halves, cot_send, w_own, mark = pack(idx, w_proj, w_skip, cotangent, after=[s_mine])
            w_far = to_cross(halves)
            cot_sib = to_core(cot_send)

        with jax.named_scope("forward"):
            far_fwd = forward_pair(
                1, idx, features, x_sib, adjacency, s_mine, s_cross, nb2, after=[par_sib, mark]
            )
            x_split, far_fwd = far_fwd[6:], far_fwd[:6]
            w_far = relay(w_far, HBM, after=[far_fwd[3]])
            far_weights = [(w_far,), (to_core(w_far),)]
            far_part = pre_pair(idx, *far_fwd[:2], x_split, far_weights, src, whole(nb2 * rows, 2 * HD))
            recv = to_cross(far_part)
            own_fwd = forward_pair(
                0, idx, *x_split, adjacency, s_mine, s_cross, nb2, after=[far_part]
            )
            own_weights = [(w_own,), (to_core(w_own),)]
            own_part = pre_pair(idx, *own_fwd[:2], x_split, own_weights, src, NEAR)

        with jax.named_scope("norm"):
            hold = [*x_split, *own_fwd[4:], *far_fwd[4:], own_fwd[0], far_fwd[0]]
            pre, stats, flipped = norm_sums(
                hold, idx, seed_counts, cotangent, cot_sib, par, par_sib, own_part, recv, nb2
            )
            stats = stats + to_core(flipped)
            for bit in bits:
                stats = stats + to_dp(stats, bit)
            act, act_send, d_own, small = norm_apply(
                hold, idx, seed_counts, pre, cotangent, cot_sib, par, par_sib, stats, nb2
            )
            act_recv = to_core(act_send)
            activations = lax.dynamic_update_slice_in_dim(
                act, act_recv, (1 - core) * nb2 * rows, 0
            )
            d_far = to_cross(d_own)

        token = [d_own]

        def note(out):
            token[:] = [out]
            return out

        flat = lambda v: v.reshape(2, 2 * cols, HD)
        backs, fars, theirs = [], [], []
        state = {}

        def scatter(send, keep, recv):
            for k, bit in enumerate(bits):
                send, keep = split_step(4 + k, idx, keep, recv, after=token)
                note(keep)
                recv = to_dp(send, bit)
                yield
            return keep, recv

        def gather(rows):
            for k, bit in reversed(list(enumerate(bits))):
                recv = to_dp(rows, bit)
                yield
                rows = note(join_step(4 + k, idx, rows, recv, after=token))
            return rows

        def own_chain(send, keep):
            keep, recv = yield from scatter(send, flat(keep), flat(to_core(send)))
            rows = note(end_step(idx, keep, recv, after=token))
            state["own"] = yield from gather(rows)

        def far_chain(send, keep):
            keep, recv = yield from scatter(send, flat(keep), flat(to_core(send)))
            while "flip" not in state:
                yield
            message, extra = swap_step(
                idx, keep, recv, state["q"], state["q_recv"], small, state["sums_recv"], after=token
            )
            note(extra)
            recv = to_cross(message)
            yield
            rows = note(enter_step(idx, recv, extra, after=token))
            state["far"] = yield from gather(rows)

        def advance(*chains):
            for c in chains:
                next(c, None)

        def back_far(b):
            fars.append(
                back_block(
                    b, 1, idx, x_split, far_fwd, d_far, far_weights, before=[backs[b][2]],
                    earlier=[f[2] for f in fars] if b == nb2 - 1 else (), after=token,
                )
            )
            note(fars[-1][2])

        half_cols = lambda i: lax.dynamic_slice_in_dim(a_all, i * cols, cols, 1)
        a_half = jnp.concatenate([half_cols(h), half_cols(h ^ 1)], axis=1)

        def features_of(b, part):
            state["gf"], other, mark = feature_block(
                b, part, idx, mixed[b], far_fwd[4:], fars[b][:2], ds, ds_cross, a_half, d_far,
                far_weights, features.shape, nb2,
                before=state.get("gf"), after=token,
            )
            note(mark)
            theirs.append(to_core(other))

        with jax.named_scope("backward"):
            state["sums_recv"] = to_core(small)
            send, keep = weight_pair(
                idx, x_split, own_fwd, d_own, src, after=token + [state["sums_recv"]]
            )
            note(keep)
            own = own_chain(send, keep)
            mixed = []
            for b in range(nb2):
                backs.append(
                    back_block(
                        b, 0, idx, x_split, own_fwd, d_own, own_weights, after=token + ([act_recv] if b else [])
                    )
                )
                note(backs[-1][2])
                if b == 0:
                    advance(own)
            for b in range(nb2):
                out, mark = mix_block(b, idx, own_fwd[4:], backs[b][:2], d_own, own_weights, after=token)
                note(mark)
                mixed.append(out)
            send, keep = weight_pair(idx, x_split, far_fwd, d_far, src, after=token)
            note(keep)
            advance(own)
            far = far_chain(relay(send, NEAR, after=token), keep)
            advance(far)
            for b in range(nb2):
                back_far(b)
                if b < nb2 - 1:
                    advance(own)
            advance(far, own)
            ds = relay(fars[-1][2], NEAR, after=token)
            ds_cross = to_cross(ds)
            state["q"], state["q_flip"] = thin_sums(idx, x_split, ds, ds_cross, after=token)
            note(state["q"])
            state["q_recv"] = to_core(state["q_flip"])
            state["flip"] = True
            advance(far, own)
            for b in range(nb2):
                for part in range(PARTS):
                    features_of(b, part)
                    advance(far)
                    if part == 1:
                        advance(own)
            grad_features, mark = place(idx, theirs, state["gf"], after=token)
            note(mark)
            for c in (own, far):
                for _ in c:
                    pass

        with jax.named_scope("last"):
            att = jnp.pad(jnp.stack([attn_src, attn_dst]), ((0, 6), (0, 0)))
            grad_proj, grad_skip, grad_src, grad_dst, grad_bias = last_step(
                idx, state["own"], state["far"], att, w_proj
            )

        return (
            activations,
            grad_features,
            grad_proj,
            grad_skip,
            grad_src[0],
            grad_dst[0],
            grad_bias[0],
            small[0, 0],
            small[0, 1],
        )

    return on_device


def solution(mesh):
    return jax.shard_map(
        make_step(mesh.shape["dp"]),
        mesh=mesh,
        in_specs=(
            P("dp", "head"),
            P("dp", None, None),
            P("dp"),
            P(None, "head"),
            P(None, "head"),
            P("head"),
            P("head"),
            P("head"),
            P("head"),
            P("head"),
            P("dp", "head"),
        ),
        out_specs=(
            P("dp", "head"),
            P("dp", "head"),
            P(None, "head"),
            P(None, "head"),
            P("head"),
            P("head"),
            P("head"),
            P("head"),
            P("head"),
        ),
        check_vma=False,
    )
```

```python
import functools

import jax
import jax.numpy as jnp
from jax import lax
from jax.experimental import pallas as pl
from jax.experimental.pallas import tpu as pltpu
from jax.sharding import PartitionSpec as P

HD = 256
HEADS = 4
TJ = 512
PARTS = 2
EXTRA = 16
eps = 1e-05
LOG2E = 1.4426950408889634
HALF_LN2 = 0.34657359027997264
F32 = jnp.float32
BF16 = jnp.bfloat16
NN = ((1,), (0,))
NT = ((1,), (1,))
TN = ((0,), (0,))
LOW = -3e38
HBM = pl.BlockSpec(memory_space=pltpu.HBM)
ANY = pl.BlockSpec(memory_space=pl.ANY)
NEAR = pl.BlockSpec(memory_space=pltpu.VMEM)


def dot(a, b, form):
    return lax.dot_general(a, b, (form, ((), ())), preferred_element_type=F32)


def split2(x):
    hi = x.astype(BF16)
    return hi, (x - hi.astype(F32)).astype(BF16)


def dot3(a, b, form):
    return dot(a[0], b[0], form) + (dot(a[0], b[1], form) + dot(a[1], b[0], form))


def cat3(a, axis, mixed):
    hi, lo = a
    return jnp.concatenate([hi, lo, hi] if mixed else [hi, hi, lo], axis=axis)


def thin_rows(d):
    hi = d.astype(BF16).astype(F32)
    return jnp.concatenate([hi, hi, d - hi, jnp.zeros_like(d)], axis=0).astype(BF16)


def thin_cols(a):
    hi = a.astype(BF16).astype(F32)
    return jnp.concatenate([hi, a - hi, hi, jnp.zeros_like(a)], axis=0).astype(BF16)


def lane_groups(v):
    out = v[:, :128]
    for k in range(128, v.shape[1], 128):
        out = out + v[:, k : k + 128]
    return out


def leaky2(u):
    soft = jnp.log2(1.0 + jnp.exp2(jnp.minimum(u, 126.0)))
    return jnp.maximum(u, 0.2 * u + 0.8 * soft)


def elu(v):
    return jnp.where(v > 0, v, jnp.exp(jnp.minimum(v, 0.0)) - 1.0)


def flip_rows(v, bit):
    return jnp.concatenate([v[m ^ bit : (m ^ bit) + 1] for m in range(8)], axis=0)


def large(v, least):
    return v.size * v.dtype.itemsize >= least


def held(v, spec, least):
    if spec is NEAR:
        return pltpu.with_memory_space_constraint(v, pltpu.VMEM)
    if spec is ANY:
        return v
    return pltpu.with_memory_space_constraint(v, pltpu.HBM) if large(v, least) else v


def result(v, spec, least):
    if spec is NEAR:
        return pltpu.VMEM(v.shape, v.dtype)
    return pltpu.HBM(v.shape, v.dtype) if large(v, least) else v


def call(kernel, name, grid, ins, outs, scratch=(), after=(), work=(1e6, 1e6), vmem=8, aliases=None, least=3 * 2**19, hold=()):
    n_in = len(ins)
    n_after = len(after) + len(hold)
    hold = [held(v, NEAR, least) for v in hold]
    scalars = 1 if ins[0][1] is None else 0
    ins = ins[:scalars] + [(held(v, spec, least), spec) for v, spec in ins[scalars:]]

    def body(*refs):
        kernel(*refs[:n_in], *refs[n_in + n_after :])

    return pl.pallas_call(
        body,
        grid_spec=pltpu.PrefetchScalarGridSpec(
            num_scalar_prefetch=scalars,
            grid=grid,
            in_specs=[s for _, s in ins[scalars:]] + [ANY] * len(after) + [NEAR] * len(hold),
            out_specs=[s for _, s in outs],
            scratch_shapes=list(scratch),
        ),
        out_shape=[result(v, spec, least) for v, spec in outs],
        compiler_params=pltpu.CompilerParams(
            dimension_semantics=("arbitrary",) * len(grid), vmem_limit_bytes=vmem * 2**20
        ),
        cost_estimate=pl.CostEstimate(
            flops=int(work[0]), bytes_accessed=int(work[1]), transcendentals=0
        ),
        input_output_aliases=aliases or {},
        name=name,
    )(*[v for v, _ in ins], *after, *hold)


class Place:
    def __getitem__(self, k):
        h = lax.axis_index("head")
        if k < 4:
            bit = (h & 1, h >> 1)[k % 2]
            return bit if k < 2 else 1 - bit
        return (lax.axis_index("dp") >> (k - 4)) & 1


def shape(*dims, dtype=F32):
    return jax.ShapeDtypeStruct(dims, dtype)


def whole(*dims):
    return pl.BlockSpec(dims, lambda *_: (0,) * len(dims))


def pack_kernel(n, idx_ref, *refs):
    for k in range(n):
        refs[n + k][...] = refs[k][...]
    refs[2 * n][...] = jnp.zeros_like(refs[2 * n])


def pack(idx, parts, after=()):
    ins, outs = [(idx, None)], []
    for v, which in parts:
        dims = (v.shape[0] // 2, v.shape[1])
        ins.append((v, pl.BlockSpec(dims, lambda g, i, which=which: (i[which], 0))))
        outs.append((shape(*dims), whole(*dims)))
    return call(
        functools.partial(pack_kernel, len(parts)),
        "pack",
        (1,),
        ins,
        outs + [(shape(8, 128), whole(8, 128))],
        after=after,
        work=(1e3, 1e5),
        least=2**18,
        vmem=16,
    )


def relay_kernel(v_ref, o_ref):
    o_ref[...] = v_ref[...]


def relay(v, spec, after=()):
    near = spec is NEAR
    return call(
        relay_kernel if near else lambda *_: None,
        "relay",
        (1,),
        [(v, spec)],
        [(shape(*v.shape), spec)],
        after=after,
        work=(1e3, 1e3),
        least=2**18,
        aliases=None if near else {0: 0},
    )[0]


def score_kernel(idx_ref, x_ref, a_ref, send_ref, keep_ref, copy_ref):
    x = x_ref[...]
    x1 = x.astype(BF16)
    rest = x - x1.astype(F32)
    x2 = rest.astype(BF16)
    x3 = (rest - x2.astype(F32)).astype(BF16)
    a = a_ref[...]
    a1 = a.astype(BF16).astype(F32)
    a2 = (a - a1).astype(BF16).astype(F32)
    a3 = (a - a1) - a2
    stack = jnp.concatenate([a1, a2, a3, jnp.zeros_like(a)], axis=0).astype(BF16)
    r1 = dot(stack, x1, NT)
    r2 = dot(stack[:16], x2, NT)
    r3 = dot(stack[:16], x3, NT)
    s = r1[:8] + (r1[8:16] + r2[:8]) + (r1[16:24] + r2[8:16] + r3[:8])

    @pl.when(pl.program_id(0) == 0)
    def _():
        send_ref[...] = flip_rows(s, 1)
        copy_ref[...] = x

    @pl.when(pl.program_id(0) == 1)
    def _():
        keep_ref[...] = s


def scores(idx, features, a_own, after=()):
    rows, cols = features.shape
    tile = 2048
    n = rows // 2 // tile
    return call(
        score_kernel,
        "scores",
        (2, n),
        [
            (idx, None),
            (features, pl.BlockSpec((tile, cols), lambda g, i, s: ((s[0] ^ 1 ^ g) * n + i, 0))),
            (a_own, whole(8, cols)),
        ],
        [
            (shape(8, rows // 2), pl.BlockSpec((8, tile), lambda g, i, s: (0, i * (1 - g) + (n - 1) * g))),
            (shape(8, rows // 2), pl.BlockSpec((8, tile), lambda g, i, s: (0, i * g))),
            (
                shape(rows // 2, cols),
                pl.BlockSpec((tile, cols), lambda g, i, s: (i * (1 - g) + (n - 1) * g, 0)),
            ),
        ],
        after=after,
        vmem=24,
        work=(1e12, 1e5),
    )


def forward_kernel(pair, idx_ref, adj_ref, sa_ref, sb_ref, xa_ref, xb_ref, *refs):
    first = pair == 1
    u_ref, linv_ref, tm_ref, s_ref, wh_ref, wl_ref = refs[:6]
    xh_ref, xl_ref = refs[6:8] if first else (xa_ref, xb_ref)
    rows, src = adj_ref.shape[1], adj_ref.shape[2]
    b = pl.program_id(0)
    nb2 = pl.num_programs(0)
    block = pl.ds(pl.multiple_of(b * src, src), src)

    def loads(blk):
        xbuf, sems = refs[8:]
        to = lax.rem(blk, 2)
        at = pl.ds(pl.multiple_of(blk * src, src), src)
        own = pl.ds(pl.multiple_of((idx_ref[0] * nb2 + blk) * src, src), src)
        return (
            pltpu.make_async_copy(xa_ref.at[own, :], xbuf.at[to, 0], sems.at[to, 0]),
            pltpu.make_async_copy(xb_ref.at[at, :], xbuf.at[to, 1], sems.at[to, 1]),
        )

    if first:

        @pl.when(b == 0)
        def _():
            for copy in loads(b):
                copy.start()

    s_all = sa_ref[:, block] + flip_rows(sb_ref[:, block], 2)
    s_ref[:, block] = s_all
    tm_ref[b, :, 0:8] = jnp.transpose(s_all[:, :rows])
    part = lambda m, k, n: s_ref[m : m + 1, pl.ds(pl.multiple_of(b * src + k, 128), n)]
    heads = (2 * pair, 2 * pair + 1)
    step = 64

    for r in range(0, rows, step):
        best = [jnp.full((step, 128), LOW, F32) for _ in heads]
        for k in range(0, src, 128):
            linked = adj_ref[0, r : r + step, k : k + 128] > 0
            for n, m in enumerate(heads):
                best[n] = jnp.maximum(best[n], jnp.where(linked, part(m, k, 128), LOW))
        for n, m in enumerate(heads):
            t = tm_ref[b, r : r + step, HEADS + m : HEADS + m + 1]
            top = leaky2(t + jnp.max(best[n], axis=1, keepdims=True))
            tm_ref[b, r : r + step, m : m + 1] = top

    for n in range(3):
        if n < 2:
            m = heads[n]
            for r in range(0, rows, 32):
                at = slice(r, r + 32)
                to = slice(n * rows + r, n * rows + r + 32)
                t = tm_ref[b, at, HEADS + m : HEADS + m + 1]
                top = tm_ref[b, at, m : m + 1]
                acc = None
                for k in range(0, src, 512):
                    ks = slice(k, k + 512)
                    q = leaky2(t + part(m, k, 512))
                    w = jnp.where(adj_ref[0, at, ks] > 0, jnp.exp2(q - top), 0.0)
                    hi, lo = split2(w)
                    wh_ref[b, to, ks] = hi
                    wl_ref[b, to, ks] = lo
                    acc = lane_groups(w) if acc is None else acc + lane_groups(w)
                linv = 1.0 / jnp.sum(acc, axis=1, keepdims=True)
                linv_ref[b, to, :] = jnp.broadcast_to(linv, (32, 128))
        if n == 0 and first:
            cols = xa_ref.shape[1]
            xbuf = refs[8]
            slot = lax.rem(b, 2)
            for copy in loads(b):
                copy.wait()

            @pl.when(b + 1 < nb2)
            def _():
                for copy in loads(b + 1):
                    copy.start()

            @pl.loop(0, src, step=256)
            def _(r):
                at = pl.ds(pl.multiple_of(b * src + r, 256), 256)
                for k in range(2):
                    hi, lo = split2(xbuf[slot, k, pl.ds(r, 256), :])
                    xh_ref[at, k * cols : (k + 1) * cols] = hi
                    xl_ref[at, k * cols : (k + 1) * cols] = lo

        if n > 0:
            at = slice((n - 1) * rows, n * rows)
            lhs = cat3((wh_ref[b, at, :], wl_ref[b, at, :]), 1, False)
            rhs = cat3((xh_ref[block, :], xl_ref[block, :]), 0, True)
            u_ref[b, at, :] = dot(lhs, rhs, NN)


def forward_pair(pair, idx, xa, xb, adjacency, s_mine, s_cross, nb2, after=()):
    rows, src = adjacency.shape[1:]
    first = pair == 1
    cols = xa.shape[1]
    kd = 2 * cols if first else cols
    two = 2 * rows
    outs = [
        shape(nb2, two, kd),
        shape(nb2, two, 128),
        shape(nb2, rows, 128),
        shape(8, nb2 * src),
        shape(nb2, two, src, dtype=BF16),
        shape(nb2, two, src, dtype=BF16),
    ]
    if first:
        outs += [shape(nb2 * src, kd, dtype=BF16)] * 2
    return call(
        functools.partial(forward_kernel, pair),
        "forward_pair",
        (nb2,),
        [
            (idx, None),
            (adjacency, pl.BlockSpec((1, rows, src), lambda b, i: (i[0] * nb2 + b, 0, 0))),
            (s_mine, NEAR),
            (s_cross, NEAR),
            (xa, HBM if first else NEAR),
            (xb, ANY if first else NEAR),
        ],
        [(v, NEAR) for v in outs],
        scratch=[pltpu.VMEM((2, 2, src, cols), F32), pltpu.SemaphoreType.DMA((2, 2))] if first else [],
        after=after,
        work=(1e12 if first else 1e8, 1e5),
        vmem=22 if first else 16,
    )


def rel_rows(piece, mat, idx_ref):
    core = idx_ref[0]
    ref = piece[mat]
    cols = ref.shape[0] // 2
    at = lambda k: pl.ds(pl.multiple_of(k * cols, cols), cols)
    return jnp.concatenate([ref[at(core), :], ref[at(core ^ 1), :]], axis=0)


def flat_weights(pieces):
    return [(v, NEAR) for p in pieces for v in p]


def take_weights(pieces, refs):
    out = []
    for p in pieces:
        out.append(refs[: len(p)])
        refs = refs[len(p) :]
    return out, refs


def pre_kernel(form, src, u_ref, linv_ref, xh_ref, xl_ref, *refs):
    idx_ref = Place()
    weights, (o_ref,) = take_weights(form, refs)
    nb2, two = u_ref.shape[:2]
    rows = two // 2
    stack = lambda parts: jnp.concatenate(list(parts), axis=0)
    tops = [slice(b * src, b * src + rows) for b in range(nb2)]
    x = (stack(xh_ref[t, :] for t in tops), stack(xl_ref[t, :] for t in tops))
    for a, piece in enumerate(weights):
        at = slice(a * rows, (a + 1) * rows)
        mixed = split2(stack(u_ref[b, at, :] * linv_ref[b, at, 0:1] for b in range(nb2)))
        lhs = jnp.concatenate([cat3(mixed, 1, False), cat3(x, 1, False)], axis=1)
        proj, skip = split2(rel_rows(piece, 0, idx_ref)), split2(rel_rows(piece, 1, idx_ref))
        rhs = jnp.concatenate([cat3(proj, 0, True), cat3(skip, 0, True)], axis=0)
        o_ref[:, a * HD : (a + 1) * HD] = dot(lhs, rhs, NN)


def pre_pair(idx, u, linv, x_split, weights, src, spec, after=()):
    nb2, two, kd = u.shape
    rows = two // 2
    return call(
        functools.partial(pre_kernel, weights, src),
        "pre_pair",
        (1,),
        [(u, NEAR), (linv, NEAR), (x_split[0], NEAR), (x_split[1], NEAR)] + flat_weights(weights),
        [(shape(nb2 * rows, 2 * HD), spec)],
        after=after,
        work=(1e8, 1e5),
        vmem=16,
    )[0]


def live_rows(idx_ref, counts_ref, nb2, rows):
    parts = []
    for b in range(nb2):
        row = lax.broadcasted_iota(jnp.int32, (rows, 1), 0)
        parts.append((row < counts_ref[idx_ref[0] * nb2 + b]).astype(F32))
    return jnp.concatenate(parts, axis=0)


def stats_kernel(nb2, idx_ref, counts_ref, ca_ref, cb_ref, pa_ref, pb_ref, part_ref, recv_ref, pre_ref, st_ref, flip_ref):
    rows = part_ref.shape[0] // nb2
    total = lambda v: jnp.sum(v, axis=0, keepdims=True)
    live = live_rows(idx_ref, counts_ref, nb2, rows)
    for a, (c_ref, p_ref) in enumerate(((ca_ref, pa_ref), (cb_ref, pb_ref))):
        cols = slice(a * HD, (a + 1) * HD)
        bias = p_ref[0:1, :]
        pre = part_ref[:, cols] + recv_ref[:, cols] + bias
        pre_ref[:, cols] = pre
        act = (elu(pre) - elu(bias)) * live
        g = c_ref[...] * live
        rows8 = [total(act), total(act * act), total(g), total(g * act)]
        rows8.append(jnp.broadcast_to(total(live), (1, HD)))
        rows8.append(jnp.zeros((3, HD), F32))
        stats = jnp.concatenate(rows8, axis=0)
        st_ref[a] = stats
        flip_ref[1 - a] = stats


def norm_sums(hold, idx, counts, cotangent, cot_sib, par, par_sib, part, recv, nb2):
    full = part.shape[0]
    return call(
        functools.partial(stats_kernel, nb2),
        "norm_sums",
        (1,),
        [
            (idx, None),
            (counts, pl.BlockSpec(memory_space=pltpu.SMEM)),
            (cotangent, pl.BlockSpec((full, HD), lambda g, i: (i[0], 0))),
            (cot_sib, whole(full, HD)),
            (par, whole(8, HD)),
            (par_sib, whole(8, HD)),
            (part, NEAR),
            (recv, whole(full, 2 * HD)),
        ],
        [
            (shape(full, 2 * HD), NEAR),
            (shape(2, 8, HD), whole(2, 8, HD)),
            (shape(2, 8, HD), whole(2, 8, HD)),
        ],
        work=(1e8, 1e5),
        least=3 * 2**19,
        hold=hold,
        vmem=14,
    )


def apply_kernel(
    nb2, idx_ref, counts_ref, pre_ref, ca_ref, cb_ref, pa_ref, pb_ref, st_ref, act_ref, send_ref, d_ref, o_ref
):
    rows = pre_ref.shape[0] // nb2
    live = live_rows(idx_ref, counts_ref, nb2, rows)
    for a, (c_ref, p_ref, out_ref) in enumerate(
        ((ca_ref, pa_ref, act_ref), (cb_ref, pb_ref, send_ref))
    ):
        cols = slice(a * HD, (a + 1) * HD)
        bias, gamma, beta = p_ref[0:1, :], p_ref[1:2, :], p_ref[2:3, :]
        count = st_ref[a, 4:5, :]
        mean = st_ref[a, 0:1, :] / count
        inv = lax.rsqrt(st_ref[a, 1:2, :] / count - mean * mean + eps)
        grad_beta = st_ref[a, 2:3, :]
        grad_gamma = inv * (st_ref[a, 3:4, :] - mean * grad_beta)
        pre = pre_ref[:, cols]
        nrm = (elu(pre) - elu(bias) - mean) * inv
        out_ref[...] = live * (gamma * nrm + beta)
        g = c_ref[...] * live
        d = live * (gamma * inv) * (g - grad_beta / count - nrm * (grad_gamma / count))
        d = d * jnp.exp(jnp.minimum(pre, 0.0))
        d_ref[:, cols] = d
        o_ref[a, 0:1, :] = grad_gamma
        o_ref[a, 1:2, :] = grad_beta
        o_ref[a, 2:3, :] = jnp.sum(d, axis=0, keepdims=True)
        o_ref[a, 3:8, :] = jnp.zeros((5, HD), F32)


def norm_apply(hold, idx, counts, pre, cotangent, cot_sib, par, par_sib, stats, nb2):
    full = pre.shape[0]
    return call(
        functools.partial(apply_kernel, nb2),
        "norm_apply",
        (1,),
        [
            (idx, None),
            (counts, pl.BlockSpec(memory_space=pltpu.SMEM)),
            (pre, NEAR),
            (cotangent, pl.BlockSpec((full, HD), lambda g, i: (i[0], 0))),
            (cot_sib, whole(full, HD)),
            (par, whole(8, HD)),
            (par_sib, whole(8, HD)),
            (stats, whole(2, 8, HD)),
        ],
        [
            (shape(2 * full, HD), pl.BlockSpec((full, HD), lambda g, i: (i[0], 0))),
            (shape(full, HD), whole(full, HD)),
            (shape(full, 2 * HD), NEAR),
            (shape(2, 8, HD), whole(2, 8, HD)),
        ],
        least=3 * 2**19,
        hold=hold,
        vmem=14,
        work=(1e8, 1e5),
    )


def back_kernel(
    blk, pair, form, prior, xh_ref, xl_ref, wh_ref, wl_ref, s_ref, tm_ref, d_ref, linv_ref, u_ref, *refs
):
    idx_ref = Place()
    weights, refs = take_weights(form, refs)
    before, refs = refs[:pair], refs[pair:]
    earlier, refs = refs[:prior], refs[prior:]
    vh_ref, vl_ref, ds_ref, dp, delta, tacc = refs
    rows = tm_ref.shape[1]
    src = wh_ref.shape[2]
    base = 8 * prior
    for n, v in enumerate(earlier):
        ds_ref[8 * n : 8 * n + 8, :] = v[...]
    ds_ref[base : base + 8, :] = before[0][...] if pair == 1 else jnp.zeros((8, src), F32)
    tacc[...] = jnp.zeros_like(tacc)
    for a, piece in enumerate(weights):
        at = slice(a * rows, (a + 1) * rows)
        linv = linv_ref[blk, at, :]
        d = split2(d_ref[blk * rows : (blk + 1) * rows, a * HD : (a + 1) * HD] * linv[:, 0:1])
        v = dot(cat3(d, 1, False), cat3(split2(rel_rows(piece, 0, idx_ref)), 1, True), NT)
        hi, lo = split2(v)
        vh_ref[at, :] = hi
        vl_ref[at, :] = lo
        delta[at, :] = jnp.sum(v * u_ref[blk, at, :], axis=1, keepdims=True) * linv
    width = dp.shape[1]
    for j in range(src // width):
        js = slice(j * width, (j + 1) * width)
        xs = slice(blk * src + j * width, blk * src + (j + 1) * width)
        x = (xh_ref[xs, :], xl_ref[xs, :])
        dp[...] = dot(cat3((vh_ref[...], vl_ref[...]), 1, False), cat3(x, 1, True), NT)
        for a in range(2):
            m = 2 * pair + a
            s = s_ref[m : m + 1, xs] * HALF_LN2
            total = None
            for r in range(0, rows, 32):
                at = slice(r, r + 32)
                ar = slice(a * rows + r, a * rows + r + 32)
                t = tm_ref[blk, at, HEADS + m : HEADS + m + 1] * HALF_LN2
                slope = 0.6 + 0.4 * jnp.tanh(t + s)
                w = wh_ref[blk, ar, js].astype(F32) + wl_ref[blk, ar, js].astype(F32)
                dv = (w * slope) * (dp[ar, :] - delta[ar, 0:1])
                tacc[ar, :] += lane_groups(dv)
                total = dv if total is None else total + dv
            ds_ref[base + m : base + m + 1, js] = jnp.sum(total, axis=0, keepdims=True)
    for a in range(2):
        m = HEADS + 2 * pair + a
        sums = jnp.sum(tacc[a * rows : (a + 1) * rows, :], axis=1, keepdims=True)
        turned = jnp.transpose(jnp.broadcast_to(sums, (rows, 128)))
        ds_ref[base + m : base + m + 1, 0:rows] = turned[0:1, :]


def back_block(blk, pair, idx, x_split, fwd, d, weights, before=(), earlier=(), after=()):
    u, linv, tm, s, wh, wl = fwd
    two, src = wh.shape[1:]
    kd = u.shape[2]
    tj = 2 * TJ
    arrays = [*x_split, wh, wl, s, tm, d, linv, u]
    rest = [*before, *earlier]
    return call(
        functools.partial(back_kernel, blk, pair, weights, len(earlier)),
        "back_block",
        (1,),
        [(v, NEAR) for v in arrays] + flat_weights(weights) + [(v, NEAR) for v in rest],
        [
            (shape(two, kd, dtype=BF16), NEAR),
            (shape(two, kd, dtype=BF16), NEAR),
            (shape(8 * len(earlier) + 8, src), NEAR),
        ],
        scratch=[pltpu.VMEM((two, tj), F32), pltpu.VMEM((two, 128), F32), pltpu.VMEM((two, 128), F32)],
        after=after,
        work=(1e8, 1e5),
        vmem=16,
    )


def weight_kernel(src, u_ref, linv_ref, d_ref, xh_ref, xl_ref, send_ref, keep_ref):
    idx_ref = Place()
    core = idx_ref[0]
    nb2, two = u_ref.shape[:2]
    rows = two // 2
    stack = lambda parts: jnp.concatenate(list(parts), axis=0)
    tops = [slice(b * src, b * src + rows) for b in range(nb2)]
    x = cat3((stack(xh_ref[t, :] for t in tops), stack(xl_ref[t, :] for t in tops)), 0, False)
    for a, ref in ((1, send_ref), (0, keep_ref)):
        at = slice(a * rows, (a + 1) * rows)
        d = d_ref[:, a * HD : (a + 1) * HD]
        u = split2(stack(u_ref[b, at, :] for b in range(nb2)))
        dn = split2(d * stack(linv_ref[b, at, 0:1] for b in range(nb2)))
        gp = dot(cat3(u, 0, False), cat3(dn, 0, True), TN)
        gs = dot(x, cat3(split2(d), 0, True), TN)
        cols = gp.shape[0] // 2
        for mat, g in enumerate((gp, gs)):
            ref[mat, core] = g[:cols]
            ref[mat, core ^ 1] = g[cols:]


def weight_pair(idx, x_split, fwd, d, src, after=()):
    u, linv = fwd[:2]
    cols = u.shape[2] // 2
    arrays = [u, linv, d, *x_split]
    out = shape(2, 2, cols, HD)
    return call(
        functools.partial(weight_kernel, src),
        "weight_pair",
        (1,),
        [(v, NEAR) for v in arrays],
        [(out, NEAR), (out, NEAR)],
        after=after,
        work=(1e8, 1e5),
        vmem=16,
    )


def thin_kernel(xh_ref, xl_ref, da_ref, db_ref, o_ref, flip_ref):
    idx_ref = Place()
    core = idx_ref[0]
    cols = xh_ref.shape[1] // 2
    nb2, src = da_ref.shape[0] // 8, da_ref.shape[1]
    total = None
    for b in range(nb2):
        rows8 = slice(8 * b, 8 * b + 8)
        d = da_ref[rows8, :] + flip_rows(db_ref[rows8, :], 2)
        hi = d.astype(BF16).astype(F32)
        stack = jnp.concatenate([hi, d - hi], axis=0).astype(BF16)
        at = slice(b * src, (b + 1) * src)
        r1 = dot(stack, xh_ref[at, :], NN)
        r2 = dot(stack, xl_ref[at, :], NN)
        q = r1[:8] + (r1[8:] + r2[:8])
        total = q if total is None else total + q
    for k, q in enumerate((total[:, :cols], total[:, cols:])):
        o_ref[core ^ k] = q
        flip_ref[core ^ k] = flip_rows(q, 1)


def thin_sums(idx, x_split, ds, ds_cross, after=()):
    cols = x_split[0].shape[1] // 2
    return call(
        thin_kernel,
        "thin_sums",
        (1,),
        [(x_split[0], NEAR), (x_split[1], NEAR), (ds, NEAR), (ds_cross, NEAR)],
        [(shape(2, 8, cols), NEAR)] * 2,
        after=after,
        work=(1e8, 1e5),
        vmem=14,
    )


def skip_back(at, d_ref, weights, idx_ref):
    pair = [split2(rel_rows(piece, 1, idx_ref)) for piece in weights]
    both = [jnp.concatenate([p[n] for p in pair], axis=1) for n in range(2)]
    return dot(cat3(split2(d_ref[at, :]), 1, False), cat3(both, 1, True), NT)


def mix_kernel(blk, form, wh, wl, vh, vl, d_ref, *refs):
    idx_ref = Place()
    weights, (o_ref, mark_ref) = take_weights(form, refs)
    mark_ref[...] = jnp.zeros_like(mark_ref)
    j = pl.program_id(0)
    rows = vh.shape[0] // 2
    js = pl.ds(pl.multiple_of(j * TJ, TJ), TJ)
    rhs = cat3((vh[...], vl[...]), 0, True)
    o_ref[...] = dot(cat3((wh[blk, :, js], wl[blk, :, js]), 0, False), rhs, TN)

    @pl.when(j == 0)
    def _():
        o_ref[0:rows, :] += skip_back(slice(blk * rows, (blk + 1) * rows), d_ref, weights, idx_ref)


def mix_block(blk, idx, w, v, d, weights, after=()):
    src = w[0].shape[2]
    kd = v[0].shape[1]
    return call(
        functools.partial(mix_kernel, blk, weights),
        "mix_block",
        (src // TJ,),
        [(a, NEAR) for a in (*w, *v, d)] + flat_weights(weights),
        [(shape(src, kd), pl.BlockSpec((TJ, kd), lambda j: (j, 0))), (shape(8, 128), whole(8, 128))],
        after=after,
        work=(1e8, 1e5),
        vmem=16,
    )


def feature_kernel(blk, part, form, idx_ref, g_ref, wh, wl, vh, vl, da_ref, db_ref, a_ref, d_ref, *refs):
    weights, refs = take_weights(form, refs)
    oo_ref, os_ref, mark_ref = refs[-3:]
    j = pl.program_id(0)
    mark_ref[...] = jnp.zeros_like(mark_ref)
    half = oo_ref.shape[1]
    rows = vh.shape[0] // 2
    js = pl.ds(pl.multiple_of((part * pl.num_programs(0) + j) * TJ, TJ), TJ)
    rows8 = slice(8 * blk, 8 * blk + 8)
    d = da_ref[rows8, js] + flip_rows(db_ref[rows8, js], 2)
    out = dot(cat3((wh[blk, :, js], wl[blk, :, js]), 0, False), cat3((vh[...], vl[...]), 0, True), TN)
    out = out + (g_ref[...] + dot(thin_rows(d), thin_cols(a_ref[...]), TN))
    oo_ref[...] = out[:, :half]
    os_ref[...] = out[:, half:]
    if part == 0:

        @pl.when(j == 0)
        def _():
            more = skip_back(slice(blk * rows, (blk + 1) * rows), d_ref, weights, idx_ref)
            oo_ref[0:rows, :] += more[:, :half]
            os_ref[0:rows, :] += more[:, half:]


def feature_block(
    blk, part, idx, mixed, w, v, ds, ds_cross, a_half, d, weights, full, nb2, before, after=()
):
    src = w[0].shape[2]
    kd = v[0].shape[1]
    half = kd // 2
    nj = src // TJ
    count = nj // PARTS
    first = part * count
    ins = [(idx, None), (mixed, pl.BlockSpec((TJ, kd), lambda j, i: (first + j, 0)))]
    ins += [(a, NEAR) for a in (*w, *v)]
    ins += [(ds, NEAR), (ds_cross, NEAR), (a_half, NEAR), (d, NEAR)]
    ins += flat_weights(weights)
    aliases = {}
    if before is not None:
        aliases[len(ins)] = 0
        ins.append((before, HBM))
    return call(
        functools.partial(feature_kernel, blk, part, weights),
        "feature_block",
        (count,),
        ins,
        [
            (shape(*full), pl.BlockSpec((TJ, half), lambda j, i: ((i[0] * nb2 + blk) * nj + first + j, 0))),
            (shape(src // PARTS, half), pl.BlockSpec((TJ, half), lambda j, i: (j, 0))),
            (shape(8, 128), whole(8, 128)),
        ],
        after=after,
        work=(6.4e9, 1e5),
        vmem=18,
        aliases=aliases,
    )


def place_kernel(nb2, idx_ref, *refs):
    parts, (out_ref, mark_ref, buf, sems) = refs[:nb2], refs[nb2 + 1 :]
    mark_ref[...] = jnp.zeros_like(mark_ref)
    src = parts[0].shape[0]
    size = buf.shape[1]
    n = src // size

    def load(b, k):
        return pltpu.make_async_copy(parts[b].at[pl.ds(k * size, size), :], buf.at[b * n + k], sems.at[0, b * n + k])

    def store(b, k):
        at = pl.multiple_of((idx_ref[2] * nb2 + b) * src + k * size, size)
        return pltpu.make_async_copy(buf.at[b * n + k], out_ref.at[pl.ds(at, size), :], sems.at[1, b * n + k])

    every = [(b, k) for b in range(nb2) for k in range(n)]
    for b, k in every:
        load(b, k).start()
    for b, k in every:
        load(b, k).wait()
        store(b, k).start()
    for b, k in every:
        store(b, k).wait()


def place(idx, parts, before, after=()):
    nb2 = len(parts)
    src, half = parts[0].shape
    count = nb2 * src // TJ
    return call(
        functools.partial(place_kernel, nb2),
        "place",
        (1,),
        [(idx, None)] + [(v, HBM) for v in parts] + [(before, HBM)],
        [(shape(*before.shape), HBM), (shape(8, 128), whole(8, 128))],
        scratch=[pltpu.VMEM((count, TJ, half), F32), pltpu.SemaphoreType.DMA((2, count))],
        after=after,
        work=(1e3, 1e6),
        least=2**18,
        vmem=14,
        aliases={1 + nb2: 0},
    )


def split_kernel(at, keep_ref, recv_ref, send_ref, next_ref):
    idx_ref = Place()
    size = next_ref.shape[1]
    mine = pl.ds(pl.multiple_of(idx_ref[at] * size, size), size)
    other = pl.ds(pl.multiple_of((1 - idx_ref[at]) * size, size), size)
    send_ref[...] = keep_ref[:, other, :] + recv_ref[:, other, :]
    next_ref[...] = keep_ref[:, mine, :] + recv_ref[:, mine, :]


def split_step(at, idx, keep, recv, after=()):
    n, rows, cols = keep.shape
    part = (n, rows // 2, cols)
    return call(
        functools.partial(split_kernel, at),
        "split_step",
        (1,),
        [(keep, NEAR), (recv, NEAR)],
        [(shape(*part), NEAR)] * 2,
        after=after,
        work=(1e3, keep.size * 8),
        vmem=8,
    )


def add_kernel(a_ref, b_ref, o_ref):
    o_ref[...] = a_ref[...] + b_ref[...]


def add_step(idx, a, b, after=()):
    return call(
        add_kernel,
        "add_step",
        (1,),
        [(a, NEAR), (b, NEAR)],
        [(shape(*a.shape), NEAR)],
        after=after,
        least=3 * 2**19,
        vmem=8,
        work=(1e3, a.size * 8),
    )[0]


def join_kernel(at, mine_ref, recv_ref, o_ref):
    idx_ref = Place()
    size = (mine_ref.shape[0] - EXTRA) // 2
    for mat in range(2):
        old = slice(mat * size, (mat + 1) * size)
        put = lambda up: pl.ds(pl.multiple_of(2 * mat * size + up * size, size), size)
        o_ref[put(idx_ref[at]), :] = mine_ref[old, :]
        o_ref[put(1 - idx_ref[at]), :] = recv_ref[old, :]
    o_ref[4 * size :, :] = mine_ref[2 * size :, :] + recv_ref[2 * size :, :]


def join_step(at, idx, mine, recv, after=()):
    rows, cols = mine.shape
    full = 2 * (rows - EXTRA) + EXTRA
    return call(
        functools.partial(join_kernel, at),
        "join_step",
        (1,),
        [(mine, NEAR), (recv, NEAR)],
        [(shape(full, cols), NEAR)],
        after=after,
        work=(1e3, mine.size * 16),
        least=3 * 2**19,
        vmem=10,
    )[0]


def end_kernel(keep_ref, recv_ref, o_ref):
    size = keep_ref.shape[1]
    for mat in range(2):
        o_ref[mat * size : (mat + 1) * size, :] = keep_ref[mat] + recv_ref[mat]
    o_ref[2 * size :, :] = jnp.zeros((EXTRA, o_ref.shape[1]), F32)


def end_step(idx, keep, recv, after=()):
    n, rows, cols = keep.shape
    full = n * rows + EXTRA
    return call(
        end_kernel,
        "end_step",
        (1,),
        [(keep, NEAR), (recv, NEAR)],
        [(shape(full, cols), NEAR)],
        after=after,
        work=(1e3, keep.size * 8),
        least=3 * 2**19,
        vmem=8,
    )[0]


def swap_kernel(keep_ref, recv_ref, q_ref, qr_ref, b_ref, br_ref, o_ref, extra_ref):
    size = keep_ref.shape[1]
    for mat in range(2):
        o_ref[mat * size : (mat + 1) * size, :] = keep_ref[mat] + recv_ref[mat]
    q = q_ref[...] + qr_ref[...]
    width = o_ref.shape[1]
    pick = lambda m: [q[k, n : n + 1, :] for k in range(2) for n in (m, HEADS + m)]
    zero = lambda n: [jnp.zeros((n, width), F32)]
    o_ref[2 * size :, :] = jnp.concatenate(pick(2) + zero(EXTRA - 4), axis=0)
    bias = b_ref[0, 2:3, :] + br_ref[1, 2:3, :]
    extra_ref[...] = jnp.concatenate(zero(4) + pick(0) + [bias] + zero(EXTRA - 9), axis=0)


def swap_step(idx, keep, recv, q, q_recv, sums, sums_recv, after=()):
    n, rows, cols = keep.shape
    full = n * rows + EXTRA
    arrays = [keep, recv, q, q_recv, sums, sums_recv]
    return call(
        swap_kernel,
        "swap_step",
        (1,),
        [(v, NEAR) for v in arrays],
        [(shape(full, cols), NEAR), (shape(EXTRA, cols), NEAR)],
        after=after,
        work=(1e3, keep.size * 8),
        least=3 * 2**19,
        vmem=8,
    )


def enter_kernel(recv_ref, extra_ref, o_ref):
    rows = recv_ref.shape[0] - EXTRA
    o_ref[:rows, :] = recv_ref[:rows, :]
    o_ref[rows:, :] = recv_ref[rows:, :] + extra_ref[...]


def enter_step(idx, recv, extra, after=()):
    return call(
        enter_kernel,
        "enter_step",
        (1,),
        [(recv, NEAR), (extra, NEAR)],
        [(shape(*recv.shape), NEAR)],
        after=after,
        work=(1e3, recv.size * 8),
        least=3 * 2**19,
        vmem=8,
    )[0]


def last_kernel(idx_ref, own_ref, far_ref, att_ref, w_ref, op_ref, os_ref, oa_ref, ob_ref, bias_ref):
    tall = own_ref.shape[0] - EXTRA
    size = tall // 2

    def put(g_ref, first):
        total = None
        for k in range(2):
            at = slice(k * size // 2, (k + 1) * size // 2)
            q = far_ref[tall + first + 2 * k : tall + first + 2 * k + 2, :]
            q = jnp.concatenate([q, jnp.zeros((6, q.shape[1]), F32)], axis=0)
            op_ref[at, :] = g_ref[at, :] + dot(thin_rows(q), thin_cols(att_ref[...]), TN)
            hi = q.astype(BF16).astype(F32)
            stack = jnp.concatenate([hi, q - hi], axis=0).astype(BF16)
            wh, wl = split2(w_ref[at, :])
            r1, r2 = dot(stack, wh, NN), dot(stack, wl, NN)
            new = r1[:8] + (r1[8:] + r2[:8])
            total = new if total is None else total + new
        os_ref[...] = g_ref[size:tall, :]
        return total[0:1], total[1:2]

    @pl.when(pl.program_id(0) == 0)
    def _():
        a, b = put(own_ref, 4)
        oa_ref[...] = a
        ob_ref[...] = b
        bias_ref[...] = far_ref[tall + 8 : tall + 9, :]

    @pl.when(pl.program_id(0) == 1)
    def _():
        a, b = put(far_ref, 0)
        oa_ref[...] += a
        ob_ref[...] += b


def last_step(idx, own, far, att, w_proj, after=()):
    rows, width = own.shape
    size = (rows - EXTRA) // 2
    out = pl.BlockSpec((size, width), lambda g, i: (i[1] ^ g, 0))
    return call(
        last_kernel,
        "last_step",
        (2,),
        [(idx, None)] + [(v, NEAR) for v in (own, far, att)] + [(w_proj, out)],
        [(shape(2 * size, width), out)] * 2 + [(shape(1, width), whole(1, width))] * 3,
        after=after,
        work=(1e12, 4e6),
        least=3 * 2**19,
        vmem=16,
    )


def make_step(dp_size):
    bits = [1 << k for k in range(dp_size.bit_length() - 1)]

    def on_device(
        features, adjacency, seed_counts, w_proj, w_skip, attn_src, attn_dst, bias, gamma, beta, cotangent
    ):
        nb, rows, src = adjacency.shape
        cols = features.shape[1]
        nb2 = nb // 2
        h = lax.axis_index("head")
        dpi = lax.axis_index("dp")
        core, side = h & 1, h >> 1
        def to_core(v):
            return lax.ppermute(v, "head", [(i, i ^ 1) for i in range(HEADS)])

        def to_cross(v):
            return lax.ppermute(v, "head", [(i, i ^ 2) for i in range(HEADS)])

        def to_dp(v, bit):
            return lax.ppermute(v, "dp", [(i, i ^ bit) for i in range(dp_size)])

        def half(v, which):
            size = v.shape[0] // 2
            return lax.dynamic_slice_in_dim(v, which * size, size, 0)

        ups = [(dpi >> k) & 1 for k in range(len(bits))]
        idx = jnp.stack([core, side, 1 - core, 1 - side] + ups).astype(jnp.int32)

        with jax.named_scope("fold_attention"):
            folded = jnp.stack(
                [jnp.sum(w_proj * attn_src, axis=1), jnp.sum(w_proj * attn_dst, axis=1)]
            )
            near_folded = to_core(folded)
            folded = jnp.stack([folded, near_folded])
            a_all = jnp.concatenate([folded, to_cross(folded)])
            a_all = a_all.transpose(1, 0, 2).reshape(2 * HEADS, -1)
            a_own = lax.dynamic_slice_in_dim(a_all, h * cols, cols, 1) * LOG2E

        with jax.named_scope("scores"):
            par = jnp.pad(jnp.stack([bias, gamma, beta]), ((0, 5), (0, 0)))
            par_sib = to_core(par)
            proj_half, mark = pack(idx, [(w_proj, 3)], after=[near_folded])
            proj_far = to_cross(proj_half)
            s_send, s_keep, x_send = scores(idx, features, a_own, after=[mark])
            s_mine = add_step(idx, s_keep, to_core(s_send), after=[proj_far])
            x_sib = to_core(relay(x_send, HBM, after=[s_mine]))
            s_cross = to_cross(s_mine)

        with jax.named_scope("share_weights"):
            skip_half, cot_send, proj_own, skip_own, mark = pack(
                idx, [(w_skip, 3), (cotangent, 2), (w_proj, 1), (w_skip, 1)], after=[s_mine]
            )
            skip_far = to_cross(skip_half)
            cot_sib = to_core(cot_send)

        with jax.named_scope("forward"):
            far_fwd = forward_pair(
                1, idx, features, x_sib, adjacency, s_mine, s_cross, nb2, after=[par_sib, mark]
            )
            x_split, far_fwd = far_fwd[6:], far_fwd[:6]
            skip_far = relay(skip_far, HBM, after=[far_fwd[3]])
            far_weights = [(proj_far, skip_far), (to_core(proj_far), to_core(skip_far))]
            far_part = pre_pair(idx, *far_fwd[:2], x_split, far_weights, src, whole(nb2 * rows, 2 * HD))
            recv = to_cross(far_part)
            own_fwd = forward_pair(0, idx, *x_split, adjacency, s_mine, s_cross, nb2, after=[far_part])
            own_weights = [(proj_own, skip_own), (to_core(proj_own), to_core(skip_own))]
            own_part = pre_pair(idx, *own_fwd[:2], x_split, own_weights, src, NEAR)

        with jax.named_scope("norm"):
            hold = [*x_split, *own_fwd[4:], *far_fwd[4:], own_fwd[0], far_fwd[0]]
            pre, stats, flipped = norm_sums(
                hold, idx, seed_counts, cotangent, cot_sib, par, par_sib, own_part, recv, nb2
            )
            stats = stats + to_core(flipped)
            for bit in bits:
                stats = stats + to_dp(stats, bit)
            act, act_send, d_own, small = norm_apply(
                hold, idx, seed_counts, pre, cotangent, cot_sib, par, par_sib, stats, nb2
            )
            act_recv = to_core(act_send)
            activations = lax.dynamic_update_slice_in_dim(
                act, act_recv, (1 - core) * nb2 * rows, 0
            )
            d_far = to_cross(d_own)

        token = [d_own]

        def note(out):
            token[:] = [out]
            return out

        flat = lambda v: v.reshape(2, 2 * cols, HD)
        backs, fars, theirs = [], [], []
        state = {}

        def scatter(send, keep, recv):
            for k, bit in enumerate(bits):
                send, keep = split_step(4 + k, idx, keep, recv, after=token)
                note(keep)
                recv = to_dp(send, bit)
                yield
            return keep, recv

        def gather(rows):
            for k, bit in reversed(list(enumerate(bits))):
                recv = to_dp(rows, bit)
                yield
                rows = note(join_step(4 + k, idx, rows, recv, after=token))
            return rows

        def own_chain(send, keep):
            keep, recv = yield from scatter(send, flat(keep), flat(to_core(send)))
            rows = note(end_step(idx, keep, recv, after=token))
            state["own"] = yield from gather(rows)

        def far_chain(send, keep):
            keep, recv = yield from scatter(send, flat(keep), flat(to_core(send)))
            while "flip" not in state:
                yield
            message, extra = swap_step(
                idx, keep, recv, state["q"], state["q_recv"], small, state["sums_recv"], after=token
            )
            note(extra)
            recv = to_cross(message)
            yield
            rows = note(enter_step(idx, recv, extra, after=token))
            state["far"] = yield from gather(rows)

        def advance(*chains):
            for c in chains:
                next(c, None)

        def back_far(b):
            fars.append(
                back_block(
                    b, 1, idx, x_split, far_fwd, d_far, far_weights, before=[backs[b][2]],
                    earlier=[f[2] for f in fars] if b == nb2 - 1 else (), after=token,
                )
            )
            note(fars[-1][2])

        half_cols = lambda i: lax.dynamic_slice_in_dim(a_all, i * cols, cols, 1)
        a_half = jnp.concatenate([half_cols(h), half_cols(h ^ 1)], axis=1)

        def features_of(b, part):
            state["gf"], other, mark = feature_block(
                b, part, idx, mixed[b], far_fwd[4:], fars[b][:2], ds, ds_cross, a_half, d_far,
                far_weights, features.shape, nb2,
                before=state.get("gf"), after=token,
            )
            note(mark)
            theirs.append(to_core(other))

        with jax.named_scope("backward"):
            state["sums_recv"] = to_core(small)
            send, keep = weight_pair(
                idx, x_split, own_fwd, d_own, src, after=token + [state["sums_recv"]]
            )
            note(keep)
            own = own_chain(send, keep)
            mixed = []
            for b in range(nb2):
                backs.append(
                    back_block(
                        b, 0, idx, x_split, own_fwd, d_own, own_weights, after=token + ([act_recv] if b else [])
                    )
                )
                note(backs[-1][2])
                if b == 0:
                    advance(own)
            for b in range(nb2):
                out, mark = mix_block(b, idx, own_fwd[4:], backs[b][:2], d_own, own_weights, after=token)
                note(mark)
                mixed.append(out)
            send, keep = weight_pair(idx, x_split, far_fwd, d_far, src, after=token)
            note(keep)
            advance(own)
            far = far_chain(relay(send, NEAR, after=token), keep)
            advance(far)
            for b in range(nb2):
                back_far(b)
                if b < nb2 - 1:
                    advance(own)
            advance(far, own)
            ds = relay(fars[-1][2], NEAR, after=token)
            ds_cross = to_cross(ds)
            state["q"], state["q_flip"] = thin_sums(idx, x_split, ds, ds_cross, after=token)
            note(state["q"])
            state["q_recv"] = to_core(state["q_flip"])
            state["flip"] = True
            advance(far, own)
            for b in range(nb2):
                for part in range(PARTS):
                    features_of(b, part)
                    advance(far)
                    if part == 1:
                        advance(own)
            grad_features, mark = place(idx, theirs, state["gf"], after=token)
            note(mark)
            for c in (own, far):
                for _ in c:
                    pass

        with jax.named_scope("last"):
            att = jnp.pad(jnp.stack([attn_src, attn_dst]), ((0, 6), (0, 0)))
            grad_proj, grad_skip, grad_src, grad_dst, grad_bias = last_step(
                idx, state["own"], state["far"], att, w_proj
            )

        return (
            activations,
            grad_features,
            grad_proj,
            grad_skip,
            grad_src[0],
            grad_dst[0],
            grad_bias[0],
            small[0, 0],
            small[0, 1],
        )

    return on_device


def solution(mesh):
    return jax.shard_map(
        make_step(mesh.shape["dp"]),
        mesh=mesh,
        in_specs=(
            P("dp", "head"),
            P("dp", None, None),
            P("dp"),
            P(None, "head"),
            P(None, "head"),
            P("head"),
            P("head"),
            P("head"),
            P("head"),
            P("head"),
            P("dp", "head"),
        ),
        out_specs=(
            P("dp", "head"),
            P("dp", "head"),
            P(None, "head"),
            P(None, "head"),
            P("head"),
            P("head"),
            P("head"),
            P("head"),
            P("head"),
        ),
        check_vma=False,
    )
```

```python
import functools

import jax
import jax.numpy as jnp
from jax import lax
from jax.experimental import pallas as pl
from jax.experimental.pallas import tpu as pltpu
from jax.sharding import PartitionSpec as P

HD = 256
HEADS = 4
TJ = 512
PARTS = 2
EXTRA = 16
eps = 1e-05
LOG2E = 1.4426950408889634
HALF_LN2 = 0.34657359027997264
F32 = jnp.float32
BF16 = jnp.bfloat16
NN = ((1,), (0,))
NT = ((1,), (1,))
TN = ((0,), (0,))
LOW = -3e38
HBM = pl.BlockSpec(memory_space=pltpu.HBM)
ANY = pl.BlockSpec(memory_space=pl.ANY)
NEAR = pl.BlockSpec(memory_space=pltpu.VMEM)


def dot(a, b, form):
    return lax.dot_general(a, b, (form, ((), ())), preferred_element_type=F32)


def split2(x):
    hi = x.astype(BF16)
    return hi, (x - hi.astype(F32)).astype(BF16)


def dot3(a, b, form):
    return dot(a[0], b[0], form) + (dot(a[0], b[1], form) + dot(a[1], b[0], form))


def cat3(a, axis, mixed):
    hi, lo = a
    return jnp.concatenate([hi, lo, hi] if mixed else [hi, hi, lo], axis=axis)


def thin_rows(d):
    hi = d.astype(BF16).astype(F32)
    return jnp.concatenate([hi, hi, d - hi, jnp.zeros_like(d)], axis=0).astype(BF16)


def thin_cols(a):
    hi = a.astype(BF16).astype(F32)
    return jnp.concatenate([hi, a - hi, hi, jnp.zeros_like(a)], axis=0).astype(BF16)


def lane_groups(v):
    out = v[:, :128]
    for k in range(128, v.shape[1], 128):
        out = out + v[:, k : k + 128]
    return out


def leaky2(u):
    soft = jnp.log2(1.0 + jnp.exp2(jnp.minimum(u, 126.0)))
    return jnp.maximum(u, 0.2 * u + 0.8 * soft)


def elu(v):
    return jnp.where(v > 0, v, jnp.exp(jnp.minimum(v, 0.0)) - 1.0)


def flip_rows(v, bit):
    return jnp.concatenate([v[m ^ bit : (m ^ bit) + 1] for m in range(8)], axis=0)


def large(v, least):
    return v.size * v.dtype.itemsize >= least


def held(v, spec, least):
    if spec is NEAR:
        return pltpu.with_memory_space_constraint(v, pltpu.VMEM)
    if spec is ANY:
        return v
    return pltpu.with_memory_space_constraint(v, pltpu.HBM) if large(v, least) else v


def result(v, spec, least):
    if spec is NEAR:
        return pltpu.VMEM(v.shape, v.dtype)
    return pltpu.HBM(v.shape, v.dtype) if large(v, least) else v


def call(kernel, name, grid, ins, outs, scratch=(), after=(), work=(1e6, 1e6), vmem=8, aliases=None, least=3 * 2**19, hold=()):
    n_in = len(ins)
    hold = [held(v.v, NEAR, least) for v in after if isinstance(v, Held)] + [held(v, NEAR, least) for v in hold]
    after = [v for v in after if not isinstance(v, Held)]
    n_after = len(after) + len(hold)
    scalars = 1 if ins[0][1] is None else 0
    ins = ins[:scalars] + [(held(v, spec, least), spec) for v, spec in ins[scalars:]]

    def body(*refs):
        kernel(*refs[:n_in], *refs[n_in + n_after :])

    return pl.pallas_call(
        body,
        grid_spec=pltpu.PrefetchScalarGridSpec(
            num_scalar_prefetch=scalars,
            grid=grid,
            in_specs=[s for _, s in ins[scalars:]] + [ANY] * len(after) + [NEAR] * len(hold),
            out_specs=[s for _, s in outs],
            scratch_shapes=list(scratch),
        ),
        out_shape=[result(v, spec, least) for v, spec in outs],
        compiler_params=pltpu.CompilerParams(
            dimension_semantics=("arbitrary",) * len(grid), vmem_limit_bytes=vmem * 2**20
        ),
        cost_estimate=pl.CostEstimate(
            flops=int(work[0]), bytes_accessed=int(work[1]), transcendentals=0
        ),
        input_output_aliases=aliases or {},
        name=name,
    )(*[v for v, _ in ins], *after, *hold)


class Held:
    def __init__(self, v):
        self.v = v


class Place:
    def __getitem__(self, k):
        h = lax.axis_index("head")
        if k < 4:
            bit = (h & 1, h >> 1)[k % 2]
            return bit if k < 2 else 1 - bit
        return (lax.axis_index("dp") >> (k - 4)) & 1


def shape(*dims, dtype=F32):
    return jax.ShapeDtypeStruct(dims, dtype)


def whole(*dims):
    return pl.BlockSpec(dims, lambda *_: (0,) * len(dims))


def pack_kernel(n, idx_ref, *refs):
    for k in range(n):
        refs[n + k][...] = refs[k][...]
    refs[2 * n][...] = jnp.zeros_like(refs[2 * n])


def pack(idx, parts, after=()):
    ins, outs = [(idx, None)], []
    for v, which in parts:
        dims = (v.shape[0] // 2, v.shape[1])
        ins.append((v, pl.BlockSpec(dims, lambda g, i, which=which: (i[which], 0))))
        outs.append((shape(*dims), whole(*dims)))
    return call(
        functools.partial(pack_kernel, len(parts)),
        "pack",
        (1,),
        ins,
        outs + [(shape(8, 128), whole(8, 128))],
        after=after,
        work=(1e3, 1e5),
        least=2**18,
        vmem=16,
    )


def relay_kernel(v_ref, o_ref):
    o_ref[...] = v_ref[...]


def relay(v, spec, after=()):
    near = spec is NEAR
    return call(
        relay_kernel if near else lambda *_: None,
        "relay",
        (1,),
        [(v, spec)],
        [(shape(*v.shape), spec)],
        after=after,
        work=(1e3, 1e3),
        least=2**18,
        aliases=None if near else {0: 0},
    )[0]


def score_kernel(idx_ref, x_ref, a_ref, send_ref, keep_ref, copy_ref):
    x = x_ref[...]
    x1 = x.astype(BF16)
    rest = x - x1.astype(F32)
    x2 = rest.astype(BF16)
    x3 = (rest - x2.astype(F32)).astype(BF16)
    a = a_ref[...]
    a1 = a.astype(BF16).astype(F32)
    a2 = (a - a1).astype(BF16).astype(F32)
    a3 = (a - a1) - a2
    stack = jnp.concatenate([a1, a2, a3, jnp.zeros_like(a)], axis=0).astype(BF16)
    r1 = dot(stack, x1, NT)
    r2 = dot(stack[:16], x2, NT)
    r3 = dot(stack[:16], x3, NT)
    s = r1[:8] + (r1[8:16] + r2[:8]) + (r1[16:24] + r2[8:16] + r3[:8])

    @pl.when(pl.program_id(0) == 0)
    def _():
        send_ref[...] = flip_rows(s, 1)
        copy_ref[...] = x

    @pl.when(pl.program_id(0) == 1)
    def _():
        keep_ref[...] = s


def scores(idx, features, a_own, after=()):
    rows, cols = features.shape
    tile = 2048
    n = rows // 2 // tile
    return call(
        score_kernel,
        "scores",
        (2, n),
        [
            (idx, None),
            (features, pl.BlockSpec((tile, cols), lambda g, i, s: ((s[0] ^ 1 ^ g) * n + i, 0))),
            (a_own, whole(8, cols)),
        ],
        [
            (shape(8, rows // 2), pl.BlockSpec((8, tile), lambda g, i, s: (0, i * (1 - g) + (n - 1) * g))),
            (shape(8, rows // 2), pl.BlockSpec((8, tile), lambda g, i, s: (0, i * g))),
            (
                shape(rows // 2, cols),
                pl.BlockSpec((tile, cols), lambda g, i, s: (i * (1 - g) + (n - 1) * g, 0)),
            ),
        ],
        after=after,
        vmem=24,
        work=(1e12, 1e5),
    )


def forward_kernel(pair, idx_ref, adj_ref, sa_ref, sb_ref, xa_ref, xb_ref, *refs):
    first = pair == 1
    u_ref, linv_ref, tm_ref, s_ref, wh_ref, wl_ref = refs[:6]
    xh_ref, xl_ref = refs[6:8] if first else (xa_ref, xb_ref)
    rows, src = adj_ref.shape[1], adj_ref.shape[2]
    b = pl.program_id(0)
    nb2 = pl.num_programs(0)
    block = pl.ds(pl.multiple_of(b * src, src), src)

    def loads(blk):
        xbuf, sems = refs[8:]
        to = lax.rem(blk, 2)
        at = pl.ds(pl.multiple_of(blk * src, src), src)
        own = pl.ds(pl.multiple_of((idx_ref[0] * nb2 + blk) * src, src), src)
        return (
            pltpu.make_async_copy(xa_ref.at[own, :], xbuf.at[to, 0], sems.at[to, 0]),
            pltpu.make_async_copy(xb_ref.at[at, :], xbuf.at[to, 1], sems.at[to, 1]),
        )

    if first:

        @pl.when(b == 0)
        def _():
            for copy in loads(b):
                copy.start()

    s_all = sa_ref[:, block] + flip_rows(sb_ref[:, block], 2)
    s_ref[:, block] = s_all
    tm_ref[b, :, 0:8] = jnp.transpose(s_all[:, :rows])
    part = lambda m, k, n: s_ref[m : m + 1, pl.ds(pl.multiple_of(b * src + k, 128), n)]
    heads = (2 * pair, 2 * pair + 1)
    step = 64

    for r in range(0, rows, step):
        best = [jnp.full((step, 128), LOW, F32) for _ in heads]
        for k in range(0, src, 128):
            linked = adj_ref[0, r : r + step, k : k + 128] > 0
            for n, m in enumerate(heads):
                best[n] = jnp.maximum(best[n], jnp.where(linked, part(m, k, 128), LOW))
        for n, m in enumerate(heads):
            t = tm_ref[b, r : r + step, HEADS + m : HEADS + m + 1]
            top = leaky2(t + jnp.max(best[n], axis=1, keepdims=True))
            tm_ref[b, r : r + step, m : m + 1] = top

    for n in range(3):
        if n < 2:
            m = heads[n]
            for r in range(0, rows, 32):
                at = slice(r, r + 32)
                to = slice(n * rows + r, n * rows + r + 32)
                t = tm_ref[b, at, HEADS + m : HEADS + m + 1]
                top = tm_ref[b, at, m : m + 1]
                acc = None
                for k in range(0, src, 512):
                    ks = slice(k, k + 512)
                    q = leaky2(t + part(m, k, 512))
                    w = jnp.where(adj_ref[0, at, ks] > 0, jnp.exp2(q - top), 0.0)
                    hi, lo = split2(w)
                    wh_ref[b, to, ks] = hi
                    wl_ref[b, to, ks] = lo
                    acc = lane_groups(w) if acc is None else acc + lane_groups(w)
                linv = 1.0 / jnp.sum(acc, axis=1, keepdims=True)
                linv_ref[b, to, :] = jnp.broadcast_to(linv, (32, 128))
        if n == 0 and first:
            cols = xa_ref.shape[1]
            xbuf = refs[8]
            slot = lax.rem(b, 2)
            for copy in loads(b):
                copy.wait()

            @pl.when(b + 1 < nb2)
            def _():
                for copy in loads(b + 1):
                    copy.start()

            @pl.loop(0, src, step=256)
            def _(r):
                at = pl.ds(pl.multiple_of(b * src + r, 256), 256)
                for k in range(2):
                    hi, lo = split2(xbuf[slot, k, pl.ds(r, 256), :])
                    xh_ref[at, k * cols : (k + 1) * cols] = hi
                    xl_ref[at, k * cols : (k + 1) * cols] = lo

        if n > 0:
            at = slice((n - 1) * rows, n * rows)
            lhs = cat3((wh_ref[b, at, :], wl_ref[b, at, :]), 1, False)
            rhs = cat3((xh_ref[block, :], xl_ref[block, :]), 0, True)
            u_ref[b, at, :] = dot(lhs, rhs, NN)


def forward_pair(pair, idx, xa, xb, adjacency, s_mine, s_cross, nb2, after=()):
    rows, src = adjacency.shape[1:]
    first = pair == 1
    cols = xa.shape[1]
    kd = 2 * cols if first else cols
    two = 2 * rows
    outs = [
        shape(nb2, two, kd),
        shape(nb2, two, 128),
        shape(nb2, rows, 128),
        shape(8, nb2 * src),
        shape(nb2, two, src, dtype=BF16),
        shape(nb2, two, src, dtype=BF16),
    ]
    if first:
        outs += [shape(nb2 * src, kd, dtype=BF16)] * 2
    return call(
        functools.partial(forward_kernel, pair),
        "forward_pair",
        (nb2,),
        [
            (idx, None),
            (adjacency, pl.BlockSpec((1, rows, src), lambda b, i: (i[0] * nb2 + b, 0, 0))),
            (s_mine, NEAR),
            (s_cross, NEAR),
            (xa, HBM if first else NEAR),
            (xb, ANY if first else NEAR),
        ],
        [(v, NEAR) for v in outs],
        scratch=[pltpu.VMEM((2, 2, src, cols), F32), pltpu.SemaphoreType.DMA((2, 2))] if first else [],
        after=after,
        work=(1e12 if first else 1e8, 1e5),
        vmem=22 if first else 16,
    )


def rel_rows(piece, mat, idx_ref):
    core = idx_ref[0]
    ref = piece[mat]
    cols = ref.shape[0] // 2
    at = lambda k: pl.ds(pl.multiple_of(k * cols, cols), cols)
    return jnp.concatenate([ref[at(core), :], ref[at(core ^ 1), :]], axis=0)


def flat_weights(pieces):
    return [(v, NEAR) for p in pieces for v in p]


def take_weights(pieces, refs):
    out = []
    for p in pieces:
        out.append(refs[: len(p)])
        refs = refs[len(p) :]
    return out, refs


def pre_kernel(form, src, u_ref, linv_ref, xh_ref, xl_ref, *refs):
    idx_ref = Place()
    weights, (o_ref,) = take_weights(form, refs)
    nb2, two = u_ref.shape[:2]
    rows = two // 2
    stack = lambda parts: jnp.concatenate(list(parts), axis=0)
    tops = [slice(b * src, b * src + rows) for b in range(nb2)]
    x = (stack(xh_ref[t, :] for t in tops), stack(xl_ref[t, :] for t in tops))
    for a, piece in enumerate(weights):
        at = slice(a * rows, (a + 1) * rows)
        mixed = split2(stack(u_ref[b, at, :] * linv_ref[b, at, 0:1] for b in range(nb2)))
        lhs = jnp.concatenate([cat3(mixed, 1, False), cat3(x, 1, False)], axis=1)
        proj, skip = split2(rel_rows(piece, 0, idx_ref)), split2(rel_rows(piece, 1, idx_ref))
        rhs = jnp.concatenate([cat3(proj, 0, True), cat3(skip, 0, True)], axis=0)
        o_ref[:, a * HD : (a + 1) * HD] = dot(lhs, rhs, NN)


def pre_pair(idx, u, linv, x_split, weights, src, spec, after=()):
    nb2, two, kd = u.shape
    rows = two // 2
    return call(
        functools.partial(pre_kernel, weights, src),
        "pre_pair",
        (1,),
        [(u, NEAR), (linv, NEAR), (x_split[0], NEAR), (x_split[1], NEAR)] + flat_weights(weights),
        [(shape(nb2 * rows, 2 * HD), spec)],
        after=after,
        work=(1e8, 1e5),
        vmem=16,
    )[0]


def live_rows(idx_ref, counts_ref, nb2, rows):
    parts = []
    for b in range(nb2):
        row = lax.broadcasted_iota(jnp.int32, (rows, 1), 0)
        parts.append((row < counts_ref[idx_ref[0] * nb2 + b]).astype(F32))
    return jnp.concatenate(parts, axis=0)


def stats_kernel(nb2, idx_ref, counts_ref, ca_ref, cb_ref, pa_ref, pb_ref, part_ref, recv_ref, pre_ref, st_ref, flip_ref):
    rows = part_ref.shape[0] // nb2
    total = lambda v: jnp.sum(v, axis=0, keepdims=True)
    live = live_rows(idx_ref, counts_ref, nb2, rows)
    for a, (c_ref, p_ref) in enumerate(((ca_ref, pa_ref), (cb_ref, pb_ref))):
        cols = slice(a * HD, (a + 1) * HD)
        bias = p_ref[0:1, :]
        pre = part_ref[:, cols] + recv_ref[:, cols] + bias
        pre_ref[:, cols] = pre
        act = (elu(pre) - elu(bias)) * live
        g = c_ref[...] * live
        rows8 = [total(act), total(act * act), total(g), total(g * act)]
        rows8.append(jnp.broadcast_to(total(live), (1, HD)))
        rows8.append(jnp.zeros((3, HD), F32))
        stats = jnp.concatenate(rows8, axis=0)
        st_ref[a] = stats
        flip_ref[1 - a] = stats


def norm_sums(hold, idx, counts, cotangent, cot_sib, par, par_sib, part, recv, nb2):
    full = part.shape[0]
    return call(
        functools.partial(stats_kernel, nb2),
        "norm_sums",
        (1,),
        [
            (idx, None),
            (counts, pl.BlockSpec(memory_space=pltpu.SMEM)),
            (cotangent, pl.BlockSpec((full, HD), lambda g, i: (i[0], 0))),
            (cot_sib, whole(full, HD)),
            (par, whole(8, HD)),
            (par_sib, whole(8, HD)),
            (part, NEAR),
            (recv, whole(full, 2 * HD)),
        ],
        [
            (shape(full, 2 * HD), NEAR),
            (shape(2, 8, HD), whole(2, 8, HD)),
            (shape(2, 8, HD), whole(2, 8, HD)),
        ],
        work=(1e8, 1e5),
        least=3 * 2**19,
        hold=hold,
        vmem=14,
    )


def apply_kernel(
    nb2, idx_ref, counts_ref, pre_ref, ca_ref, cb_ref, pa_ref, pb_ref, st_ref, act_ref, send_ref, d_ref, o_ref
):
    rows = pre_ref.shape[0] // nb2
    live = live_rows(idx_ref, counts_ref, nb2, rows)
    for a, (c_ref, p_ref, out_ref) in enumerate(
        ((ca_ref, pa_ref, act_ref), (cb_ref, pb_ref, send_ref))
    ):
        cols = slice(a * HD, (a + 1) * HD)
        bias, gamma, beta = p_ref[0:1, :], p_ref[1:2, :], p_ref[2:3, :]
        count = st_ref[a, 4:5, :]
        mean = st_ref[a, 0:1, :] / count
        inv = lax.rsqrt(st_ref[a, 1:2, :] / count - mean * mean + eps)
        grad_beta = st_ref[a, 2:3, :]
        grad_gamma = inv * (st_ref[a, 3:4, :] - mean * grad_beta)
        pre = pre_ref[:, cols]
        nrm = (elu(pre) - elu(bias) - mean) * inv
        out_ref[...] = live * (gamma * nrm + beta)
        g = c_ref[...] * live
        d = live * (gamma * inv) * (g - grad_beta / count - nrm * (grad_gamma / count))
        d = d * jnp.exp(jnp.minimum(pre, 0.0))
        d_ref[:, cols] = d
        o_ref[a, 0:1, :] = grad_gamma
        o_ref[a, 1:2, :] = grad_beta
        o_ref[a, 2:3, :] = jnp.sum(d, axis=0, keepdims=True)
        o_ref[a, 3:8, :] = jnp.zeros((5, HD), F32)


def norm_apply(hold, idx, counts, pre, cotangent, cot_sib, par, par_sib, stats, nb2):
    full = pre.shape[0]
    return call(
        functools.partial(apply_kernel, nb2),
        "norm_apply",
        (1,),
        [
            (idx, None),
            (counts, pl.BlockSpec(memory_space=pltpu.SMEM)),
            (pre, NEAR),
            (cotangent, pl.BlockSpec((full, HD), lambda g, i: (i[0], 0))),
            (cot_sib, whole(full, HD)),
            (par, whole(8, HD)),
            (par_sib, whole(8, HD)),
            (stats, whole(2, 8, HD)),
        ],
        [
            (shape(2 * full, HD), pl.BlockSpec((full, HD), lambda g, i: (i[0], 0))),
            (shape(full, HD), whole(full, HD)),
            (shape(full, 2 * HD), NEAR),
            (shape(2, 8, HD), whole(2, 8, HD)),
        ],
        least=3 * 2**19,
        hold=hold,
        vmem=14,
        work=(1e8, 1e5),
    )


def back_kernel(
    blk, pair, form, prior, xh_ref, xl_ref, wh_ref, wl_ref, s_ref, tm_ref, d_ref, linv_ref, u_ref, *refs
):
    idx_ref = Place()
    weights, refs = take_weights(form, refs)
    before, refs = refs[:pair], refs[pair:]
    earlier, refs = refs[:prior], refs[prior:]
    vh_ref, vl_ref, ds_ref, dp, delta, tacc = refs
    rows = tm_ref.shape[1]
    src = wh_ref.shape[2]
    base = 8 * prior
    for n, v in enumerate(earlier):
        ds_ref[8 * n : 8 * n + 8, :] = v[...]
    ds_ref[base : base + 8, :] = before[0][...] if pair == 1 else jnp.zeros((8, src), F32)
    tacc[...] = jnp.zeros_like(tacc)
    for a, piece in enumerate(weights):
        at = slice(a * rows, (a + 1) * rows)
        linv = linv_ref[blk, at, :]
        d = split2(d_ref[blk * rows : (blk + 1) * rows, a * HD : (a + 1) * HD] * linv[:, 0:1])
        v = dot(cat3(d, 1, False), cat3(split2(rel_rows(piece, 0, idx_ref)), 1, True), NT)
        hi, lo = split2(v)
        vh_ref[at, :] = hi
        vl_ref[at, :] = lo
        delta[at, :] = jnp.sum(v * u_ref[blk, at, :], axis=1, keepdims=True) * linv
    width = dp.shape[1]
    for j in range(src // width):
        js = slice(j * width, (j + 1) * width)
        xs = slice(blk * src + j * width, blk * src + (j + 1) * width)
        x = (xh_ref[xs, :], xl_ref[xs, :])
        dp[...] = dot(cat3((vh_ref[...], vl_ref[...]), 1, False), cat3(x, 1, True), NT)
        for a in range(2):
            m = 2 * pair + a
            s = s_ref[m : m + 1, xs] * HALF_LN2
            total = None
            for r in range(0, rows, 32):
                at = slice(r, r + 32)
                ar = slice(a * rows + r, a * rows + r + 32)
                t = tm_ref[blk, at, HEADS + m : HEADS + m + 1] * HALF_LN2
                slope = 0.6 + 0.4 * jnp.tanh(t + s)
                w = wh_ref[blk, ar, js].astype(F32) + wl_ref[blk, ar, js].astype(F32)
                dv = (w * slope) * (dp[ar, :] - delta[ar, 0:1])
                tacc[ar, :] += lane_groups(dv)
                total = dv if total is None else total + dv
            ds_ref[base + m : base + m + 1, js] = jnp.sum(total, axis=0, keepdims=True)
    for a in range(2):
        m = HEADS + 2 * pair + a
        sums = jnp.sum(tacc[a * rows : (a + 1) * rows, :], axis=1, keepdims=True)
        turned = jnp.transpose(jnp.broadcast_to(sums, (rows, 128)))
        ds_ref[base + m : base + m + 1, 0:rows] = turned[0:1, :]


def back_block(blk, pair, idx, x_split, fwd, d, weights, before=(), earlier=(), after=()):
    u, linv, tm, s, wh, wl = fwd
    two, src = wh.shape[1:]
    kd = u.shape[2]
    tj = 2 * TJ
    arrays = [*x_split, wh, wl, s, tm, d, linv, u]
    rest = [*before, *earlier]
    return call(
        functools.partial(back_kernel, blk, pair, weights, len(earlier)),
        "back_block",
        (1,),
        [(v, NEAR) for v in arrays] + flat_weights(weights) + [(v, NEAR) for v in rest],
        [
            (shape(two, kd, dtype=BF16), NEAR),
            (shape(two, kd, dtype=BF16), NEAR),
            (shape(8 * len(earlier) + 8, src), NEAR),
        ],
        scratch=[pltpu.VMEM((two, tj), F32), pltpu.VMEM((two, 128), F32), pltpu.VMEM((two, 128), F32)],
        after=after,
        work=(1e8, 1e5),
        vmem=16,
    )


def weight_kernel(src, u_ref, linv_ref, d_ref, xh_ref, xl_ref, send_ref, keep_ref):
    idx_ref = Place()
    core = idx_ref[0]
    nb2, two = u_ref.shape[:2]
    rows = two // 2
    stack = lambda parts: jnp.concatenate(list(parts), axis=0)
    tops = [slice(b * src, b * src + rows) for b in range(nb2)]
    x = cat3((stack(xh_ref[t, :] for t in tops), stack(xl_ref[t, :] for t in tops)), 0, False)
    for a, ref in ((1, send_ref), (0, keep_ref)):
        at = slice(a * rows, (a + 1) * rows)
        d = d_ref[:, a * HD : (a + 1) * HD]
        u = split2(stack(u_ref[b, at, :] for b in range(nb2)))
        dn = split2(d * stack(linv_ref[b, at, 0:1] for b in range(nb2)))
        gp = dot(cat3(u, 0, False), cat3(dn, 0, True), TN)
        gs = dot(x, cat3(split2(d), 0, True), TN)
        cols = gp.shape[0] // 2
        for mat, g in enumerate((gp, gs)):
            ref[mat, core] = g[:cols]
            ref[mat, core ^ 1] = g[cols:]


def weight_pair(idx, x_split, fwd, d, src, after=()):
    u, linv = fwd[:2]
    cols = u.shape[2] // 2
    arrays = [u, linv, d, *x_split]
    out = shape(2, 2, cols, HD)
    return call(
        functools.partial(weight_kernel, src),
        "weight_pair",
        (1,),
        [(v, NEAR) for v in arrays],
        [(out, NEAR), (out, NEAR)],
        after=after,
        work=(1e8, 1e5),
        vmem=16,
    )


def thin_kernel(xh_ref, xl_ref, da_ref, db_ref, o_ref, flip_ref):
    idx_ref = Place()
    core = idx_ref[0]
    cols = xh_ref.shape[1] // 2
    nb2, src = da_ref.shape[0] // 8, da_ref.shape[1]
    total = None
    for b in range(nb2):
        rows8 = slice(8 * b, 8 * b + 8)
        d = da_ref[rows8, :] + flip_rows(db_ref[rows8, :], 2)
        hi = d.astype(BF16).astype(F32)
        stack = jnp.concatenate([hi, d - hi], axis=0).astype(BF16)
        at = slice(b * src, (b + 1) * src)
        r1 = dot(stack, xh_ref[at, :], NN)
        r2 = dot(stack, xl_ref[at, :], NN)
        q = r1[:8] + (r1[8:] + r2[:8])
        total = q if total is None else total + q
    for k, q in enumerate((total[:, :cols], total[:, cols:])):
        o_ref[core ^ k] = q
        flip_ref[core ^ k] = flip_rows(q, 1)


def thin_sums(idx, x_split, ds, ds_cross, after=()):
    cols = x_split[0].shape[1] // 2
    return call(
        thin_kernel,
        "thin_sums",
        (1,),
        [(x_split[0], NEAR), (x_split[1], NEAR), (ds, NEAR), (ds_cross, NEAR)],
        [(shape(2, 8, cols), NEAR)] * 2,
        after=after,
        work=(1e8, 1e5),
        vmem=14,
    )


def skip_back(at, d_ref, weights, idx_ref):
    pair = [split2(rel_rows(piece, 1, idx_ref)) for piece in weights]
    both = [jnp.concatenate([p[n] for p in pair], axis=1) for n in range(2)]
    return dot(cat3(split2(d_ref[at, :]), 1, False), cat3(both, 1, True), NT)


def mix_kernel(blk, form, wh, wl, vh, vl, d_ref, *refs):
    idx_ref = Place()
    weights, (o_ref, mark_ref) = take_weights(form, refs)
    mark_ref[...] = jnp.zeros_like(mark_ref)
    j = pl.program_id(0)
    rows = vh.shape[0] // 2
    js = pl.ds(pl.multiple_of(j * TJ, TJ), TJ)
    rhs = cat3((vh[...], vl[...]), 0, True)
    o_ref[...] = dot(cat3((wh[blk, :, js], wl[blk, :, js]), 0, False), rhs, TN)

    @pl.when(j == 0)
    def _():
        o_ref[0:rows, :] += skip_back(slice(blk * rows, (blk + 1) * rows), d_ref, weights, idx_ref)


def mix_block(blk, idx, w, v, d, weights, after=()):
    src = w[0].shape[2]
    kd = v[0].shape[1]
    return call(
        functools.partial(mix_kernel, blk, weights),
        "mix_block",
        (src // TJ,),
        [(a, NEAR) for a in (*w, *v, d)] + flat_weights(weights),
        [(shape(src, kd), pl.BlockSpec((TJ, kd), lambda j: (j, 0))), (shape(8, 128), whole(8, 128))],
        after=after,
        work=(1e8, 1e5),
        vmem=16,
    )


def feature_kernel(blk, part, form, idx_ref, g_ref, wh, wl, vh, vl, da_ref, db_ref, a_ref, d_ref, *refs):
    weights, refs = take_weights(form, refs)
    oo_ref, os_ref, mark_ref = refs[-3:]
    j = pl.program_id(0)
    mark_ref[...] = jnp.zeros_like(mark_ref)
    half = oo_ref.shape[1]
    rows = vh.shape[0] // 2
    js = pl.ds(pl.multiple_of((part * pl.num_programs(0) + j) * TJ, TJ), TJ)
    rows8 = slice(8 * blk, 8 * blk + 8)
    d = da_ref[rows8, js] + flip_rows(db_ref[rows8, js], 2)
    out = dot(cat3((wh[blk, :, js], wl[blk, :, js]), 0, False), cat3((vh[...], vl[...]), 0, True), TN)
    out = out + (g_ref[...] + dot(thin_rows(d), thin_cols(a_ref[...]), TN))
    oo_ref[...] = out[:, :half]
    os_ref[...] = out[:, half:]
    if part == 0:

        @pl.when(j == 0)
        def _():
            more = skip_back(slice(blk * rows, (blk + 1) * rows), d_ref, weights, idx_ref)
            oo_ref[0:rows, :] += more[:, :half]
            os_ref[0:rows, :] += more[:, half:]


def feature_block(
    blk, part, idx, mixed, w, v, ds, ds_cross, a_half, d, weights, full, nb2, before, after=()
):
    src = w[0].shape[2]
    kd = v[0].shape[1]
    half = kd // 2
    nj = src // TJ
    count = nj // PARTS
    first = part * count
    ins = [(idx, None), (mixed, pl.BlockSpec((TJ, kd), lambda j, i: (first + j, 0)))]
    ins += [(a, NEAR) for a in (*w, *v)]
    ins += [(ds, NEAR), (ds_cross, NEAR), (a_half, NEAR), (d, NEAR)]
    ins += flat_weights(weights)
    aliases = {}
    if before is not None:
        aliases[len(ins)] = 0
        ins.append((before, HBM))
    return call(
        functools.partial(feature_kernel, blk, part, weights),
        "feature_block",
        (count,),
        ins,
        [
            (shape(*full), pl.BlockSpec((TJ, half), lambda j, i: ((i[0] * nb2 + blk) * nj + first + j, 0))),
            (shape(src // PARTS, half), pl.BlockSpec((TJ, half), lambda j, i: (j, 0))),
            (shape(8, 128), whole(8, 128)),
        ],
        after=after,
        work=(1e8, 1e5),
        vmem=18,
        aliases=aliases,
    )


def place_kernel(nb2, idx_ref, *refs):
    parts, (out_ref, mark_ref, buf, sems) = refs[:nb2], refs[nb2 + 1 :]
    mark_ref[...] = jnp.zeros_like(mark_ref)
    src = parts[0].shape[0]
    size = buf.shape[1]
    n = src // size

    def load(b, k):
        return pltpu.make_async_copy(parts[b].at[pl.ds(k * size, size), :], buf.at[b * n + k], sems.at[0, b * n + k])

    def store(b, k):
        at = pl.multiple_of((idx_ref[2] * nb2 + b) * src + k * size, size)
        return pltpu.make_async_copy(buf.at[b * n + k], out_ref.at[pl.ds(at, size), :], sems.at[1, b * n + k])

    every = [(b, k) for b in range(nb2) for k in range(n)]
    for b, k in every:
        load(b, k).start()
    for b, k in every:
        load(b, k).wait()
        store(b, k).start()
    for b, k in every:
        store(b, k).wait()


def place(idx, parts, before, after=()):
    nb2 = len(parts)
    src, half = parts[0].shape
    count = nb2 * src // TJ
    return call(
        functools.partial(place_kernel, nb2),
        "place",
        (1,),
        [(idx, None)] + [(v, HBM) for v in parts] + [(before, HBM)],
        [(shape(*before.shape), HBM), (shape(8, 128), whole(8, 128))],
        scratch=[pltpu.VMEM((count, TJ, half), F32), pltpu.SemaphoreType.DMA((2, count))],
        after=after,
        work=(1e3, 1e6),
        least=2**18,
        vmem=14,
        aliases={1 + nb2: 0},
    )


def split_kernel(at, keep_ref, recv_ref, send_ref, next_ref):
    idx_ref = Place()
    size = next_ref.shape[1]
    mine = pl.ds(pl.multiple_of(idx_ref[at] * size, size), size)
    other = pl.ds(pl.multiple_of((1 - idx_ref[at]) * size, size), size)
    send_ref[...] = keep_ref[:, other, :] + recv_ref[:, other, :]
    next_ref[...] = keep_ref[:, mine, :] + recv_ref[:, mine, :]


def split_step(at, idx, keep, recv, after=()):
    n, rows, cols = keep.shape
    part = (n, rows // 2, cols)
    return call(
        functools.partial(split_kernel, at),
        "split_step",
        (1,),
        [(keep, NEAR), (recv, NEAR)],
        [(shape(*part), NEAR)] * 2,
        after=after,
        work=(1e3, keep.size * 8),
        vmem=8,
    )


def add_kernel(a_ref, b_ref, o_ref):
    o_ref[...] = a_ref[...] + b_ref[...]


def add_step(idx, a, b, after=()):
    return call(
        add_kernel,
        "add_step",
        (1,),
        [(a, NEAR), (b, NEAR)],
        [(shape(*a.shape), NEAR)],
        after=after,
        least=3 * 2**19,
        vmem=8,
        work=(1e3, a.size * 8),
    )[0]


def join_kernel(at, mine_ref, recv_ref, o_ref):
    idx_ref = Place()
    size = (mine_ref.shape[0] - EXTRA) // 2
    for mat in range(2):
        old = slice(mat * size, (mat + 1) * size)
        put = lambda up: pl.ds(pl.multiple_of(2 * mat * size + up * size, size), size)
        o_ref[put(idx_ref[at]), :] = mine_ref[old, :]
        o_ref[put(1 - idx_ref[at]), :] = recv_ref[old, :]
    o_ref[4 * size :, :] = mine_ref[2 * size :, :] + recv_ref[2 * size :, :]


def join_step(at, idx, mine, recv, after=()):
    rows, cols = mine.shape
    full = 2 * (rows - EXTRA) + EXTRA
    return call(
        functools.partial(join_kernel, at),
        "join_step",
        (1,),
        [(mine, NEAR), (recv, NEAR)],
        [(shape(full, cols), NEAR)],
        after=after,
        work=(1e3, mine.size * 16),
        least=3 * 2**19,
        vmem=10,
    )[0]


def end_kernel(keep_ref, recv_ref, o_ref):
    size = keep_ref.shape[1]
    for mat in range(2):
        o_ref[mat * size : (mat + 1) * size, :] = keep_ref[mat] + recv_ref[mat]
    o_ref[2 * size :, :] = jnp.zeros((EXTRA, o_ref.shape[1]), F32)


def end_step(idx, keep, recv, after=()):
    n, rows, cols = keep.shape
    full = n * rows + EXTRA
    return call(
        end_kernel,
        "end_step",
        (1,),
        [(keep, NEAR), (recv, NEAR)],
        [(shape(full, cols), NEAR)],
        after=after,
        work=(1e3, keep.size * 8),
        least=3 * 2**19,
        vmem=8,
    )[0]


def swap_kernel(keep_ref, recv_ref, q_ref, qr_ref, b_ref, br_ref, o_ref, extra_ref):
    size = keep_ref.shape[1]
    for mat in range(2):
        o_ref[mat * size : (mat + 1) * size, :] = keep_ref[mat] + recv_ref[mat]
    q = q_ref[...] + qr_ref[...]
    width = o_ref.shape[1]
    pick = lambda m: [q[k, n : n + 1, :] for k in range(2) for n in (m, HEADS + m)]
    zero = lambda n: [jnp.zeros((n, width), F32)]
    o_ref[2 * size :, :] = jnp.concatenate(pick(2) + zero(EXTRA - 4), axis=0)
    bias = b_ref[0, 2:3, :] + br_ref[1, 2:3, :]
    extra_ref[...] = jnp.concatenate(zero(4) + pick(0) + [bias] + zero(EXTRA - 9), axis=0)


def swap_step(idx, keep, recv, q, q_recv, sums, sums_recv, after=()):
    n, rows, cols = keep.shape
    full = n * rows + EXTRA
    arrays = [keep, recv, q, q_recv, sums, sums_recv]
    return call(
        swap_kernel,
        "swap_step",
        (1,),
        [(v, NEAR) for v in arrays],
        [(shape(full, cols), NEAR), (shape(EXTRA, cols), NEAR)],
        after=after,
        work=(1e3, keep.size * 8),
        least=3 * 2**19,
        vmem=8,
    )


def enter_kernel(a_ref, b_ref, extra_ref, more_ref, o_ref):
    rows = a_ref.shape[0] - EXTRA
    o_ref[...] = a_ref[...] + b_ref[...]
    o_ref[rows:, :] += extra_ref[...] + more_ref[...]


def enter_step(a, b, extra, more, after=()):
    return call(
        enter_kernel,
        "enter_step",
        (1,),
        [(v, NEAR) for v in (a, b, extra, more)],
        [(shape(*a.shape), NEAR)],
        after=after,
        work=(1e3, a.size * 8),
        vmem=8,
    )[0]


def last_kernel(idx_ref, own_ref, far_ref, att_ref, w_ref, op_ref, os_ref, oa_ref, ob_ref, bias_ref):
    tall = own_ref.shape[0] - EXTRA
    size = tall // 2

    def put(g_ref, first):
        total = None
        for k in range(2):
            at = slice(k * size // 2, (k + 1) * size // 2)
            q = far_ref[tall + first + 2 * k : tall + first + 2 * k + 2, :]
            q = jnp.concatenate([q, jnp.zeros((6, q.shape[1]), F32)], axis=0)
            op_ref[at, :] = g_ref[at, :] + dot(thin_rows(q), thin_cols(att_ref[...]), TN)
            hi = q.astype(BF16).astype(F32)
            stack = jnp.concatenate([hi, q - hi], axis=0).astype(BF16)
            wh, wl = split2(w_ref[at, :])
            r1, r2 = dot(stack, wh, NN), dot(stack, wl, NN)
            new = r1[:8] + (r1[8:] + r2[:8])
            total = new if total is None else total + new
        os_ref[...] = g_ref[size:tall, :]
        return total[0:1], total[1:2]

    @pl.when(pl.program_id(0) == 0)
    def _():
        a, b = put(own_ref, 4)
        oa_ref[...] = a
        ob_ref[...] = b
        bias_ref[...] = far_ref[tall + 8 : tall + 9, :]

    @pl.when(pl.program_id(0) == 1)
    def _():
        a, b = put(far_ref, 0)
        oa_ref[...] += a
        ob_ref[...] += b


def last_step(idx, own, far, att, w_proj, after=()):
    rows, width = own.shape
    size = (rows - EXTRA) // 2
    out = pl.BlockSpec((size, width), lambda g, i: (i[1] ^ g, 0))
    return call(
        last_kernel,
        "last_step",
        (2,),
        [(idx, None)] + [(v, NEAR) for v in (own, far, att)] + [(w_proj, out)],
        [(shape(2 * size, width), out)] * 2 + [(shape(1, width), whole(1, width))] * 3,
        after=after,
        work=(1e12, 4e6),
        least=3 * 2**19,
        vmem=16,
    )


def make_step(dp_size):
    bits = [1 << k for k in range(dp_size.bit_length() - 1)]

    def on_device(
        features, adjacency, seed_counts, w_proj, w_skip, attn_src, attn_dst, bias, gamma, beta, cotangent
    ):
        nb, rows, src = adjacency.shape
        cols = features.shape[1]
        nb2 = nb // 2
        h = lax.axis_index("head")
        dpi = lax.axis_index("dp")
        core, side = h & 1, h >> 1
        def to_core(v):
            return lax.ppermute(v, "head", [(i, i ^ 1) for i in range(HEADS)])

        def to_cross(v):
            return lax.ppermute(v, "head", [(i, i ^ 2) for i in range(HEADS)])

        def to_both(v, bit):
            pairs = [(d * HEADS + i, (d ^ bit) * HEADS + (i ^ 2)) for d in range(dp_size) for i in range(HEADS)]
            return lax.ppermute(v, ("dp", "head"), pairs)

        def to_dp(v, bit):
            return lax.ppermute(v, "dp", [(i, i ^ bit) for i in range(dp_size)])

        def half(v, which):
            size = v.shape[0] // 2
            return lax.dynamic_slice_in_dim(v, which * size, size, 0)

        ups = [(dpi >> k) & 1 for k in range(len(bits))]
        idx = jnp.stack([core, side, 1 - core, 1 - side] + ups).astype(jnp.int32)

        with jax.named_scope("fold_attention"):
            folded = jnp.stack(
                [jnp.sum(w_proj * attn_src, axis=1), jnp.sum(w_proj * attn_dst, axis=1)]
            )
            near_folded = to_core(folded)
            folded = jnp.stack([folded, near_folded])
            a_all = jnp.concatenate([folded, to_cross(folded)])
            a_all = a_all.transpose(1, 0, 2).reshape(2 * HEADS, -1)
            a_own = lax.dynamic_slice_in_dim(a_all, h * cols, cols, 1) * LOG2E

        with jax.named_scope("scores"):
            par = jnp.pad(jnp.stack([bias, gamma, beta]), ((0, 5), (0, 0)))
            par_sib = to_core(par)
            att = jnp.pad(jnp.stack([attn_src, attn_dst]), ((0, 6), (0, 0)))
            proj_half, mark = pack(idx, [(w_proj, 3)], after=[near_folded])
            proj_far = to_cross(proj_half)
            s_send, s_keep, x_send = scores(idx, features, a_own, after=[mark])
            s_mine = add_step(idx, s_keep, to_core(s_send), after=[proj_far])
            x_sib = to_core(relay(x_send, HBM, after=[s_mine]))
            s_cross = to_cross(s_mine)

        with jax.named_scope("share_weights"):
            skip_half, cot_send, proj_own, skip_own, mark = pack(
                idx, [(w_skip, 3), (cotangent, 2), (w_proj, 1), (w_skip, 1)], after=[s_mine]
            )
            skip_far = to_cross(skip_half)
            cot_sib = to_core(cot_send)

        with jax.named_scope("forward"):
            far_fwd = forward_pair(
                1, idx, features, x_sib, adjacency, s_mine, s_cross, nb2, after=[par_sib, mark, att]
            )
            x_split, far_fwd = far_fwd[6:], far_fwd[:6]
            skip_far = relay(skip_far, HBM, after=[far_fwd[3]])
            far_weights = [(proj_far, skip_far), (to_core(proj_far), to_core(skip_far))]
            far_part = pre_pair(idx, *far_fwd[:2], x_split, far_weights, src, whole(nb2 * rows, 2 * HD))
            recv = to_cross(far_part)
            own_fwd = forward_pair(0, idx, *x_split, adjacency, s_mine, s_cross, nb2, after=[far_part])
            own_weights = [(proj_own, skip_own), (to_core(proj_own), to_core(skip_own))]
            own_part = pre_pair(idx, *own_fwd[:2], x_split, own_weights, src, NEAR)

        with jax.named_scope("norm"):
            hold = [*x_split, *own_fwd[4:], *far_fwd[4:], own_fwd[0], far_fwd[0]]
            pre, stats, flipped = norm_sums(
                hold, idx, seed_counts, cotangent, cot_sib, par, par_sib, own_part, recv, nb2
            )
            stats = stats + to_core(flipped)
            for bit in bits:
                stats = stats + to_dp(stats, bit)
            act, act_send, d_own, small = norm_apply(
                hold, idx, seed_counts, pre, cotangent, cot_sib, par, par_sib, stats, nb2
            )
            act_recv = to_core(act_send)
            d_far = to_cross(d_own)

        token = [d_own]
        resident = []

        def note(out):
            token[:] = [out] + [Held(v) for v in resident]
            return out

        flat = lambda v: v.reshape(2, 2 * cols, HD)
        backs, fars, theirs = [], [], []
        state = {}

        def scatter(send, keep, recv, bits):
            for k, bit in enumerate(bits):
                send, keep = split_step(4 + k, idx, keep, recv, after=token)
                note(keep)
                recv = to_dp(send, bit)
                yield
            return keep, recv

        def gather(rows, bits):
            for k, bit in reversed(list(enumerate(bits))):
                recv = to_dp(rows, bit)
                yield
                rows = note(join_step(4 + k, idx, rows, recv, after=token))
            return rows

        def own_chain(send, keep):
            keep, recv = yield from scatter(send, flat(keep), flat(to_core(send)), bits)
            rows = note(end_step(idx, keep, recv, after=token))
            state["own"] = yield from gather(rows, bits)

        def far_chain(send, keep):
            keep, recv = yield from scatter(send, flat(keep), flat(to_core(send)), bits[:-1])
            while "flip" not in state:
                yield
            message, extra = swap_step(
                idx, keep, recv, state["q"], state["q_recv"], small, state["sums_recv"], after=token
            )
            note(extra)
            arrived = [to_cross(message), to_both(message, bits[-1]), extra, to_dp(extra, bits[-1])]
            yield
            rows = note(enter_step(*arrived, after=token))
            state["far"] = yield from gather(rows, bits[:-1])

        def advance(*chains):
            for c in chains:
                next(c, None)

        def back_far(b):
            fars.append(
                back_block(
                    b, 1, idx, x_split, far_fwd, d_far, far_weights, before=[backs[b][2]],
                    earlier=[f[2] for f in fars] if b == nb2 - 1 else (), after=token,
                )
            )
            note(fars[-1][2])

        half_cols = lambda i: lax.dynamic_slice_in_dim(a_all, i * cols, cols, 1)
        a_half = jnp.concatenate([half_cols(h), half_cols(h ^ 1)], axis=1)

        def features_of(b, part):
            state["gf"], other, mark = feature_block(
                b, part, idx, mixed[b], far_fwd[4:], fars[b][:2], ds, ds_cross, a_half, d_far,
                far_weights, features.shape, nb2,
                before=state.get("gf"), after=token,
            )
            note(mark)
            theirs.append(to_core(other))

        with jax.named_scope("backward"):
            state["sums_recv"] = to_core(small)
            send, keep = weight_pair(
                idx, x_split, own_fwd, d_own, src, after=token + [state["sums_recv"]]
            )
            note(keep)
            own = own_chain(send, keep)
            mixed = []
            for b in range(nb2):
                backs.append(
                    back_block(
                        b, 0, idx, x_split, own_fwd, d_own, own_weights, after=token + ([act_recv] if b else [])
                    )
                )
                note(backs[-1][2])
                if b == 0:
                    advance(own)
            for b in range(nb2):
                out, mark = mix_block(b, idx, own_fwd[4:], backs[b][:2], d_own, own_weights, after=token)
                note(mark)
                mixed.append(out)
                if b == 0:
                    advance(own)
            send, keep = weight_pair(idx, x_split, far_fwd, d_far, src, after=token)
            note(keep)
            advance(own)
            resident[:] = [*x_split, *far_fwd[4:], far_fwd[0], far_fwd[1]]
            far = far_chain(relay(send, NEAR, after=token), keep)
            advance(far)
            for b in range(nb2):
                back_far(b)
                if b < nb2 - 1:
                    advance(own)
            advance(far)
            ds = relay(fars[-1][2], NEAR, after=token)
            ds_cross = to_cross(ds)
            state["q"], state["q_flip"] = thin_sums(idx, x_split, ds, ds_cross, after=token)
            note(state["q"])
            state["q_recv"] = to_core(state["q_flip"])
            state["flip"] = True
            resident[:] = far_fwd[4:]
            note(state["q"])
            advance(far, own)
            for b in range(nb2):
                for part in range(PARTS):
                    features_of(b, part)
                    n = b * PARTS + part
                    if 0 < n < nb2 * PARTS - 1:
                        advance(far)
                    if n == 0:
                        advance(own)
            resident[:] = []
            note(token[0])
            activations, mark = place(idx, [act_recv], act, after=token)
            note(mark)
            for c in (own, far):
                for _ in c:
                    pass

        with jax.named_scope("last"):
            grad_proj, grad_skip, grad_src, grad_dst, grad_bias = last_step(
                idx, state["own"], state["far"], att, w_proj
            )
            grad_features, mark = place(idx, theirs, state["gf"], after=[grad_src])

        return (
            activations,
            grad_features,
            grad_proj,
            grad_skip,
            grad_src[0],
            grad_dst[0],
            grad_bias[0],
            small[0, 0],
            small[0, 1],
        )

    return on_device


def solution(mesh):
    return jax.shard_map(
        make_step(mesh.shape["dp"]),
        mesh=mesh,
        in_specs=(
            P("dp", "head"),
            P("dp", None, None),
            P("dp"),
            P(None, "head"),
            P(None, "head"),
            P("head"),
            P("head"),
            P("head"),
            P("head"),
            P("head"),
            P("dp", "head"),
        ),
        out_specs=(
            P("dp", "head"),
            P("dp", "head"),
            P(None, "head"),
            P(None, "head"),
            P("head"),
            P("head"),
            P("head"),
            P("head"),
            P("head"),
        ),
        check_vma=False,
    )
```

```python
import functools

import jax
import jax.numpy as jnp
from jax import lax
from jax.experimental import pallas as pl
from jax.experimental.pallas import tpu as pltpu
from jax.sharding import PartitionSpec as P

HD = 256
HEADS = 4
TJ = 512
PARTS = 2
EXTRA = 16
eps = 1e-05
LOG2E = 1.4426950408889634
HALF_LN2 = 0.34657359027997264
F32 = jnp.float32
BF16 = jnp.bfloat16
NN = ((1,), (0,))
NT = ((1,), (1,))
TN = ((0,), (0,))
LOW = -3e38
HBM = pl.BlockSpec(memory_space=pltpu.HBM)
ANY = pl.BlockSpec(memory_space=pl.ANY)
NEAR = pl.BlockSpec(memory_space=pltpu.VMEM)


def dot(a, b, form):
    return lax.dot_general(a, b, (form, ((), ())), preferred_element_type=F32)


def split2(x):
    hi = x.astype(BF16)
    return hi, (x - hi.astype(F32)).astype(BF16)


def dot3(a, b, form):
    return dot(a[0], b[0], form) + (dot(a[0], b[1], form) + dot(a[1], b[0], form))


def cat3(a, axis, mixed):
    hi, lo = a
    return jnp.concatenate([hi, lo, hi] if mixed else [hi, hi, lo], axis=axis)


def thin_rows(d):
    hi = d.astype(BF16).astype(F32)
    return jnp.concatenate([hi, hi, d - hi, jnp.zeros_like(d)], axis=0).astype(BF16)


def thin_cols(a):
    hi = a.astype(BF16).astype(F32)
    return jnp.concatenate([hi, a - hi, hi, jnp.zeros_like(a)], axis=0).astype(BF16)


def lane_groups(v):
    out = v[:, :128]
    for k in range(128, v.shape[1], 128):
        out = out + v[:, k : k + 128]
    return out


def leaky2(u):
    soft = jnp.log2(1.0 + jnp.exp2(jnp.minimum(u, 126.0)))
    return jnp.maximum(u, 0.2 * u + 0.8 * soft)


def elu(v):
    return jnp.where(v > 0, v, jnp.exp(jnp.minimum(v, 0.0)) - 1.0)


def flip_rows(v, bit):
    return jnp.concatenate([v[m ^ bit : (m ^ bit) + 1] for m in range(8)], axis=0)


def large(v, least):
    return v.size * v.dtype.itemsize >= least


def held(v, spec, least):
    if spec is NEAR:
        return pltpu.with_memory_space_constraint(v, pltpu.VMEM)
    if spec is ANY:
        return v
    return pltpu.with_memory_space_constraint(v, pltpu.HBM) if large(v, least) else v


def result(v, spec, least):
    if spec is NEAR:
        return pltpu.VMEM(v.shape, v.dtype)
    return pltpu.HBM(v.shape, v.dtype) if large(v, least) else v


def call(kernel, name, grid, ins, outs, scratch=(), after=(), work=(1e6, 1e6), vmem=8, aliases=None, least=3 * 2**19, hold=()):
    n_in = len(ins)
    hold = [held(v.v, NEAR, least) for v in after if isinstance(v, Held)] + [held(v, NEAR, least) for v in hold]
    after = [v for v in after if not isinstance(v, Held)]
    n_after = len(after) + len(hold)
    scalars = 1 if ins[0][1] is None else 0
    ins = ins[:scalars] + [(held(v, spec, least), spec) for v, spec in ins[scalars:]]

    def body(*refs):
        kernel(*refs[:n_in], *refs[n_in + n_after :])

    return pl.pallas_call(
        body,
        grid_spec=pltpu.PrefetchScalarGridSpec(
            num_scalar_prefetch=scalars,
            grid=grid,
            in_specs=[s for _, s in ins[scalars:]] + [ANY] * len(after) + [NEAR] * len(hold),
            out_specs=[s for _, s in outs],
            scratch_shapes=list(scratch),
        ),
        out_shape=[result(v, spec, least) for v, spec in outs],
        compiler_params=pltpu.CompilerParams(
            dimension_semantics=("arbitrary",) * len(grid), vmem_limit_bytes=vmem * 2**20
        ),
        cost_estimate=pl.CostEstimate(
            flops=int(work[0]), bytes_accessed=int(work[1]), transcendentals=0
        ),
        input_output_aliases=aliases or {},
        name=name,
    )(*[v for v, _ in ins], *after, *hold)


class Held:
    def __init__(self, v):
        self.v = v


class Place:
    def __getitem__(self, k):
        h = lax.axis_index("head")
        if k < 4:
            bit = (h & 1, h >> 1)[k % 2]
            return bit if k < 2 else 1 - bit
        return (lax.axis_index("dp") >> (k - 4)) & 1


def shape(*dims, dtype=F32):
    return jax.ShapeDtypeStruct(dims, dtype)


def whole(*dims):
    return pl.BlockSpec(dims, lambda *_: (0,) * len(dims))


def pack_kernel(n, idx_ref, *refs):
    for k in range(n):
        refs[n + k][...] = refs[k][...]
    refs[2 * n][...] = jnp.zeros_like(refs[2 * n])


def pack(idx, parts, after=()):
    ins, outs = [(idx, None)], []
    for v, which in parts:
        dims = (v.shape[0] // 2, v.shape[1])
        ins.append((v, pl.BlockSpec(dims, lambda g, i, which=which: (i[which], 0))))
        outs.append((shape(*dims), whole(*dims)))
    return call(
        functools.partial(pack_kernel, len(parts)),
        "pack",
        (1,),
        ins,
        outs + [(shape(8, 128), whole(8, 128))],
        after=after,
        work=(1e3, 1e5),
        least=2**18,
        vmem=16,
    )


def relay_kernel(v_ref, o_ref):
    o_ref[...] = v_ref[...]


def relay(v, spec, after=()):
    near = spec is NEAR
    return call(
        relay_kernel if near else lambda *_: None,
        "relay",
        (1,),
        [(v, spec)],
        [(shape(*v.shape), spec)],
        after=after,
        work=(1e3, 1e3),
        least=2**18,
        aliases=None if near else {0: 0},
    )[0]


def score_kernel(idx_ref, x_ref, a_ref, send_ref, keep_ref, copy_ref):
    x = x_ref[...]
    x1 = x.astype(BF16)
    rest = x - x1.astype(F32)
    x2 = rest.astype(BF16)
    x3 = (rest - x2.astype(F32)).astype(BF16)
    a = a_ref[...]
    a1 = a.astype(BF16).astype(F32)
    a2 = (a - a1).astype(BF16).astype(F32)
    a3 = (a - a1) - a2
    stack = jnp.concatenate([a1, a2, a3, jnp.zeros_like(a)], axis=0).astype(BF16)
    r1 = dot(stack, x1, NT)
    r2 = dot(stack[:16], x2, NT)
    r3 = dot(stack[:16], x3, NT)
    s = r1[:8] + (r1[8:16] + r2[:8]) + (r1[16:24] + r2[8:16] + r3[:8])

    @pl.when(pl.program_id(0) == 0)
    def _():
        send_ref[...] = flip_rows(s, 1)
        copy_ref[...] = x

    @pl.when(pl.program_id(0) == 1)
    def _():
        keep_ref[...] = s


def scores(idx, features, a_own, after=()):
    rows, cols = features.shape
    tile = 2048
    n = rows // 2 // tile
    return call(
        score_kernel,
        "scores",
        (2, n),
        [
            (idx, None),
            (features, pl.BlockSpec((tile, cols), lambda g, i, s: ((s[0] ^ 1 ^ g) * n + i, 0))),
            (a_own, whole(8, cols)),
        ],
        [
            (shape(8, rows // 2), pl.BlockSpec((8, tile), lambda g, i, s: (0, i * (1 - g) + (n - 1) * g))),
            (shape(8, rows // 2), pl.BlockSpec((8, tile), lambda g, i, s: (0, i * g))),
            (
                shape(rows // 2, cols),
                pl.BlockSpec((tile, cols), lambda g, i, s: (i * (1 - g) + (n - 1) * g, 0)),
            ),
        ],
        after=after,
        vmem=24,
        work=(1e12, 1e5),
    )


def forward_kernel(pair, idx_ref, adj_ref, sa_ref, sb_ref, xa_ref, xb_ref, *refs):
    first = pair == 1
    u_ref, linv_ref, tm_ref, s_ref, wh_ref, wl_ref = refs[:6]
    xh_ref, xl_ref = refs[6:8] if first else (xa_ref, xb_ref)
    rows, src = adj_ref.shape[1], adj_ref.shape[2]
    b = pl.program_id(0)
    nb2 = pl.num_programs(0)
    block = pl.ds(pl.multiple_of(b * src, src), src)

    def loads(blk):
        xbuf, sems = refs[8:]
        to = lax.rem(blk, 2)
        at = pl.ds(pl.multiple_of(blk * src, src), src)
        own = pl.ds(pl.multiple_of((idx_ref[0] * nb2 + blk) * src, src), src)
        return (
            pltpu.make_async_copy(xa_ref.at[own, :], xbuf.at[to, 0], sems.at[to, 0]),
            pltpu.make_async_copy(xb_ref.at[at, :], xbuf.at[to, 1], sems.at[to, 1]),
        )

    if first:

        @pl.when(b == 0)
        def _():
            for copy in loads(b):
                copy.start()

    s_all = sa_ref[:, block] + flip_rows(sb_ref[:, block], 2)
    s_ref[:, block] = s_all
    tm_ref[b, :, 0:8] = jnp.transpose(s_all[:, :rows])
    part = lambda m, k, n: s_ref[m : m + 1, pl.ds(pl.multiple_of(b * src + k, 128), n)]
    heads = (2 * pair, 2 * pair + 1)
    step = 64

    for r in range(0, rows, step):
        best = [jnp.full((step, 128), LOW, F32) for _ in heads]
        for k in range(0, src, 128):
            linked = adj_ref[0, r : r + step, k : k + 128] > 0
            for n, m in enumerate(heads):
                best[n] = jnp.maximum(best[n], jnp.where(linked, part(m, k, 128), LOW))
        for n, m in enumerate(heads):
            t = tm_ref[b, r : r + step, HEADS + m : HEADS + m + 1]
            top = leaky2(t + jnp.max(best[n], axis=1, keepdims=True))
            tm_ref[b, r : r + step, m : m + 1] = top

    for n in range(3):
        if n < 2:
            m = heads[n]
            for r in range(0, rows, 32):
                at = slice(r, r + 32)
                to = slice(n * rows + r, n * rows + r + 32)
                t = tm_ref[b, at, HEADS + m : HEADS + m + 1]
                top = tm_ref[b, at, m : m + 1]
                acc = None
                for k in range(0, src, 512):
                    ks = slice(k, k + 512)
                    q = leaky2(t + part(m, k, 512))
                    w = jnp.where(adj_ref[0, at, ks] > 0, jnp.exp2(q - top), 0.0)
                    hi, lo = split2(w)
                    wh_ref[b, to, ks] = hi
                    wl_ref[b, to, ks] = lo
                    acc = lane_groups(w) if acc is None else acc + lane_groups(w)
                linv = 1.0 / jnp.sum(acc, axis=1, keepdims=True)
                linv_ref[b, to, :] = jnp.broadcast_to(linv, (32, 128))
        if n == 0 and first:
            cols = xa_ref.shape[1]
            xbuf = refs[8]
            slot = lax.rem(b, 2)
            for copy in loads(b):
                copy.wait()

            @pl.when(b + 1 < nb2)
            def _():
                for copy in loads(b + 1):
                    copy.start()

            @pl.loop(0, src, step=256)
            def _(r):
                at = pl.ds(pl.multiple_of(b * src + r, 256), 256)
                for k in range(2):
                    hi, lo = split2(xbuf[slot, k, pl.ds(r, 256), :])
                    xh_ref[at, k * cols : (k + 1) * cols] = hi
                    xl_ref[at, k * cols : (k + 1) * cols] = lo

        if n > 0:
            at = slice((n - 1) * rows, n * rows)
            lhs = cat3((wh_ref[b, at, :], wl_ref[b, at, :]), 1, False)
            rhs = cat3((xh_ref[block, :], xl_ref[block, :]), 0, True)
            u_ref[b, at, :] = dot(lhs, rhs, NN)


def forward_pair(pair, idx, xa, xb, adjacency, s_mine, s_cross, nb2, after=()):
    rows, src = adjacency.shape[1:]
    first = pair == 1
    cols = xa.shape[1]
    kd = 2 * cols if first else cols
    two = 2 * rows
    outs = [
        shape(nb2, two, kd),
        shape(nb2, two, 128),
        shape(nb2, rows, 128),
        shape(8, nb2 * src),
        shape(nb2, two, src, dtype=BF16),
        shape(nb2, two, src, dtype=BF16),
    ]
    if first:
        outs += [shape(nb2 * src, kd, dtype=BF16)] * 2
    return call(
        functools.partial(forward_kernel, pair),
        "forward_pair",
        (nb2,),
        [
            (idx, None),
            (adjacency, pl.BlockSpec((1, rows, src), lambda b, i: (i[0] * nb2 + b, 0, 0))),
            (s_mine, NEAR),
            (s_cross, NEAR),
            (xa, HBM if first else NEAR),
            (xb, ANY if first else NEAR),
        ],
        [(v, NEAR) for v in outs],
        scratch=[pltpu.VMEM((2, 2, src, cols), F32), pltpu.SemaphoreType.DMA((2, 2))] if first else [],
        after=after,
        work=(1e12 if first else 1e8, 1e5),
        vmem=22 if first else 16,
    )


def rel_rows(piece, mat, idx_ref):
    core = idx_ref[0]
    ref = piece[mat]
    cols = ref.shape[0] // 2
    at = lambda k: pl.ds(pl.multiple_of(k * cols, cols), cols)
    return jnp.concatenate([ref[at(core), :], ref[at(core ^ 1), :]], axis=0)


def flat_weights(pieces):
    return [(v, NEAR) for p in pieces for v in p]


def take_weights(pieces, refs):
    out = []
    for p in pieces:
        out.append(refs[: len(p)])
        refs = refs[len(p) :]
    return out, refs


def pre_kernel(form, src, u_ref, linv_ref, xh_ref, xl_ref, *refs):
    idx_ref = Place()
    weights, (o_ref,) = take_weights(form, refs)
    nb2, two = u_ref.shape[:2]
    rows = two // 2
    stack = lambda parts: jnp.concatenate(list(parts), axis=0)
    tops = [slice(b * src, b * src + rows) for b in range(nb2)]
    x = (stack(xh_ref[t, :] for t in tops), stack(xl_ref[t, :] for t in tops))
    for a, piece in enumerate(weights):
        at = slice(a * rows, (a + 1) * rows)
        mixed = split2(stack(u_ref[b, at, :] * linv_ref[b, at, 0:1] for b in range(nb2)))
        lhs = jnp.concatenate([cat3(mixed, 1, False), cat3(x, 1, False)], axis=1)
        proj, skip = split2(rel_rows(piece, 0, idx_ref)), split2(rel_rows(piece, 1, idx_ref))
        rhs = jnp.concatenate([cat3(proj, 0, True), cat3(skip, 0, True)], axis=0)
        o_ref[:, a * HD : (a + 1) * HD] = dot(lhs, rhs, NN)


def pre_pair(idx, u, linv, x_split, weights, src, spec, after=()):
    nb2, two, kd = u.shape
    rows = two // 2
    return call(
        functools.partial(pre_kernel, weights, src),
        "pre_pair",
        (1,),
        [(u, NEAR), (linv, NEAR), (x_split[0], NEAR), (x_split[1], NEAR)] + flat_weights(weights),
        [(shape(nb2 * rows, 2 * HD), spec)],
        after=after,
        work=(1e8, 1e5),
        vmem=16,
    )[0]


def live_rows(idx_ref, counts_ref, nb2, rows):
    parts = []
    for b in range(nb2):
        row = lax.broadcasted_iota(jnp.int32, (rows, 1), 0)
        parts.append((row < counts_ref[idx_ref[0] * nb2 + b]).astype(F32))
    return jnp.concatenate(parts, axis=0)


def stats_kernel(nb2, idx_ref, counts_ref, ca_ref, cb_ref, pa_ref, pb_ref, part_ref, recv_ref, pre_ref, st_ref, flip_ref):
    rows = part_ref.shape[0] // nb2
    total = lambda v: jnp.sum(v, axis=0, keepdims=True)
    live = live_rows(idx_ref, counts_ref, nb2, rows)
    for a, (c_ref, p_ref) in enumerate(((ca_ref, pa_ref), (cb_ref, pb_ref))):
        cols = slice(a * HD, (a + 1) * HD)
        bias = p_ref[0:1, :]
        pre = part_ref[:, cols] + recv_ref[:, cols] + bias
        pre_ref[:, cols] = pre
        act = (elu(pre) - elu(bias)) * live
        g = c_ref[...] * live
        rows8 = [total(act), total(act * act), total(g), total(g * act)]
        rows8.append(jnp.broadcast_to(total(live), (1, HD)))
        rows8.append(jnp.zeros((3, HD), F32))
        stats = jnp.concatenate(rows8, axis=0)
        st_ref[a] = stats
        flip_ref[1 - a] = stats


def norm_sums(hold, idx, counts, cotangent, cot_sib, par, par_sib, part, recv, nb2):
    full = part.shape[0]
    return call(
        functools.partial(stats_kernel, nb2),
        "norm_sums",
        (1,),
        [
            (idx, None),
            (counts, pl.BlockSpec(memory_space=pltpu.SMEM)),
            (cotangent, pl.BlockSpec((full, HD), lambda g, i: (i[0], 0))),
            (cot_sib, whole(full, HD)),
            (par, whole(8, HD)),
            (par_sib, whole(8, HD)),
            (part, NEAR),
            (recv, whole(full, 2 * HD)),
        ],
        [
            (shape(full, 2 * HD), NEAR),
            (shape(2, 8, HD), whole(2, 8, HD)),
            (shape(2, 8, HD), whole(2, 8, HD)),
        ],
        work=(1e8, 1e5),
        least=3 * 2**19,
        hold=hold,
        vmem=14,
    )


def apply_kernel(
    nb2, idx_ref, counts_ref, pre_ref, ca_ref, cb_ref, pa_ref, pb_ref, st_ref, act_ref, send_ref, d_ref, o_ref
):
    rows = pre_ref.shape[0] // nb2
    live = live_rows(idx_ref, counts_ref, nb2, rows)
    for a, (c_ref, p_ref, out_ref) in enumerate(
        ((ca_ref, pa_ref, act_ref), (cb_ref, pb_ref, send_ref))
    ):
        cols = slice(a * HD, (a + 1) * HD)
        bias, gamma, beta = p_ref[0:1, :], p_ref[1:2, :], p_ref[2:3, :]
        count = st_ref[a, 4:5, :]
        mean = st_ref[a, 0:1, :] / count
        inv = lax.rsqrt(st_ref[a, 1:2, :] / count - mean * mean + eps)
        grad_beta = st_ref[a, 2:3, :]
        grad_gamma = inv * (st_ref[a, 3:4, :] - mean * grad_beta)
        pre = pre_ref[:, cols]
        nrm = (elu(pre) - elu(bias) - mean) * inv
        out_ref[...] = live * (gamma * nrm + beta)
        g = c_ref[...] * live
        d = live * (gamma * inv) * (g - grad_beta / count - nrm * (grad_gamma / count))
        d = d * jnp.exp(jnp.minimum(pre, 0.0))
        d_ref[:, cols] = d
        o_ref[a, 0:1, :] = grad_gamma
        o_ref[a, 1:2, :] = grad_beta
        o_ref[a, 2:3, :] = jnp.sum(d, axis=0, keepdims=True)
        o_ref[a, 3:8, :] = jnp.zeros((5, HD), F32)


def norm_apply(hold, idx, counts, pre, cotangent, cot_sib, par, par_sib, stats, nb2):
    full = pre.shape[0]
    return call(
        functools.partial(apply_kernel, nb2),
        "norm_apply",
        (1,),
        [
            (idx, None),
            (counts, pl.BlockSpec(memory_space=pltpu.SMEM)),
            (pre, NEAR),
            (cotangent, pl.BlockSpec((full, HD), lambda g, i: (i[0], 0))),
            (cot_sib, whole(full, HD)),
            (par, whole(8, HD)),
            (par_sib, whole(8, HD)),
            (stats, whole(2, 8, HD)),
        ],
        [
            (shape(2 * full, HD), pl.BlockSpec((full, HD), lambda g, i: (i[0], 0))),
            (shape(full, HD), whole(full, HD)),
            (shape(full, 2 * HD), NEAR),
            (shape(2, 8, HD), whole(2, 8, HD)),
        ],
        least=3 * 2**19,
        hold=hold,
        vmem=14,
        work=(1e8, 1e5),
    )


def back_kernel(
    blk, pair, form, prior, xh_ref, xl_ref, wh_ref, wl_ref, s_ref, tm_ref, d_ref, linv_ref, u_ref, *refs
):
    idx_ref = Place()
    weights, refs = take_weights(form, refs)
    before, refs = refs[:pair], refs[pair:]
    earlier, refs = refs[:prior], refs[prior:]
    vh_ref, vl_ref, ds_ref, dp, delta, tacc = refs
    rows = tm_ref.shape[1]
    src = wh_ref.shape[2]
    base = 8 * prior
    for n, v in enumerate(earlier):
        ds_ref[8 * n : 8 * n + 8, :] = v[...]
    ds_ref[base : base + 8, :] = before[0][...] if pair == 1 else jnp.zeros((8, src), F32)
    tacc[...] = jnp.zeros_like(tacc)
    for a, piece in enumerate(weights):
        at = slice(a * rows, (a + 1) * rows)
        linv = linv_ref[blk, at, :]
        d = split2(d_ref[blk * rows : (blk + 1) * rows, a * HD : (a + 1) * HD] * linv[:, 0:1])
        v = dot(cat3(d, 1, False), cat3(split2(rel_rows(piece, 0, idx_ref)), 1, True), NT)
        hi, lo = split2(v)
        vh_ref[at, :] = hi
        vl_ref[at, :] = lo
        delta[at, :] = jnp.sum(v * u_ref[blk, at, :], axis=1, keepdims=True) * linv
    width = dp.shape[1]
    for j in range(src // width):
        js = slice(j * width, (j + 1) * width)
        xs = slice(blk * src + j * width, blk * src + (j + 1) * width)
        x = (xh_ref[xs, :], xl_ref[xs, :])
        dp[...] = dot(cat3((vh_ref[...], vl_ref[...]), 1, False), cat3(x, 1, True), NT)
        for a in range(2):
            m = 2 * pair + a
            s = s_ref[m : m + 1, xs] * HALF_LN2
            total = None
            for r in range(0, rows, 32):
                at = slice(r, r + 32)
                ar = slice(a * rows + r, a * rows + r + 32)
                t = tm_ref[blk, at, HEADS + m : HEADS + m + 1] * HALF_LN2
                slope = 0.6 + 0.4 * jnp.tanh(t + s)
                w = wh_ref[blk, ar, js].astype(F32) + wl_ref[blk, ar, js].astype(F32)
                dv = (w * slope) * (dp[ar, :] - delta[ar, 0:1])
                tacc[ar, :] += lane_groups(dv)
                total = dv if total is None else total + dv
            ds_ref[base + m : base + m + 1, js] = jnp.sum(total, axis=0, keepdims=True)
    for a in range(2):
        m = HEADS + 2 * pair + a
        sums = jnp.sum(tacc[a * rows : (a + 1) * rows, :], axis=1, keepdims=True)
        turned = jnp.transpose(jnp.broadcast_to(sums, (rows, 128)))
        ds_ref[base + m : base + m + 1, 0:rows] = turned[0:1, :]


def back_block(blk, pair, idx, x_split, fwd, d, weights, before=(), earlier=(), after=()):
    u, linv, tm, s, wh, wl = fwd
    two, src = wh.shape[1:]
    kd = u.shape[2]
    tj = 2 * TJ
    arrays = [*x_split, wh, wl, s, tm, d, linv, u]
    rest = [*before, *earlier]
    return call(
        functools.partial(back_kernel, blk, pair, weights, len(earlier)),
        "back_block",
        (1,),
        [(v, NEAR) for v in arrays] + flat_weights(weights) + [(v, NEAR) for v in rest],
        [
            (shape(two, kd, dtype=BF16), NEAR),
            (shape(two, kd, dtype=BF16), NEAR),
            (shape(8 * len(earlier) + 8, src), NEAR),
        ],
        scratch=[pltpu.VMEM((two, tj), F32), pltpu.VMEM((two, 128), F32), pltpu.VMEM((two, 128), F32)],
        after=after,
        work=(1e8, 1e5),
        vmem=16,
    )


def weight_kernel(src, u_ref, linv_ref, d_ref, xh_ref, xl_ref, send_ref, keep_ref):
    idx_ref = Place()
    core = idx_ref[0]
    nb2, two = u_ref.shape[:2]
    rows = two // 2
    stack = lambda parts: jnp.concatenate(list(parts), axis=0)
    tops = [slice(b * src, b * src + rows) for b in range(nb2)]
    x = cat3((stack(xh_ref[t, :] for t in tops), stack(xl_ref[t, :] for t in tops)), 0, False)
    for a, ref in ((1, send_ref), (0, keep_ref)):
        at = slice(a * rows, (a + 1) * rows)
        d = d_ref[:, a * HD : (a + 1) * HD]
        u = split2(stack(u_ref[b, at, :] for b in range(nb2)))
        dn = split2(d * stack(linv_ref[b, at, 0:1] for b in range(nb2)))
        gp = dot(cat3(u, 0, False), cat3(dn, 0, True), TN)
        gs = dot(x, cat3(split2(d), 0, True), TN)
        cols = gp.shape[0] // 2
        for mat, g in enumerate((gp, gs)):
            ref[mat, core] = g[:cols]
            ref[mat, core ^ 1] = g[cols:]


def weight_pair(idx, x_split, fwd, d, src, after=()):
    u, linv = fwd[:2]
    cols = u.shape[2] // 2
    arrays = [u, linv, d, *x_split]
    out = shape(2, 2, cols, HD)
    return call(
        functools.partial(weight_kernel, src),
        "weight_pair",
        (1,),
        [(v, NEAR) for v in arrays],
        [(out, NEAR), (out, NEAR)],
        after=after,
        work=(1e8, 1e5),
        vmem=16,
    )


def thin_kernel(xh_ref, xl_ref, da_ref, db_ref, o_ref, flip_ref):
    idx_ref = Place()
    core = idx_ref[0]
    cols = xh_ref.shape[1] // 2
    nb2, src = da_ref.shape[0] // 8, da_ref.shape[1]
    total = None
    for b in range(nb2):
        rows8 = slice(8 * b, 8 * b + 8)
        d = da_ref[rows8, :] + flip_rows(db_ref[rows8, :], 2)
        hi = d.astype(BF16).astype(F32)
        stack = jnp.concatenate([hi, d - hi], axis=0).astype(BF16)
        at = slice(b * src, (b + 1) * src)
        r1 = dot(stack, xh_ref[at, :], NN)
        r2 = dot(stack, xl_ref[at, :], NN)
        q = r1[:8] + (r1[8:] + r2[:8])
        total = q if total is None else total + q
    for k, q in enumerate((total[:, :cols], total[:, cols:])):
        o_ref[core ^ k] = q
        flip_ref[core ^ k] = flip_rows(q, 1)


def thin_sums(idx, x_split, ds, ds_cross, after=()):
    cols = x_split[0].shape[1] // 2
    return call(
        thin_kernel,
        "thin_sums",
        (1,),
        [(x_split[0], NEAR), (x_split[1], NEAR), (ds, NEAR), (ds_cross, NEAR)],
        [(shape(2, 8, cols), NEAR)] * 2,
        after=after,
        work=(1e8, 1e5),
        vmem=14,
    )


def skip_back(at, d_ref, weights, idx_ref):
    pair = [split2(rel_rows(piece, 1, idx_ref)) for piece in weights]
    both = [jnp.concatenate([p[n] for p in pair], axis=1) for n in range(2)]
    return dot(cat3(split2(d_ref[at, :]), 1, False), cat3(both, 1, True), NT)


def mix_kernel(blk, form, wh, wl, vh, vl, d_ref, *refs):
    idx_ref = Place()
    weights, (o_ref, mark_ref) = take_weights(form, refs)
    mark_ref[...] = jnp.zeros_like(mark_ref)
    j = pl.program_id(0)
    rows = vh.shape[0] // 2
    js = pl.ds(pl.multiple_of(j * TJ, TJ), TJ)
    rhs = cat3((vh[...], vl[...]), 0, True)
    o_ref[...] = dot(cat3((wh[blk, :, js], wl[blk, :, js]), 0, False), rhs, TN)

    @pl.when(j == 0)
    def _():
        o_ref[0:rows, :] += skip_back(slice(blk * rows, (blk + 1) * rows), d_ref, weights, idx_ref)


def mix_block(blk, idx, w, v, d, weights, after=()):
    src = w[0].shape[2]
    kd = v[0].shape[1]
    return call(
        functools.partial(mix_kernel, blk, weights),
        "mix_block",
        (src // TJ,),
        [(a, NEAR) for a in (*w, *v, d)] + flat_weights(weights),
        [(shape(src, kd), pl.BlockSpec((TJ, kd), lambda j: (j, 0))), (shape(8, 128), whole(8, 128))],
        after=after,
        work=(1e8, 1e5),
        vmem=16,
    )


def feature_kernel(blk, part, form, idx_ref, g_ref, wh, wl, vh, vl, da_ref, db_ref, a_ref, d_ref, *refs):
    weights, refs = take_weights(form, refs)
    oo_ref, os_ref, mark_ref = refs[-3:]
    j = pl.program_id(0)
    mark_ref[...] = jnp.zeros_like(mark_ref)
    half = oo_ref.shape[1]
    rows = vh.shape[0] // 2
    js = pl.ds(pl.multiple_of((part * pl.num_programs(0) + j) * TJ, TJ), TJ)
    rows8 = slice(8 * blk, 8 * blk + 8)
    d = da_ref[rows8, js] + flip_rows(db_ref[rows8, js], 2)
    out = dot(cat3((wh[blk, :, js], wl[blk, :, js]), 0, False), cat3((vh[...], vl[...]), 0, True), TN)
    out = out + (g_ref[...] + dot(thin_rows(d), thin_cols(a_ref[...]), TN))
    oo_ref[...] = out[:, :half]
    os_ref[...] = out[:, half:]
    if part == 0:

        @pl.when(j == 0)
        def _():
            more = skip_back(slice(blk * rows, (blk + 1) * rows), d_ref, weights, idx_ref)
            oo_ref[0:rows, :] += more[:, :half]
            os_ref[0:rows, :] += more[:, half:]


def feature_block(
    blk, part, idx, mixed, w, v, ds, ds_cross, a_half, d, weights, full, nb2, before, after=()
):
    src = w[0].shape[2]
    kd = v[0].shape[1]
    half = kd // 2
    nj = src // TJ
    count = nj // PARTS
    first = part * count
    ins = [(idx, None), (mixed, pl.BlockSpec((TJ, kd), lambda j, i: (first + j, 0)))]
    ins += [(a, NEAR) for a in (*w, *v)]
    ins += [(ds, NEAR), (ds_cross, NEAR), (a_half, NEAR), (d, NEAR)]
    ins += flat_weights(weights)
    aliases = {}
    if before is not None:
        aliases[len(ins)] = 0
        ins.append((before, HBM))
    return call(
        functools.partial(feature_kernel, blk, part, weights),
        "feature_block",
        (count,),
        ins,
        [
            (shape(*full), pl.BlockSpec((TJ, half), lambda j, i: ((i[0] * nb2 + blk) * nj + first + j, 0))),
            (shape(src // PARTS, half), pl.BlockSpec((TJ, half), lambda j, i: (j, 0))),
            (shape(8, 128), whole(8, 128)),
        ],
        after=after,
        work=(1e8, 1e5),
        vmem=18,
        aliases=aliases,
    )


def place_kernel(nb2, first, total, idx_ref, *refs):
    parts, (out_ref, mark_ref, buf, sems) = refs[:nb2], refs[nb2 + 1 :]
    mark_ref[...] = jnp.zeros_like(mark_ref)
    src = parts[0].shape[0]
    size = buf.shape[1]
    n = src // size

    def load(b, k):
        return pltpu.make_async_copy(parts[b].at[pl.ds(k * size, size), :], buf.at[b * n + k], sems.at[0, b * n + k])

    def store(b, k):
        at = pl.multiple_of(idx_ref[2] * total + (first + b) * src + k * size, size)
        return pltpu.make_async_copy(buf.at[b * n + k], out_ref.at[pl.ds(at, size), :], sems.at[1, b * n + k])

    every = [(b, k) for b in range(nb2) for k in range(n)]
    for b, k in every:
        load(b, k).start()
    for b, k in every:
        load(b, k).wait()
        store(b, k).start()
    for b, k in every:
        store(b, k).wait()


def place(idx, parts, before, after=(), first=0):
    nb2 = len(parts)
    src, half = parts[0].shape
    count = nb2 * src // TJ
    return call(
        functools.partial(place_kernel, nb2, first, before.shape[0] // 2),
        "place",
        (1,),
        [(idx, None)] + [(v, HBM) for v in parts] + [(before, HBM)],
        [(shape(*before.shape), HBM), (shape(8, 128), whole(8, 128))],
        scratch=[pltpu.VMEM((count, TJ, half), F32), pltpu.SemaphoreType.DMA((2, count))],
        after=after,
        work=(1e3, 1e6),
        least=2**18,
        vmem=14,
        aliases={1 + nb2: 0},
    )


def split_kernel(at, keep_ref, recv_ref, send_ref, next_ref):
    idx_ref = Place()
    size = next_ref.shape[1]
    mine = pl.ds(pl.multiple_of(idx_ref[at] * size, size), size)
    other = pl.ds(pl.multiple_of((1 - idx_ref[at]) * size, size), size)
    send_ref[...] = keep_ref[:, other, :] + recv_ref[:, other, :]
    next_ref[...] = keep_ref[:, mine, :] + recv_ref[:, mine, :]


def split_step(at, idx, keep, recv, after=()):
    n, rows, cols = keep.shape
    part = (n, rows // 2, cols)
    return call(
        functools.partial(split_kernel, at),
        "split_step",
        (1,),
        [(keep, NEAR), (recv, NEAR)],
        [(shape(*part), NEAR)] * 2,
        after=after,
        work=(1e3, keep.size * 8),
        vmem=8,
    )


def add_kernel(a_ref, b_ref, o_ref):
    o_ref[...] = a_ref[...] + b_ref[...]


def add_step(idx, a, b, after=()):
    return call(
        add_kernel,
        "add_step",
        (1,),
        [(a, NEAR), (b, NEAR)],
        [(shape(*a.shape), NEAR)],
        after=after,
        least=3 * 2**19,
        vmem=8,
        work=(1e3, a.size * 8),
    )[0]


def join_kernel(at, mine_ref, recv_ref, o_ref):
    idx_ref = Place()
    size = (mine_ref.shape[0] - EXTRA) // 2
    for mat in range(2):
        old = slice(mat * size, (mat + 1) * size)
        put = lambda up: pl.ds(pl.multiple_of(2 * mat * size + up * size, size), size)
        o_ref[put(idx_ref[at]), :] = mine_ref[old, :]
        o_ref[put(1 - idx_ref[at]), :] = recv_ref[old, :]
    o_ref[4 * size :, :] = mine_ref[2 * size :, :] + recv_ref[2 * size :, :]


def join_step(at, idx, mine, recv, after=()):
    rows, cols = mine.shape
    full = 2 * (rows - EXTRA) + EXTRA
    return call(
        functools.partial(join_kernel, at),
        "join_step",
        (1,),
        [(mine, NEAR), (recv, NEAR)],
        [(shape(full, cols), NEAR)],
        after=after,
        work=(1e3, mine.size * 16),
        least=3 * 2**19,
        vmem=10,
    )[0]


def end_kernel(keep_ref, recv_ref, o_ref):
    size = keep_ref.shape[1]
    for mat in range(2):
        o_ref[mat * size : (mat + 1) * size, :] = keep_ref[mat] + recv_ref[mat]
    o_ref[2 * size :, :] = jnp.zeros((EXTRA, o_ref.shape[1]), F32)


def end_step(idx, keep, recv, after=()):
    n, rows, cols = keep.shape
    full = n * rows + EXTRA
    return call(
        end_kernel,
        "end_step",
        (1,),
        [(keep, NEAR), (recv, NEAR)],
        [(shape(full, cols), NEAR)],
        after=after,
        work=(1e3, keep.size * 8),
        least=3 * 2**19,
        vmem=8,
    )[0]


def swap_kernel(keep_ref, recv_ref, q_ref, qr_ref, b_ref, br_ref, o_ref, extra_ref):
    size = keep_ref.shape[1]
    for mat in range(2):
        o_ref[mat * size : (mat + 1) * size, :] = keep_ref[mat] + recv_ref[mat]
    q = q_ref[...] + qr_ref[...]
    width = o_ref.shape[1]
    pick = lambda m: [q[k, n : n + 1, :] for k in range(2) for n in (m, HEADS + m)]
    zero = lambda n: [jnp.zeros((n, width), F32)]
    o_ref[2 * size :, :] = jnp.concatenate(pick(2) + zero(EXTRA - 4), axis=0)
    bias = b_ref[0, 2:3, :] + br_ref[1, 2:3, :]
    extra_ref[...] = jnp.concatenate(zero(4) + pick(0) + [bias] + zero(EXTRA - 9), axis=0)


def swap_step(idx, keep, recv, q, q_recv, sums, sums_recv, after=()):
    n, rows, cols = keep.shape
    full = n * rows + EXTRA
    arrays = [keep, recv, q, q_recv, sums, sums_recv]
    return call(
        swap_kernel,
        "swap_step",
        (1,),
        [(v, NEAR) for v in arrays],
        [(shape(full, cols), NEAR), (shape(EXTRA, cols), NEAR)],
        after=after,
        work=(1e3, keep.size * 8),
        least=3 * 2**19,
        vmem=8,
    )


def enter_kernel(a_ref, b_ref, extra_ref, more_ref, o_ref):
    rows = a_ref.shape[0] - EXTRA
    o_ref[...] = a_ref[...] + b_ref[...]
    o_ref[rows:, :] += extra_ref[...] + more_ref[...]


def enter_step(a, b, extra, more, after=()):
    return call(
        enter_kernel,
        "enter_step",
        (1,),
        [(v, NEAR) for v in (a, b, extra, more)],
        [(shape(*a.shape), NEAR)],
        after=after,
        work=(1e3, a.size * 8),
        vmem=8,
    )[0]


def last_kernel(idx_ref, own_ref, far_ref, att_ref, w_ref, op_ref, os_ref, oa_ref, ob_ref, bias_ref):
    tall = own_ref.shape[0] - EXTRA
    size = tall // 2

    def put(g_ref, first):
        total = None
        for k in range(2):
            at = slice(k * size // 2, (k + 1) * size // 2)
            q = far_ref[tall + first + 2 * k : tall + first + 2 * k + 2, :]
            q = jnp.concatenate([q, jnp.zeros((6, q.shape[1]), F32)], axis=0)
            op_ref[at, :] = g_ref[at, :] + dot(thin_rows(q), thin_cols(att_ref[...]), TN)
            hi = q.astype(BF16).astype(F32)
            stack = jnp.concatenate([hi, q - hi], axis=0).astype(BF16)
            wh, wl = split2(w_ref[at, :])
            r1, r2 = dot(stack, wh, NN), dot(stack, wl, NN)
            new = r1[:8] + (r1[8:] + r2[:8])
            total = new if total is None else total + new
        os_ref[...] = g_ref[size:tall, :]
        return total[0:1], total[1:2]

    @pl.when(pl.program_id(0) == 0)
    def _():
        a, b = put(own_ref, 4)
        oa_ref[...] = a
        ob_ref[...] = b
        bias_ref[...] = far_ref[tall + 8 : tall + 9, :]

    @pl.when(pl.program_id(0) == 1)
    def _():
        a, b = put(far_ref, 0)
        oa_ref[...] += a
        ob_ref[...] += b


def last_step(idx, own, far, att, w_proj, after=()):
    rows, width = own.shape
    size = (rows - EXTRA) // 2
    out = pl.BlockSpec((size, width), lambda g, i: (i[1] ^ g, 0))
    return call(
        last_kernel,
        "last_step",
        (2,),
        [(idx, None)] + [(v, NEAR) for v in (own, far, att)] + [(w_proj, out)],
        [(shape(2 * size, width), out)] * 2 + [(shape(1, width), whole(1, width))] * 3,
        after=after,
        work=(1e12, 4e6),
        least=3 * 2**19,
        vmem=16,
    )


def make_step(dp_size):
    bits = [1 << k for k in range(dp_size.bit_length() - 1)]

    def on_device(
        features, adjacency, seed_counts, w_proj, w_skip, attn_src, attn_dst, bias, gamma, beta, cotangent
    ):
        nb, rows, src = adjacency.shape
        cols = features.shape[1]
        nb2 = nb // 2
        h = lax.axis_index("head")
        dpi = lax.axis_index("dp")
        core, side = h & 1, h >> 1
        def to_core(v):
            return lax.ppermute(v, "head", [(i, i ^ 1) for i in range(HEADS)])

        def to_cross(v):
            return lax.ppermute(v, "head", [(i, i ^ 2) for i in range(HEADS)])

        def to_both(v, bit):
            pairs = [(d * HEADS + i, (d ^ bit) * HEADS + (i ^ 2)) for d in range(dp_size) for i in range(HEADS)]
            return lax.ppermute(v, ("dp", "head"), pairs)

        def to_dp(v, bit):
            return lax.ppermute(v, "dp", [(i, i ^ bit) for i in range(dp_size)])

        def half(v, which):
            size = v.shape[0] // 2
            return lax.dynamic_slice_in_dim(v, which * size, size, 0)

        ups = [(dpi >> k) & 1 for k in range(len(bits))]
        idx = jnp.stack([core, side, 1 - core, 1 - side] + ups).astype(jnp.int32)

        with jax.named_scope("fold_attention"):
            folded = jnp.stack(
                [jnp.sum(w_proj * attn_src, axis=1), jnp.sum(w_proj * attn_dst, axis=1)]
            )
            near_folded = to_core(folded)
            folded = jnp.stack([folded, near_folded])
            a_all = jnp.concatenate([folded, to_cross(folded)])
            a_all = a_all.transpose(1, 0, 2).reshape(2 * HEADS, -1)
            a_own = lax.dynamic_slice_in_dim(a_all, h * cols, cols, 1) * LOG2E

        with jax.named_scope("scores"):
            par = jnp.pad(jnp.stack([bias, gamma, beta]), ((0, 5), (0, 0)))
            par_sib = to_core(par)
            att = jnp.pad(jnp.stack([attn_src, attn_dst]), ((0, 6), (0, 0)))
            proj_half, mark = pack(idx, [(w_proj, 3)], after=[near_folded])
            proj_far = to_cross(proj_half)
            s_send, s_keep, x_send = scores(idx, features, a_own, after=[mark])
            s_mine = add_step(idx, s_keep, to_core(s_send), after=[proj_far])
            x_sib = to_core(relay(x_send, HBM, after=[s_mine]))
            s_cross = to_cross(s_mine)

        with jax.named_scope("share_weights"):
            skip_half, cot_send, proj_own, skip_own, mark = pack(
                idx, [(w_skip, 3), (cotangent, 2), (w_proj, 1), (w_skip, 1)], after=[s_mine]
            )
            skip_far = to_cross(skip_half)
            cot_sib = to_core(cot_send)

        with jax.named_scope("forward"):
            far_fwd = forward_pair(
                1, idx, features, x_sib, adjacency, s_mine, s_cross, nb2, after=[par_sib, mark, att]
            )
            x_split, far_fwd = far_fwd[6:], far_fwd[:6]
            skip_far = relay(skip_far, HBM, after=[far_fwd[3]])
            far_weights = [(proj_far, skip_far), (to_core(proj_far), to_core(skip_far))]
            far_part = pre_pair(idx, *far_fwd[:2], x_split, far_weights, src, whole(nb2 * rows, 2 * HD))
            recv = to_cross(far_part)
            own_fwd = forward_pair(0, idx, *x_split, adjacency, s_mine, s_cross, nb2, after=[far_part])
            own_weights = [(proj_own, skip_own), (to_core(proj_own), to_core(skip_own))]
            own_part = pre_pair(idx, *own_fwd[:2], x_split, own_weights, src, NEAR)

        with jax.named_scope("norm"):
            hold = [*x_split, *own_fwd[4:], *far_fwd[4:], own_fwd[0], far_fwd[0]]
            pre, stats, flipped = norm_sums(
                hold, idx, seed_counts, cotangent, cot_sib, par, par_sib, own_part, recv, nb2
            )
            stats = stats + to_core(flipped)
            for bit in bits:
                stats = stats + to_dp(stats, bit)
            act, act_send, d_own, small = norm_apply(
                hold, idx, seed_counts, pre, cotangent, cot_sib, par, par_sib, stats, nb2
            )
            act_recv = to_core(act_send)
            d_far = to_cross(d_own)

        token = [d_own]
        resident = []

        def note(out):
            token[:] = [out] + [Held(v) for v in resident]
            return out

        flat = lambda v: v.reshape(2, 2 * cols, HD)
        backs, fars, theirs = [], [], []
        state = {}

        def scatter(send, keep, recv, bits):
            for k, bit in enumerate(bits):
                send, keep = split_step(4 + k, idx, keep, recv, after=token)
                note(keep)
                recv = to_dp(send, bit)
                yield
            return keep, recv

        def gather(rows, bits):
            for k, bit in reversed(list(enumerate(bits))):
                recv = to_dp(rows, bit)
                yield
                rows = note(join_step(4 + k, idx, rows, recv, after=token))
            return rows

        def own_chain(send, keep):
            keep, recv = yield from scatter(send, flat(keep), flat(to_core(send)), bits)
            rows = note(end_step(idx, keep, recv, after=token))
            state["own"] = yield from gather(rows, bits)

        def far_chain(send, keep):
            keep, recv = yield from scatter(send, flat(keep), flat(to_core(send)), bits[:-1])
            while "flip" not in state:
                yield
            message, extra = swap_step(
                idx, keep, recv, state["q"], state["q_recv"], small, state["sums_recv"], after=token
            )
            note(extra)
            arrived = [to_cross(message), to_both(message, bits[-1]), extra, to_dp(extra, bits[-1])]
            yield
            rows = note(enter_step(*arrived, after=token))
            state["far"] = yield from gather(rows, bits[:-1])

        def advance(*chains):
            for c in chains:
                next(c, None)

        def back_far(b):
            fars.append(
                back_block(
                    b, 1, idx, x_split, far_fwd, d_far, far_weights, before=[backs[b][2]],
                    earlier=[f[2] for f in fars] if b == nb2 - 1 else (), after=token,
                )
            )
            note(fars[-1][2])

        half_cols = lambda i: lax.dynamic_slice_in_dim(a_all, i * cols, cols, 1)
        a_half = jnp.concatenate([half_cols(h), half_cols(h ^ 1)], axis=1)

        def features_of(b, part):
            state["gf"], other, mark = feature_block(
                b, part, idx, mixed[b], far_fwd[4:], fars[b][:2], ds, ds_cross, a_half, d_far,
                far_weights, features.shape, nb2,
                before=state.get("gf"), after=token,
            )
            note(mark)
            theirs.append(to_core(other))

        with jax.named_scope("backward"):
            state["sums_recv"] = to_core(small)
            send, keep = weight_pair(
                idx, x_split, own_fwd, d_own, src, after=token + [state["sums_recv"]]
            )
            note(keep)
            own = own_chain(send, keep)
            mixed = []
            for b in range(nb2):
                backs.append(
                    back_block(
                        b, 0, idx, x_split, own_fwd, d_own, own_weights, after=token + ([act_recv] if b else [])
                    )
                )
                note(backs[-1][2])
                if b == 0:
                    advance(own)
            for b in range(nb2):
                out, mark = mix_block(b, idx, own_fwd[4:], backs[b][:2], d_own, own_weights, after=token)
                note(mark)
                mixed.append(out)
                if b == 0:
                    advance(own)
            send, keep = weight_pair(idx, x_split, far_fwd, d_far, src, after=token)
            note(keep)
            advance(own)
            resident[:] = [*x_split, *far_fwd[4:], far_fwd[0], far_fwd[1]]
            far = far_chain(relay(send, NEAR, after=token), keep)
            advance(far)
            for b in range(nb2):
                back_far(b)
                if b < nb2 - 1:
                    advance(own)
            advance(far)
            ds = relay(fars[-1][2], NEAR, after=token)
            ds_cross = to_cross(ds)
            state["q"], state["q_flip"] = thin_sums(idx, x_split, ds, ds_cross, after=token)
            note(state["q"])
            state["q_recv"] = to_core(state["q_flip"])
            state["flip"] = True
            resident[:] = far_fwd[4:]
            note(state["q"])
            advance(far, own)
            for b in range(nb2):
                for part in range(PARTS):
                    features_of(b, part)
                    n = b * PARTS + part
                    if 0 < n < nb2 * PARTS - 1:
                        advance(far)
                    if n == 0:
                        advance(own)
            resident[:] = []
            note(token[0])
            activations, mark = place(idx, [act_recv], act, after=token)
            note(mark)
            early = len(theirs) - PARTS
            state["gf"], mark = place(idx, theirs[:early], state["gf"], after=token)
            note(mark)
            for c in (own, far):
                for _ in c:
                    pass

        with jax.named_scope("last"):
            grad_proj, grad_skip, grad_src, grad_dst, grad_bias = last_step(
                idx, state["own"], state["far"], att, w_proj
            )
            grad_features, mark = place(
                idx, theirs[early:], state["gf"], after=[grad_src], first=early
            )

        return (
            activations,
            grad_features,
            grad_proj,
            grad_skip,
            grad_src[0],
            grad_dst[0],
            grad_bias[0],
            small[0, 0],
            small[0, 1],
        )

    return on_device


def solution(mesh):
    return jax.shard_map(
        make_step(mesh.shape["dp"]),
        mesh=mesh,
        in_specs=(
            P("dp", "head"),
            P("dp", None, None),
            P("dp"),
            P(None, "head"),
            P(None, "head"),
            P("head"),
            P("head"),
            P("head"),
            P("head"),
            P("head"),
            P("dp", "head"),
        ),
        out_specs=(
            P("dp", "head"),
            P("dp", "head"),
            P(None, "head"),
            P(None, "head"),
            P("head"),
            P("head"),
            P("head"),
            P("head"),
            P("head"),
        ),
        check_vma=False,
    )
```
